128 devices in a mesh: ctx: 32 (over y_lo, x, z), fsdp: 4 (over y_hi, core).
Axes of the slice: x: 4, y: 4 (y_hi: 2, y_lo: 2; y = y_hi * 2 + y_lo), z: 4, core: 2. Of those that a mesh axis runs over, the one named last changes fastest.
Arguments:
- tokens: bfloat16 [4, 6144, 896], P('fsdp', 'ctx'), may hold values from -6 to 6
- block_order: int32 [64], replicated, may hold values from 0 to 63, each once
- query_weight: bfloat16 [896, 896], P('fsdp'), may hold values from -0.1875 to 0.1875
- key_weight: bfloat16 [896, 128], P('fsdp'), may hold values from -0.1875 to 0.1875
- value_weight: bfloat16 [896, 128], P('fsdp'), may hold values from -0.1875 to 0.1875
- output_weight: bfloat16 [896, 896], P('fsdp'), may hold values from -0.5 to 0.5
- gate_weight: bfloat16 [896, 4864], P('fsdp'), may hold values from -0.1875 to 0.1875
- up_weight: bfloat16 [896, 4864], P('fsdp'), may hold values from -0.1875 to 0.1875
- down_weight: bfloat16 [4864, 896], P('fsdp'), may hold values from -0.078125 to 0.078125
- query_bias: bfloat16 [896], P('fsdp'), may hold values from -3 to 3
- key_bias: bfloat16 [128], P('fsdp'), may hold values from -3 to 3
- value_bias: bfloat16 [128], P('fsdp'), may hold values from -3 to 3
- attention_gain: bfloat16 [896], P('fsdp'), may hold values from 0.099609375 to 1.8984375
- hidden_gain: bfloat16 [896], P('fsdp'), may hold values from 0.099609375 to 1.8984375
- cotangent: bfloat16 [4, 6144, 896], P('fsdp', 'ctx'), may hold values from -6 to 6
Outputs:
- output: bfloat16 [4, 6144, 896], P('fsdp', 'ctx')
- token_grad: float32 [4, 6144, 896], P('fsdp', 'ctx')
- query_weight_grad: float32 [896, 896], P('fsdp')
- key_weight_grad: float32 [896, 128], P('fsdp')
- value_weight_grad: float32 [896, 128], P('fsdp')
- output_weight_grad: float32 [896, 896], P('fsdp')
- gate_weight_grad: float32 [896, 4864], P('fsdp')
- up_weight_grad: float32 [896, 4864], P('fsdp')
- down_weight_grad: float32 [4864, 896], P('fsdp')
- query_bias_grad: float32 [896], P('fsdp')
- key_bias_grad: float32 [128], P('fsdp')
- value_bias_grad: float32 [128], P('fsdp')
- attention_gain_grad: float32 [896], P('fsdp')
- hidden_gain_grad: float32 [896], P('fsdp')
The draws below stay inside these ranges and needn't reach their ends.
Inputs may be any that keep to these rules, and one draw needn't show every extreme that they name: `block_order`: a permutation; index ctx device i holds layout blocks 2i and 2i + 1 of 96 tokens each.
All inputs are finite; a program needn't handle non-finite values.
Results may differ from the reference program's by a relative error of at most 0.02.
Values may be sent and summed in bfloat16 or wider, within the bound.
A program may use at most 256 MiB of HBM per device.

```python
import math
import jax
import jax.numpy as jnp
from jax import lax

D = 896
H = 14
KVH = 2
HD = 64
FF = 4864
SEQ = 6144
SEQS = 4
BLK = 96
BLOCKS = 64


def shard_levels(key, shape, split, low, high):
    def one(axis_at, blocks):
        draws = jax.random.uniform(jax.random.fold_in(jax.random.fold_in(key, 6), axis_at), (blocks,), jnp.float32, low / len(split), high / len(split))
        return jnp.repeat(jnp.exp(draws), shape[axis_at] // blocks).reshape((-1,) + (1,) * (len(shape) - axis_at - 1))

    factor_of = one(*split[0])
    for cut in split[1:]:
        factor_of = factor_of * one(*cut)
    return factor_of


def normal_values(stream_key, extent, width, reach, pieces=(), kind=jnp.bfloat16):
    level = shard_levels(stream_key, extent, pieces, -0.22, 0.18) if pieces else 1.0
    values = jax.random.normal(stream_key, extent, jnp.float32) * width * level
    return jnp.minimum(jnp.maximum(values, -reach), reach).astype(kind)


def setup_inputs(seed: int = 0) -> dict:
    key_of = jax.random.split(jax.random.key(seed), 16)
    return {
        "tokens": normal_values(key_of[0], (SEQS, SEQ, D), 1.0, 6.0, ((0, 4), (1, 32))),
        "block_order": jax.random.permutation(key_of[1], BLOCKS).astype(jnp.int32),
        "query_weight": normal_values(key_of[2], (D, H * HD), D ** -0.5, 0.1875, ((0, 4),)),
        "key_weight": normal_values(key_of[3], (D, KVH * HD), D ** -0.5, 0.1875, ((0, 4),)),
        "value_weight": normal_values(key_of[4], (D, KVH * HD), D ** -0.5, 0.1875, ((0, 4),)),
        "output_weight": normal_values(key_of[5], (H * HD, D), (H * HD // 8) ** -0.5, 0.5, ((0, 4),)),
        "gate_weight": normal_values(key_of[6], (D, FF), D ** -0.5, 0.1875, ((0, 4),)),
        "up_weight": normal_values(key_of[7], (D, FF), D ** -0.5, 0.1875, ((0, 4),)),
        "down_weight": normal_values(key_of[8], (FF, D), FF ** -0.5, 0.078125, ((0, 4),)),
        "query_bias": normal_values(key_of[9], (H * HD,), 0.5, 3.0, ((0, 4),)),
        "key_bias": normal_values(key_of[10], (KVH * HD,), 0.5, 3.0, ((0, 4),)),
        "value_bias": normal_values(key_of[11], (KVH * HD,), 0.5, 3.0, ((0, 4),)),
        "attention_gain": jnp.clip(1.0 + 0.18 * jax.random.normal(key_of[12], (D,), jnp.float32), 0.099609375, 1.8984375).astype(jnp.bfloat16),
        "hidden_gain": jnp.clip(1.0 + 0.18 * jax.random.normal(key_of[13], (D,), jnp.float32), 0.099609375, 1.8984375).astype(jnp.bfloat16),
        "cotangent": normal_values(key_of[14], (SEQS, SEQ, D), 1.0, 6.0, ((0, 4), (1, 32))),
    }


@jax.custom_vjp
def low(v):
    return lax.optimization_barrier(v.astype(jnp.bfloat16)).astype(jnp.float32)

@jax.custom_vjp
def low_back(v):
    return v

def low_keep(v):
    return (low(v), None)

def low_pass(kept, grad):
    return (grad,)

def back_keep(v):
    return (v, None)

def back_low(kept, grad):
    return (low(grad),)
low.defvjp(low_keep, low_pass)
low_back.defvjp(back_keep, back_low)
HIGHEST = lax.Precision.HIGHEST
EPSILON = 1e-06
THETA = 1000000.0

def rms_scale(values, gain):
    return values * lax.rsqrt(lax.optimization_barrier(jnp.mean(values * values, axis=-1, keepdims=True)) + EPSILON) * gain

def rotary(values, positions):
    half_width = HD // 2
    frequency = jnp.exp(jnp.arange(half_width, dtype=jnp.float32) * (-2.0 * math.log(THETA) / HD))
    angles = positions.astype(jnp.float32)[:, None] * frequency[None, :]
    cosine = jnp.cos(angles)[:, None, :]
    sine_table = jnp.sin(angles)[:, None, :]
    front_half = values[..., :half_width]
    back_half = values[..., half_width:]
    return jnp.concatenate([front_half * cosine - back_half * sine_table, back_half * cosine + front_half * sine_table], axis=-1)

def layer(inputs, positions, params):
    query_weight, key_weight, value_weight, output_weight, gate_weight, up_weight, down_weight, query_bias, key_bias, value_bias, attention_gain, hidden_gain = params
    normed = low(rms_scale(inputs, attention_gain))
    queries = low_back(jnp.dot(normed, query_weight, precision=HIGHEST) + query_bias)
    key_pre = low_back(jnp.dot(normed, key_weight, precision=HIGHEST) + key_bias)
    value_low = low(low_back(jnp.dot(normed, value_weight, precision=HIGHEST) + value_bias)).reshape(SEQ, KVH, HD)
    query_rot = low(rotary(queries.reshape(SEQ, H, HD), positions))
    key_rot = low(rotary(key_pre.reshape(SEQ, KVH, HD), positions))
    query_span = min(512, SEQ)
    score_scale = 1.0 / math.sqrt(HD)

    def attend_block(block_pair):
        query_block, block_pos = block_pair
        grouped = query_block.reshape(query_span, KVH, H // KVH, HD)
        scores = jnp.einsum('tkgd,skd->kgts', grouped, key_rot, precision=HIGHEST)
        scores = low_back(scores * score_scale)
        allowed = positions[None, :] <= block_pos[:, None]
        scores = jnp.where(allowed[None, None], scores, -1e+30)
        weights = low(jax.nn.softmax(scores, axis=-1))
        mixed_heads = jnp.einsum('kgts,skd->tkgd', weights, value_low, precision=HIGHEST)
        return mixed_heads.reshape(query_span, H * HD)
    attended = lax.map(jax.checkpoint(attend_block), (query_rot.reshape(SEQ // query_span, query_span, H, HD), positions.reshape(SEQ // query_span, query_span)))
    attended = low(low_back(attended.reshape(SEQ, H * HD)))
    middle = inputs + low_back(jnp.dot(attended, output_weight, precision=HIGHEST))
    normed_two = low(rms_scale(middle, hidden_gain))
    gate_pre = low_back(jnp.dot(normed_two, gate_weight, precision=HIGHEST))
    upward = low_back(jnp.dot(normed_two, up_weight, precision=HIGHEST))
    hidden = low(jax.nn.silu(gate_pre) * upward)
    return middle + low_back(jnp.dot(hidden, down_weight, precision=HIGHEST))

def reference(tokens, block_order, query_weight, key_weight, value_weight, output_weight, gate_weight, up_weight, down_weight, query_bias, key_bias, value_bias, attention_gain, hidden_gain, cotangent):
    layout_rows = jnp.arange(SEQ, dtype=jnp.int32)
    positions = (block_order[layout_rows // BLK] * BLK + layout_rows % BLK).astype(jnp.int32)
    params = (query_weight.astype(jnp.float32), key_weight.astype(jnp.float32), value_weight.astype(jnp.float32), output_weight.astype(jnp.float32), gate_weight.astype(jnp.float32), up_weight.astype(jnp.float32), down_weight.astype(jnp.float32), query_bias.astype(jnp.float32), key_bias.astype(jnp.float32), value_bias.astype(jnp.float32), attention_gain.astype(jnp.float32), hidden_gain.astype(jnp.float32))

    def forward(inputs, weights):
        return lax.map(lambda sequence: layer(sequence, positions, weights), inputs)
    output, pullback = jax.vjp(forward, tokens.astype(jnp.float32), params)
    token_grad, grads = pullback(cotangent.astype(jnp.float32))
    return (output.astype(jnp.bfloat16), token_grad, grads[0], grads[1], grads[2], grads[3], grads[4], grads[5], grads[6], grads[7], grads[8], grads[9], grads[10], grads[11])
```

```python
import functools
import math

import jax
import jax.numpy as jnp
from jax import lax
from jax.experimental import pallas as pl
from jax.experimental.pallas import tpu as pltpu
from jax.sharding import PartitionSpec as P

H = 14
KVH = 2
GROUP = H // KVH
HD = 64
ROWS = 192
BLK = 96
LANES = 1408
SLAB = 1536
SLABS = 4
OWN = 256

EPSILON = 1e-06
THETA = 1000000.0
MASKED = -1e30

BF = jnp.bfloat16
F32 = jnp.float32
VMEM = pl.BlockSpec(memory_space=pltpu.VMEM)
NT = (((1,), (1,)), ((), ()))
TN = (((0,), (0,)), ((), ()))


def dot(left, right):
    return jnp.dot(left, right, preferred_element_type=F32)


def dot_nt(left, right):
    return lax.dot_general(left, right, NT, preferred_element_type=F32)


def dot_tn(left, right):
    return lax.dot_general(left, right, TN, preferred_element_type=F32)


def thirds(value):
    high = value.astype(BF).astype(F32)
    rest = value - high
    middle = rest.astype(BF).astype(F32)
    low = (rest - middle).astype(BF).astype(F32)
    return high, middle, low


MESH = pl.DeviceIdType.MESH
ANY = pl.BlockSpec(memory_space=pl.ANY)
WINDOW = 1280
UNITS = 1216
SHARD = 224
WIDTH = 896
MIB = 2**20


def place():
    ctx, f = lax.axis_index("ctx"), lax.axis_index("fsdp")
    return lax.div(ctx, 16), lax.rem(lax.div(ctx, 4), 4), lax.rem(ctx, 4), lax.div(f, 2), lax.rem(f, 2)


def at(yl, x, z, yh, c):
    return ((yl * 4 + x) * 4 + z, yh * 2 + c)


def turn(index, by):
    return lax.rem(index + by, 4)


def greet(devices):
    barrier = pltpu.get_barrier_semaphore()
    for device in devices:
        pl.semaphore_signal(barrier, inc=1, device_id=device, device_id_type=MESH)
    pl.semaphore_wait(barrier, len(devices))


class Links:
    def __init__(self, send, recv):
        self.send, self.recv, self.used = send, recv, 0

    def reserve(self, count):
        first = self.used
        self.used += count
        return first

    def copy(self, src, dst, device, slot):
        return pltpu.make_async_remote_copy(
            src_ref=src,
            dst_ref=dst,
            send_sem=self.send.at[slot],
            recv_sem=self.recv.at[slot],
            device_id=device,
            device_id_type=MESH,
        )

    def push(self, src, dst, device):
        copy = self.copy(src, dst, device, self.reserve(1))
        copy.start()
        return copy


def lanes_below(shape, bound):
    return lax.broadcasted_iota(jnp.int32, shape, 1) < bound


def swap64(value):
    return pltpu.roll(value, 64, axis=1)


def turn_pairs(value, cosine, sine):
    lane = lax.broadcasted_iota(jnp.int32, value.shape, 1)
    other = jnp.where(
        lax.rem(lane, 64) < 32, pltpu.roll(value, 96, axis=1), pltpu.roll(value, 32, axis=1)
    )
    return value * cosine + other * sine


def key_extra(rows):
    count = rows.shape[0]
    return jnp.broadcast_to(rows[:, None, :], (count, BLK, 128)).reshape(count * BLK, 128).astype(BF)


def own_extra():
    lane = lax.broadcasted_iota(jnp.int32, (OWN, 128), 1)
    return jnp.where((lane >= 2) & (lane < 5), 1.0, 0.0).astype(BF)


def window_start(f):
    return pl.multiple_of(lax.div(19 * f, 2) * 128, 128)


def front_kernel(
    tokens_ref,
    wq_ref,
    wk_ref,
    wv_ref,
    small_ref,
    cos_ref,
    sin_ref,
    extra_ref,
    kpos_ref,
    qpos_ref,
    wo_ref,
    gate_ref,
    up_ref,
    cot_ref,
    attended_ref,
    ot_ref,
    lse_ref,
    q_ref,
    kv_ref,
    normed_ref,
    wq_all,
    wk_all,
    wv_all,
    small_all,
    wo_all,
    gate_all,
    up_all,
    cot_all,
    own,
    acc,
    top,
    natural,
    send,
    recv,
    local,
):
    yl, x, z, yh, c = place()
    f = yh * 2 + c
    f_cross = (1 - yh) * 2 + c
    f_sib = yh * 2 + 1 - c
    f_far = (1 - yh) * 2 + 1 - c
    sib = at(yl, x, z, yh, 1 - c)
    cross = at(1 - yl, x, z, 1 - yh, c)
    far = at(1 - yl, x, z, 1 - yh, 1 - c)
    mate = at(1 - yl, x, z, yh, c)
    on_x = [at(yl, turn(x, d), z, yh, c) for d in (1, 2, 3)]
    on_z = [at(yl, x, turn(z, d), yh, c) for d in (1, 2, 3)]
    links = Links(send, recv)
    greet([sib, cross, far, mate] + on_x + on_z)

    def gather_start(pairs):
        return [
            (links.push(mine, whole.at[f], sib), links.push(mine, whole.at[f], cross), whole)
            for mine, whole in pairs
        ]

    def gather_relay(started):
        relays = []
        for _, over, whole in started:
            over.wait_recv()
            relays.append(links.push(whole.at[f_cross], whole.at[f_cross], sib))
        return relays

    def gather_end(started, relays):
        for beside, over, _ in started:
            beside.wait()
            over.wait_send()
        for relay in relays:
            relay.wait()

    first = gather_start(
        [(wq_ref, wq_all), (wk_ref, wk_all), (wv_ref, wv_all), (small_ref, small_all)]
    )
    keep = []
    for n, (mine, whole) in enumerate(
        [(wo_ref, wo_all.at[f]), (cot_ref, cot_all.at[f])]
        + [
            (ref.at[:, pl.ds(window_start(f), WINDOW)], whole.at[f])
            for ref, whole in ((gate_ref, gate_all), (up_ref, up_all))
        ]
    ):
        copy = pltpu.make_async_copy(mine, whole, local.at[n])
        copy.start()
        keep.append(copy)
    wq_all[f] = wq_ref[...]
    wk_all[f] = wk_ref[...]
    wv_all[f] = wv_ref[...]
    small_all[f] = small_ref[...]
    inputs = tokens_ref[...].astype(F32)
    scale = lax.rsqrt(jnp.mean(inputs * inputs, axis=-1, keepdims=True) + EPSILON)
    relays = gather_relay(first)
    second = gather_start([(wo_ref, wo_all), (cot_ref, cot_all)])
    spread = []
    for ref, whole in ((gate_ref, gate_all), (up_ref, up_all)):
        for device, index in ((cross, f_cross), (far, f_far), (sib, f_sib)):
            part = ref.at[:, pl.ds(window_start(index), WINDOW)]
            spread.append(links.push(part, whole.at[f], device))
    gather_end(first, relays)

    def vector(row, count):
        return jnp.concatenate([small_all[n, row : row + 1, 0:count] for n in range(4)], axis=1)

    normed = (inputs * scale * vector(1, SHARD)).astype(BF)
    normed_ref[...] = normed
    cosine, sine = cos_ref[...], sin_ref[...]
    low = lanes_below((ROWS, 128), 64)

    queries = dot(normed, wq_all[...].reshape(WIDTH, WIDTH)) + vector(0, SHARD)
    keys = dot(normed, wk_all[...].reshape(WIDTH, 128)) + vector(3, 32)
    values = dot(normed, wv_all[...].reshape(WIDTH, 128)) + vector(4, 32)
    keys = turn_pairs(keys, cosine, sine).astype(BF).astype(F32)
    values = values.astype(BF).astype(F32)
    own[...] = jnp.zeros(own.shape, BF)
    own[0, 0:ROWS] = jnp.where(low, keys, swap64(values)).astype(BF)
    own[1, 0:ROWS] = jnp.where(low, swap64(keys), values).astype(BF)

    slab_of = (x, z)
    spot = [
        pl.ds(pl.multiple_of((z * 2 + yl) * ROWS, ROWS), ROWS),
        pl.ds(pl.multiple_of((x * 2 + yl) * ROWS, ROWS), ROWS),
    ]
    pair = [
        pl.ds(pl.multiple_of(z * 2 * ROWS, 2 * ROWS), 2 * ROWS),
        pl.ds(pl.multiple_of(x * 2 * ROWS, 2 * ROWS), 2 * ROWS),
    ]
    mates = [
        links.push(own.at[g, 0:ROWS], kv_ref.at[g, slab_of[g], spot[g]], mate) for g in range(KVH)
    ]
    for g in range(KVH):
        kv_ref[g, slab_of[g], spot[g], :] = own[g, 0:ROWS]

    for tile in range(H // 2):
        part = turn_pairs(queries[:, tile * 128 : tile * 128 + 128], cosine, sine)
        part = part.astype(BF).astype(F32) * (1.0 / math.sqrt(HD))
        for half in range(2):
            head = tile * 2 + half
            j = head % GROUP
            mine = part if half == 0 else swap64(part)
            q_ref[head // GROUP, j * ROWS : (j + 1) * ROWS, 0:128] = jnp.where(
                low, mine, 0.0
            ).astype(BF)
    row = lax.broadcasted_iota(jnp.int32, (LANES, 128), 0)
    lane = lax.broadcasted_iota(jnp.int32, (LANES, 128), 1)
    block = lax.rem(lax.div(row, BLK), 2)
    hot = jnp.where((block == lane) & (row < GROUP * ROWS), 1.0, 0.0).astype(BF)
    for g in range(KVH):
        q_ref[g, :, 128:256] = hot
        q_ref[g, GROUP * ROWS :, 0:128] = jnp.zeros((LANES - GROUP * ROWS, 128), BF)

    def mix(g, keys, scores):
        old = top[g, 0:1]
        new = jnp.maximum(old, jnp.max(scores, axis=0, keepdims=True))
        weights = jnp.exp(scores - new).astype(BF)
        acc[g] = acc[g] * jnp.exp(old - new) + dot(keys.T[64:136], weights)
        top[g, 0:1] = new

    top[...] = jnp.full(top.shape, MASKED, F32)
    acc[...] = jnp.zeros(acc.shape, F32)
    for copy in mates:
        copy.wait()
    pairs = [
        links.push(kv_ref.at[0, x, pair[0]], kv_ref.at[0, x, pair[0]], device) for device in on_z
    ] + [links.push(kv_ref.at[1, z, pair[1]], kv_ref.at[1, z, pair[1]], device) for device in on_x]
    mask = jnp.where(kpos_ref[:, 0:1] <= qpos_ref[0:1], 0.0, MASKED)
    for g in range(KVH):
        keys = jnp.concatenate([own[g], own_extra()], axis=1)
        mix(g, keys, dot_nt(keys, q_ref[g]) + mask)
    for copy in pairs:
        copy.wait()
    base = links.reserve(6)

    def slab_copy(g, d, slab):
        device = (
            ((yl * 4 + jnp.where(g == 0, turn(x, d), x)) * 4 + jnp.where(g == 0, z, turn(z, d))),
            f,
        )
        return links.copy(kv_ref.at[g, slab], kv_ref.at[g, slab], device, base + g * 3 + d - 1)

    slabs = [slab_copy(g, d, slab_of[g]) for d in (1, 3, 2) for g in range(KVH)]
    for copy in slabs:
        copy.start()
    relays = []

    def step(i, _):
        g, n = lax.rem(i, 2), lax.div(i, 2)
        d = jnp.where(n == 2, 3, jnp.where(n == 3, 2, n))
        slab = turn(jnp.where(g == 0, x, z), d)

        @pl.when(n > 0)
        def _():
            slab_copy(g, 4 - d, slab).wait_recv()

        rows = extra_ref[g, pl.ds(pl.multiple_of(slab * 16, 16), 16), :]
        keys = jnp.concatenate([kv_ref[g, slab], key_extra(rows)], axis=1)
        mix(g, keys, dot_nt(keys, q_ref[g]))
        return 0

    lax.fori_loop(0, 8, step, 0)
    for copy in slabs:
        copy.wait_send()
    relays = gather_relay(second)

    for g in range(KVH):
        total = acc[g, 66:67]
        out = acc[g, 0:64] / total
        ot_ref[g] = out
        lse_ref[g] = jnp.broadcast_to(top[g, 0:1] + jnp.log(total), (8, LANES))
        natural[g] = jnp.concatenate([out, jnp.zeros((64, LANES), F32)], axis=0).T
    for tile in range(H // 2):
        even, odd = tile * 2, tile * 2 + 1
        left = natural[even // GROUP, (even % GROUP) * ROWS : (even % GROUP + 1) * ROWS]
        right = natural[odd // GROUP, (odd % GROUP) * ROWS : (odd % GROUP + 1) * ROWS]
        attended_ref[:, tile * 128 : tile * 128 + 128] = jnp.where(
            low, left, swap64(right)
        ).astype(BF)
    for copy in spread:
        copy.wait()
    gather_end(second, relays)
    for copy in keep:
        copy.wait()


def front(tokens, wq, wk, wv, small, cosine, sine, extra, kpos, qpos, wo, gate, up, cot):
    shape = jax.ShapeDtypeStruct
    return pl.pallas_call(
        front_kernel,
        out_shape=[
            shape((ROWS, WIDTH), BF),
            shape((KVH, HD, LANES), F32),
            shape((KVH, 8, LANES), F32),
            shape((KVH, LANES, 256), BF),
            shape((KVH, SLABS, SLAB, 128), BF),
            shape((ROWS, WIDTH), BF),
            shape((4, SHARD, WIDTH), BF),
            shape((4, SHARD, 128), BF),
            shape((4, SHARD, 128), BF),
            shape((4, 8, 256), F32),
            shape((4, SHARD, WIDTH), BF),
            shape((4, SHARD, WINDOW), BF),
            shape((4, SHARD, WINDOW), BF),
            shape((4, ROWS, WIDTH), BF),
        ],
        in_specs=[VMEM] * 10 + [ANY] * 4,
        out_specs=[VMEM] * 10 + [ANY] * 4,
        scratch_shapes=[
            pltpu.VMEM((KVH, OWN, 128), BF),
            pltpu.VMEM((KVH, 72, LANES), F32),
            pltpu.VMEM((KVH, 8, LANES), F32),
            pltpu.VMEM((KVH, LANES, 128), F32),
            pltpu.SemaphoreType.DMA((48,)),
            pltpu.SemaphoreType.DMA((48,)),
            pltpu.SemaphoreType.DMA((4,)),
        ],
        compiler_params=pltpu.CompilerParams(
            vmem_limit_bytes=58 * MIB, collective_id=0, has_side_effects=True
        ),
        name="front",
    )(tokens, wq, wk, wv, small, cosine, sine, extra, kpos, qpos, wo, gate, up, cot)


UNIT = 106
HALF = 53
CHUNK = 768


def widen(ref, index):
    return ref[index].astype(F32)


def back_kernel(
    q_ref,
    do_ref,
    ot_ref,
    lse_ref,
    kv_ref,
    extra_ref,
    kpos_ref,
    qpos_ref,
    grads_ref,
    dkv_ref,
    dq_ref,
    sum_ref,
    qx,
    dox,
    own,
    own_grad,
    parts,
    parts_in,
    pairs,
    pairs_in,
    single,
    single_in,
    side_a,
    side_b,
    in_a,
    in_b,
    late_a,
    late_b,
    whole,
    whole_in,
    send,
    recv,
    local,
):
    yl, x, z, yh, c = place()
    f = yh * 2 + c
    mate = at(1 - yl, x, z, yh, c)
    on_x = [at(yl, turn(x, d), z, yh, c) for d in (1, 2, 3)]
    on_z = [at(yl, x, turn(z, d), yh, c) for d in (1, 2, 3)]
    links = Links(send, recv)
    greet([mate] + on_x + on_z)

    first = []
    for n in range(3):
        first.append(
            links.push(grads_ref.at[turn(x, n + 1), :, 0:HALF], in_a.at[n], on_x[n])
        )
        first.append(
            links.push(grads_ref.at[:, turn(z, n + 1), HALF:UNIT], in_b.at[n], on_z[n])
        )
    keep = [
        pltpu.make_async_copy(grads_ref.at[x, :, 0:HALF], side_a, local.at[0]),
        pltpu.make_async_copy(grads_ref.at[:, z, HALF:UNIT], side_b, local.at[1]),
    ]
    for copy in keep:
        copy.start()

    row = lax.broadcasted_iota(jnp.int32, (128, LANES), 0)
    for g in range(KVH):
        lse = thirds(lse_ref[g, 0:1])
        inner = jnp.sum(do_ref[g].astype(F32).T[64:128] * ot_ref[g], axis=0, keepdims=True)
        inner = thirds(inner)
        extra_q = jnp.zeros((128, LANES), F32)
        extra_d = jnp.zeros((128, LANES), F32)
        for n in range(3):
            extra_q = jnp.where(row == 2 + n, -lse[n], extra_q)
            extra_d = jnp.where(row == 2 + n, -inner[n], extra_d)
        qx[g, :, 0:128] = q_ref[g, :, 0:128]
        qx[g, :, 128:256] = (q_ref[g, :, 128:256].astype(F32) + extra_q.T).astype(BF)
        dox[g, :, 0:128] = do_ref[g]
        dox[g, :, 128:256] = extra_d.T.astype(BF)

    def piece(g, keys, mask):
        scores = dot_nt(keys, qx[g])
        if mask is not None:
            scores = scores + mask
        probs = jnp.exp(scores)
        grad = (probs * dot_nt(keys, dox[g])).astype(BF)
        both = dot(grad, qx[g, :, 0:128]) + dot(probs.astype(BF), dox[g, :, 0:128])
        return both, dot(keys[:, 0:128].T[0:64], grad)

    mask = jnp.where(kpos_ref[:, 0:1] <= qpos_ref[0:1], 0.0, MASKED)
    spots = (
        pl.ds(pl.multiple_of((z * 2 + yl) * ROWS, ROWS), ROWS),
        pl.ds(pl.multiple_of((x * 2 + yl) * ROWS, ROWS), ROWS),
    )
    slab_of = (x, z)
    for g in range(KVH):
        own[...] = jnp.zeros(own.shape, BF)
        own[0:ROWS] = kv_ref[g, slab_of[g], spots[g], :]
        both, dq = piece(g, jnp.concatenate([own[...], own_extra()], axis=1), mask)
        own_grad[g] = both[0:ROWS]
        dq_ref[g] = dq
    count = SLAB // CHUNK
    base = links.reserve(6)

    def part_copy(g, d, slab):
        device = (
            ((yl * 4 + jnp.where(g == 0, slab, x)) * 4 + jnp.where(g == 0, z, slab)),
            f,
        )
        n = g * 3 + d - 1
        return links.copy(parts.at[g, slab], parts_in.at[g, d - 1], device, base + n)

    def step(i, _):
        g = lax.div(i, SLABS * count)
        d = lax.rem(lax.rem(lax.div(i, count), SLABS) + 1, 4)
        part = lax.rem(i, count)
        slab = turn(jnp.where(g == 0, x, z), d)
        start = pl.multiple_of(part * CHUNK, CHUNK)
        rows = extra_ref[g, pl.ds(pl.multiple_of(slab * 16 + part * 8, 8), 8), :]
        keys = jnp.concatenate([kv_ref[g, slab, pl.ds(start, CHUNK), :], key_extra(rows)], axis=1)
        both, dq = piece(g, keys, None)
        parts[g, slab, pl.ds(start, CHUNK), :] = both.astype(BF)
        dq_ref[g] += dq

        @pl.when((part == count - 1) & (d > 0))
        def _():
            part_copy(g, d, slab).start()

        return 0

    pair_copies = []

    def pair_start(g):
        slab = slab_of[g]
        for d in (1, 2, 3):
            part_copy(g, d, turn(slab, d)).wait()
        for n in range(4):
            rows = slice(n * 2 * ROWS, (n + 1) * 2 * ROWS)
            total = parts[g, slab, rows, :].astype(F32)
            for m in range(3):
                total = total + parts_in[g, m, rows, :].astype(F32)
            pairs[g, n] = total.astype(BF)
        other = (z, x)[g]
        devices = (on_z, on_x)[g]
        return [
            links.push(pairs.at[g, turn(other, n + 1)], pairs_in.at[g, n], devices[n])
            for n in range(3)
        ]

    def single_start(g, copies):
        for copy in copies:
            copy.wait()
        total = pairs[g, (z, x)[g]].astype(F32)
        for m in range(3):
            total = total + pairs_in[g, m].astype(F32)
        single[g, 0] = total[0:ROWS]
        single[g, 1] = total[ROWS:]
        low = jnp.where(yl == 0, total[ROWS:], total[0:ROWS])
        single_low = low.astype(BF)
        single_in[g, 0] = single_low
        return links.push(single_in.at[g, 0], single_in.at[g, 1], mate)

    def single_end(g, copy):
        copy.wait()
        dkv_ref[g] = single[g, yl] + single_in[g, 1].astype(F32) + own_grad[g]

    def second_start():
        for copy in keep + first:
            copy.wait()

        def add(n, _):
            a = side_a[n].astype(F32)
            b = side_b[n].astype(F32)
            for m in range(3):
                a = a + in_a[m, n].astype(F32)
                b = b + in_b[m, n].astype(F32)
            side_a[n] = a.astype(BF)
            side_b[n] = b.astype(BF)
            return 0

        lax.fori_loop(0, 4, add, 0)
        copies = []
        for n in range(3):
            copies.append(links.push(side_a.at[turn(z, n + 1)], late_a.at[n], on_z[n]))
            copies.append(links.push(side_b.at[turn(x, n + 1)], late_b.at[n], on_x[n]))
        return copies

    def third_start(copies):
        for copy in copies:
            copy.wait()
        a = side_a[z].astype(F32)
        b = side_b[x].astype(F32)
        for m in range(3):
            a = a + late_a[m].astype(F32)
            b = b + late_b[m].astype(F32)
        whole[0:HALF] = a.astype(BF)
        whole[HALF:UNIT] = b.astype(BF)
        return links.push(whole, whole_in, mate)

    steps = SLABS * count
    lax.fori_loop(0, steps, step, 0)
    pair_copies = pair_start(0)
    lax.fori_loop(steps, 2 * steps, step, 0)
    single_copy = single_start(0, pair_copies)
    second = second_start()
    pair_copies = pair_start(1)
    single_end(0, single_copy)
    third = third_start(second)
    single_copy = single_start(1, pair_copies)
    single_end(1, single_copy)
    third.wait()
    sum_ref[...] = (whole[...].astype(F32) + whole_in[...].astype(F32)).astype(BF)


def back(q, do, ot, lse, kv, extra, kpos, qpos, grads):
    shape = jax.ShapeDtypeStruct
    return pl.pallas_call(
        back_kernel,
        out_shape=[
            shape((KVH, ROWS, 128), F32),
            shape((KVH, HD, LANES), F32),
            shape((UNIT, 16, 128), BF),
        ],
        in_specs=[VMEM] * 8 + [ANY],
        out_specs=[VMEM] * 3,
        scratch_shapes=[
            pltpu.VMEM((KVH, LANES, 256), BF),
            pltpu.VMEM((KVH, LANES, 256), BF),
            pltpu.VMEM((OWN, 128), BF),
            pltpu.VMEM((KVH, ROWS, 128), F32),
            pltpu.VMEM((KVH, SLABS, SLAB, 128), BF),
            pltpu.VMEM((KVH, 3, SLAB, 128), BF),
            pltpu.VMEM((KVH, 4, 2 * ROWS, 128), BF),
            pltpu.VMEM((KVH, 3, 2 * ROWS, 128), BF),
            pltpu.VMEM((KVH, 2, ROWS, 128), F32),
            pltpu.VMEM((KVH, 2, ROWS, 128), BF),
            pltpu.VMEM((4, HALF, 16, 128), BF),
            pltpu.VMEM((4, HALF, 16, 128), BF),
            pltpu.VMEM((3, 4, HALF, 16, 128), BF),
            pltpu.VMEM((3, 4, HALF, 16, 128), BF),
            pltpu.VMEM((3, HALF, 16, 128), BF),
            pltpu.VMEM((3, HALF, 16, 128), BF),
            pltpu.VMEM((UNIT, 16, 128), BF),
            pltpu.VMEM((UNIT, 16, 128), BF),
            pltpu.SemaphoreType.DMA((48,)),
            pltpu.SemaphoreType.DMA((48,)),
            pltpu.SemaphoreType.DMA((2,)),
        ],
        compiler_params=pltpu.CompilerParams(
            vmem_limit_bytes=62 * MIB, collective_id=1, has_side_effects=True
        ),
        name="back",
    )(q, do, ot, lse, kv, extra, kpos, qpos, grads)


def last_kernel(
    sum_ref,
    dq_ref,
    dkv_ref,
    cos_ref,
    sin_ref,
    normed_ref,
    attended_ref,
    grad_attn_ref,
    grad_middle_ref,
    tokens_ref,
    wq_all,
    wk_all,
    wv_all,
    small_all,
    hidden_gain_ref,
    token_grad_ref,
    late_ref,
    thin_ref,
    whole_ref,
    natural,
    table,
    table_in,
    lines,
    lines_in,
    cols,
    cols_in,
    ends,
    ends_in,
    thin,
    send,
    recv,
    local,
):
    yl, x, z, yh, c = place()
    f = yh * 2 + c
    f_cross = (1 - yh) * 2 + c
    f_sib = yh * 2 + 1 - c
    f_far = (1 - yh) * 2 + 1 - c
    sib = at(yl, x, z, yh, 1 - c)
    cross = at(1 - yl, x, z, 1 - yh, c)
    far = at(1 - yl, x, z, 1 - yh, 1 - c)
    mate = at(1 - yl, x, z, yh, c)
    on_x = [at(yl, turn(x, d), z, yh, c) for d in (1, 2, 3)]
    on_z = [at(yl, x, turn(z, d), yh, c) for d in (1, 2, 3)]
    links = Links(send, recv)
    greet([sib, cross, far, mate] + on_x + on_z)

    shared = []
    for device, index in ((sib, f_sib), (cross, f_cross), (far, f_far)):
        shared.append(
            links.push(
                sum_ref.at[pl.ds(18 * index, 18)], whole_ref.at[x, z, pl.ds(18 * f, 18)], device
            )
        )
    keep = [
        pltpu.make_async_copy(
            sum_ref.at[pl.ds(18 * f, 18)], whole_ref.at[x, z, pl.ds(18 * f, 18)], local.at[0]
        ),
        pltpu.make_async_copy(
            sum_ref.at[72:UNIT], whole_ref.at[x, z, 72:UNIT], local.at[1]
        ),
    ]
    for copy in keep:
        copy.start()

    def assemble(tile):
        even, odd = tile * 2, tile * 2 + 1
        left = natural[even // GROUP, (even % GROUP) * ROWS : (even % GROUP + 1) * ROWS]
        right = natural[odd // GROUP, (odd % GROUP) * ROWS : (odd % GROUP + 1) * ROWS]
        return jnp.where(low, left, swap64(right))

    low = lanes_below((ROWS, 128), 64)
    cosine, sine = cos_ref[...], -sin_ref[...]
    for g in range(KVH):
        natural[g] = jnp.concatenate([dq_ref[g], jnp.zeros((64, LANES), F32)], axis=0).T
    grad_queries = jnp.concatenate(
        [
            turn_pairs(assemble(tile) * (1.0 / math.sqrt(HD)), cosine, sine)
            for tile in range(H // 2)
        ],
        axis=1,
    ).astype(BF)
    grad_keys = turn_pairs(jnp.where(low, dkv_ref[0], swap64(dkv_ref[1])), cosine, sine).astype(BF)
    grad_values = jnp.where(low, swap64(dkv_ref[0]), dkv_ref[1]).astype(BF)

    normed, attended = normed_ref[...], attended_ref[...]
    column = 0
    for left, right in (
        (normed, grad_queries),
        (normed, grad_keys),
        (normed, grad_values),
        (attended, grad_attn_ref[...]),
    ):
        product = dot_tn(left, right).astype(BF)
        for n in range(right.shape[1] // 128):
            table[column] = product[:, n * 128 : n * 128 + 128].reshape(4, SHARD, 128)
            column += 1
    beside = [
        links.push(table.at[:, 2 * n + 1 - c], table_in.at[n], sib) for n in range(2)
    ]

    inputs = tokens_ref[...].astype(F32)
    scale = lax.rsqrt(jnp.mean(inputs * inputs, axis=-1, keepdims=True) + EPSILON)

    def vector(row, count):
        return jnp.concatenate([small_all[n, row : row + 1, 0:count] for n in range(4)], axis=1)

    grad_normed = (
        dot_nt(grad_queries, wq_all[...].reshape(WIDTH, WIDTH))
        + dot_nt(grad_keys, wk_all[...].reshape(WIDTH, 128))
        + dot_nt(grad_values, wv_all[...].reshape(WIDTH, 128))
    )
    weighted = grad_normed * vector(1, SHARD)
    token_grad_ref[...] = (
        grad_middle_ref[...]
        + scale * weighted
        - inputs * (scale * scale * scale) * jnp.mean(weighted * inputs, axis=-1, keepdims=True)
    )
    thin[0, c] = jnp.concatenate(
        [
            jnp.sum(grad_queries.astype(F32), axis=0, keepdims=True),
            jnp.sum(grad_normed * inputs * scale, axis=0, keepdims=True),
            hidden_gain_ref[0:1],
            jnp.concatenate(
                [
                    jnp.sum(grad_keys.astype(F32), axis=0, keepdims=True),
                    jnp.sum(grad_values.astype(F32), axis=0, keepdims=True),
                    jnp.zeros((1, WIDTH - 256), F32),
                ],
                axis=1,
            ),
            jnp.zeros((4, WIDTH), F32),
        ],
        axis=0,
    )

    def thin_push(level, index, device):
        return links.push(thin.at[level, index], thin.at[level, index], device)

    thin_copies = [thin_push(0, c, sib)]

    for copy in keep + shared:
        copy.wait()
    spread = []
    for n in range(3):
        spread.append(
            links.push(whole_ref.at[x, z, 0:HALF], whole_ref.at[x, z, 0:HALF], on_z[n])
        )
        spread.append(
            links.push(whole_ref.at[x, z, HALF:UNIT], whole_ref.at[x, z, HALF:UNIT], on_x[n])
        )

    for copy in beside + thin_copies:
        copy.wait()

    def add_beside(n, _):
        for m in range(2):
            total = table[n, 2 * m + c].astype(F32) + table_in[m, n].astype(F32)
            lines[m, n] = total.astype(BF)
        return 0

    lax.fori_loop(0, 16, add_beside, 0)
    thin[1, x] = thin[0, 0] + thin[0, 1]
    along = []
    for n in range(3):
        xt, zt = turn(x, n + 1), turn(z, n + 1)
        along.append(links.push(lines.at[0, pl.ds(xt * 4, 4)], lines_in.at[0, n], on_x[n]))
        for m in range(4):
            along.append(
                links.push(lines.at[1, m * 4 + zt], lines_in.at[1, n, m], on_z[n])
            )
        along.append(thin_push(1, x, on_x[n]))
    for copy in along:
        copy.wait()
    for m in range(4):
        a = lines[0, x * 4 + m].astype(F32)
        b = lines[1, m * 4 + z].astype(F32)
        for n in range(3):
            a = a + lines_in[0, n, m].astype(F32)
            b = b + lines_in[1, n, m].astype(F32)
        cols[0, m] = a.astype(BF)
        cols[1, m] = b.astype(BF)
    thin[2, z] = (thin[1, 0] + thin[1, 1]) + (thin[1, 2] + thin[1, 3])
    along = []
    for n in range(3):
        along.append(links.push(cols.at[0, turn(z, n + 1)], cols_in.at[0, n], on_z[n]))
        along.append(links.push(cols.at[1, turn(x, n + 1)], cols_in.at[1, n], on_x[n]))
        along.append(thin_push(2, z, on_z[n]))
    for copy in along:
        copy.wait()
    a = cols[0, z].astype(F32)
    b = cols[1, x].astype(F32)
    for n in range(3):
        a = a + cols_in[0, n].astype(F32)
        b = b + cols_in[1, n].astype(F32)
    ends[0] = a.astype(BF)
    ends[1] = b.astype(BF)
    thin[3, yh] = (thin[2, 0] + thin[2, 1]) + (thin[2, 2] + thin[2, 3])
    along = [links.push(ends.at[1 - yh], ends_in.at[0], cross), thin_push(3, yh, cross)]
    for copy in along:
        copy.wait()
    ends[2] = (ends[yh].astype(F32) + ends_in[0].astype(F32)).astype(BF)
    thin[4, yl] = thin[3, 0] + thin[3, 1]
    along = [links.push(ends.at[2], ends_in.at[1], mate), thin_push(4, yl, mate)]
    for copy in along:
        copy.wait()
    late_ref[x, z] = (ends[2].astype(F32) + ends_in[1].astype(F32)).astype(BF)
    thin_ref[...] = thin[4, 0] + thin[4, 1]

    for copy in spread:
        copy.wait()
    cut = SHARD // 2
    last = []
    for n in range(3):
        last.append(links.push(late_ref.at[x, z, 0:cut], late_ref.at[x, z, 0:cut], on_z[n]))
        last.append(links.push(late_ref.at[x, z, cut:], late_ref.at[x, z, cut:], on_x[n]))
    spread = []
    for n in range(3):
        spread.append(links.push(whole_ref.at[x, :, 0:HALF], whole_ref.at[x, :, 0:HALF], on_x[n]))
        spread.append(
            links.push(whole_ref.at[:, z, HALF:UNIT], whole_ref.at[:, z, HALF:UNIT], on_z[n])
        )
    for copy in last:
        copy.wait()
    last = []
    for n in range(3):
        last.append(links.push(late_ref.at[x, :, 0:cut], late_ref.at[x, :, 0:cut], on_x[n]))
        last.append(links.push(late_ref.at[:, z, cut:], late_ref.at[:, z, cut:], on_z[n]))
    for copy in last + spread:
        copy.wait()


def last_call(*operands):
    shape = jax.ShapeDtypeStruct
    return pl.pallas_call(
        last_kernel,
        out_shape=[
            shape((ROWS, WIDTH), F32),
            shape((4, 4, SHARD, 128), BF),
            shape((8, WIDTH), F32),
            shape((4, 4, UNIT, 16, 128), BF),
        ],
        in_specs=[VMEM] * 15,
        out_specs=[VMEM] * 3 + [ANY],
        scratch_shapes=[
            pltpu.VMEM((KVH, LANES, 128), F32),
            pltpu.VMEM((16, 4, SHARD, 128), BF),
            pltpu.VMEM((2, 16, SHARD, 128), BF),
            pltpu.VMEM((2, 16, SHARD, 128), BF),
            pltpu.VMEM((2, 3, 4, SHARD, 128), BF),
            pltpu.VMEM((2, 4, SHARD, 128), BF),
            pltpu.VMEM((2, 3, SHARD, 128), BF),
            pltpu.VMEM((3, SHARD, 128), BF),
            pltpu.VMEM((2, SHARD, 128), BF),
            pltpu.VMEM((5, 4, 8, WIDTH), F32),
            pltpu.SemaphoreType.DMA((72,)),
            pltpu.SemaphoreType.DMA((72,)),
            pltpu.SemaphoreType.DMA((2,)),
        ],
        compiler_params=pltpu.CompilerParams(
            vmem_limit_bytes=58 * MIB, collective_id=2, has_side_effects=True
        ),
        name="last",
    )(*operands)


def tables(block_order, ctx):
    own_blocks = lax.dynamic_slice_in_dim(block_order, ctx * 2, 2)
    own_pos = (own_blocks[:, None] * BLK + jnp.arange(BLK, dtype=jnp.int32)[None, :]).reshape(ROWS)
    own_pos = own_pos.astype(F32)
    frequency = jnp.exp(jnp.arange(HD // 2, dtype=F32) * (-2.0 * math.log(THETA) / HD))
    angles = own_pos[:, None] * frequency[None, :]
    cosine, sine = jnp.cos(angles), jnp.sin(angles)
    cosine = jnp.concatenate([cosine] * 4, axis=1)
    sine = jnp.concatenate([-sine, sine] * 2, axis=1)
    slots = jnp.arange(64, dtype=jnp.int32)
    shown = (block_order[:, None] < own_blocks[None, :]) & (slots // 2 != ctx)[:, None]
    lane = jnp.arange(128)[None, :]
    bias = jnp.where(shown, 0.0, MASKED)
    extra = jnp.where(lane == 0, bias[:, 0:1], jnp.where(lane == 1, bias[:, 1:2], 0.0))
    extra = jnp.where((lane >= 2) & (lane < 5), 1.0, extra).astype(F32).reshape(2, 4, 4, 2, 128)
    extra = jnp.stack(
        [
            extra.transpose(1, 2, 0, 3, 4).reshape(64, 128),
            extra.transpose(2, 1, 0, 3, 4).reshape(64, 128),
        ]
    )
    kpos = jnp.pad(own_pos, (0, OWN - ROWS), constant_values=1e9)
    kpos = jnp.broadcast_to(kpos[:, None], (OWN, 128))
    qpos = jnp.pad(jnp.tile(own_pos, GROUP), (0, LANES - GROUP * ROWS), constant_values=5e8)
    qpos = jnp.broadcast_to(qpos[None, :], (8, LANES))
    return cosine, sine, extra, kpos, qpos


def by_head(rows):
    split = rows.reshape(ROWS, KVH, GROUP, HD).transpose(1, 2, 0, 3)
    return jnp.pad(split.reshape(KVH, GROUP * ROWS, HD), ((0, 0), (0, LANES - GROUP * ROWS), (0, 0)))


def body(
    tokens,
    block_order,
    query_weight,
    key_weight,
    value_weight,
    output_weight,
    gate_weight,
    up_weight,
    down_weight,
    query_bias,
    key_bias,
    value_bias,
    attention_gain,
    hidden_gain,
    cotangent,
):
    ctx, f = lax.axis_index("ctx"), lax.axis_index("fsdp")
    cosine, sine, extra, kpos, qpos = tables(block_order, ctx)

    def line(vector):
        return jnp.pad(vector.astype(F32), (0, 256 - vector.shape[0]))

    small = jnp.stack(
        [line(v) for v in (query_bias, attention_gain, hidden_gain, key_bias, value_bias)]
        + [jnp.zeros((256,), F32)] * 3
    )
    (
        attended,
        ot,
        lse,
        q,
        kv,
        normed,
        wq_all,
        wk_all,
        wv_all,
        small_all,
        wo_all,
        gate_all,
        up_all,
        cot_all,
    ) = front(
        tokens[0],
        query_weight,
        key_weight,
        value_weight,
        small,
        cosine,
        sine,
        extra,
        kpos,
        qpos,
        output_weight,
        gate_weight,
        up_weight,
        cotangent[0],
    )
    out_weight = wo_all.reshape(WIDTH, WIDTH)
    gate_cols = gate_all.reshape(WIDTH, WINDOW)
    up_cols = up_all.reshape(WIDTH, WINDOW)
    shift = 64 * (f % 2)
    down_rows = lax.dynamic_update_slice_in_dim(
        jnp.zeros((WINDOW, WIDTH), BF), down_weight, shift, axis=0
    )
    inputs = tokens[0].astype(F32)
    second_gain = small_all[:, 2, :SHARD].reshape(WIDTH)
    middle = inputs + dot(attended, out_weight)
    second_scale = lax.rsqrt(jnp.mean(middle * middle, axis=-1, keepdims=True) + EPSILON)
    normed_two = (middle * second_scale * second_gain).astype(BF)
    grad_out = cotangent[0].astype(F32)
    grad_all = lax.all_gather(cotangent[0], "fsdp", axis=0, tiled=True)
    normed_all = lax.all_gather(normed_two, "fsdp", axis=0, tiled=True)
    gate_pre = dot(normed_all, gate_cols)
    upward = dot(normed_all, up_cols)
    sigmoid = jax.nn.sigmoid(gate_pre)
    swish = gate_pre * sigmoid
    hidden = (swish * upward).astype(BF)
    out_part = dot(hidden, down_rows)
    output = middle + lax.psum_scatter(
        out_part.astype(BF), "fsdp", scatter_dimension=0, tiled=True
    ).astype(F32)
    grad_hidden = dot_nt(grad_all, down_rows)
    grad_gate = (grad_hidden * upward * sigmoid * (1.0 + gate_pre * (1.0 - sigmoid))).astype(BF)
    grad_up = (grad_hidden * swish).astype(BF)
    two_part = dot_nt(grad_gate, gate_cols) + dot_nt(grad_up, up_cols)
    grad_two = lax.psum_scatter(
        two_part.astype(BF), "fsdp", scatter_dimension=0, tiled=True
    ).astype(F32)
    gate_up_grad = dot_tn(normed_all, jnp.concatenate([grad_gate, grad_up], axis=1)).astype(BF)
    down_grad = lax.dynamic_slice_in_dim(dot_tn(hidden, grad_all), shift, UNITS).astype(BF)
    grads = gate_up_grad.reshape(4, 14, 16, 20, 128).transpose(0, 1, 3, 2, 4).reshape(4, 280, 16, 128)
    grads = jnp.pad(grads, ((0, 0), (0, 8), (0, 0), (0, 0))).reshape(4, 16, 18, 16, 128)
    grads = grads.transpose(1, 0, 2, 3, 4).reshape(16, 72, 16, 128)
    downs = down_grad.reshape(76, 16, 7, 128).transpose(0, 2, 1, 3).reshape(532, 16, 128)
    downs = jnp.pad(downs, ((0, 12), (0, 0), (0, 0))).reshape(16, 34, 16, 128)
    grads = jnp.concatenate([grads, downs], axis=1).reshape(4, 4, UNIT, 16, 128)

    hidden_gain_part = jnp.sum(grad_two * middle * second_scale, axis=0)
    weighted_two = grad_two * second_gain
    grad_middle = (
        grad_out
        + second_scale * weighted_two
        - middle
        * (second_scale * second_scale * second_scale)
        * jnp.mean(weighted_two * middle, axis=-1, keepdims=True)
    )
    grad_attn = grad_middle.astype(BF)
    grad_attended = by_head(dot_nt(grad_attn, out_weight).astype(BF))
    grad_attended = jnp.concatenate([jnp.zeros_like(grad_attended), grad_attended], axis=-1)
    dkv, dq, total = back(q, grad_attended, ot, lse, kv, extra, kpos, qpos, grads)
    token_grad, late, thin, whole = last_call(
        total,
        dq,
        dkv,
        cosine,
        sine,
        normed,
        attended,
        grad_attn,
        grad_middle,
        tokens[0],
        wq_all,
        wk_all,
        wv_all,
        small_all,
        jnp.broadcast_to(hidden_gain_part[None], (8, WIDTH)),
    )
    late = late.reshape(16, SHARD, 128).transpose(1, 0, 2).reshape(SHARD, 2048).astype(F32)
    whole = whole.reshape(16, UNIT, 16, 128)
    down_out = whole[:, 72:].reshape(544, 16, 128)[:532].reshape(76, 7, 16, 128)
    down_out = down_out.transpose(0, 2, 1, 3).reshape(UNITS, WIDTH).astype(F32)
    both = []
    for n in range(4):
        block = whole[:, 18 * n : 18 * n + 18].reshape(288, 16, 128)[:280].reshape(14, 20, 16, 128)
        block = block.transpose(0, 2, 1, 3).reshape(SHARD, 2 * WINDOW)
        start = 128 * ((19 * n) // 2)
        both.append(
            [
                jnp.pad(half, ((0, 0), (start, 4 * UNITS - WINDOW - start)))
                for half in (block[:, :WINDOW], block[:, WINDOW:])
            ]
        )
    gate_out, up_out = (
        ((both[0][n] + both[1][n]) + (both[2][n] + both[3][n])).astype(F32) for n in range(2)
    )
    wide, narrow = WIDTH, 128

    def share(row, start, count):
        part = count // 4
        return lax.dynamic_slice_in_dim(thin[row], start + f * part, part)

    return (
        output.astype(BF)[None],
        token_grad[None],
        late[:, :wide],
        late[:, wide : wide + narrow],
        late[:, wide + narrow : wide + 2 * narrow],
        late[:, wide + 2 * narrow :],
        gate_out,
        up_out,
        down_out,
        share(0, 0, wide),
        share(3, 0, narrow),
        share(3, narrow, narrow),
        share(1, 0, wide),
        share(2, 0, wide),
    )


def solution(mesh):
    rows = P("fsdp", "ctx", None)
    matrix = P("fsdp", None)
    vector = P("fsdp")
    placed = (rows, P()) + (matrix,) * 7 + (vector,) * 5 + (rows,)
    return jax.shard_map(
        body,
        mesh=mesh,
        in_specs=placed,
        out_specs=(rows, rows) + (matrix,) * 7 + (vector,) * 5,
        check_vma=False,
    )
```

```python
import functools
import math

import jax
import jax.numpy as jnp
from jax import lax
from jax.experimental import pallas as pl
from jax.experimental.pallas import tpu as pltpu
from jax.sharding import PartitionSpec as P

H = 14
KVH = 2
GROUP = H // KVH
HD = 64
ROWS = 192
BLK = 96
LANES = 1408
SLAB = 1536
SLABS = 4
OWN = 256

EPSILON = 1e-06
THETA = 1000000.0
MASKED = -1e30

BF = jnp.bfloat16
F32 = jnp.float32
VMEM = pl.BlockSpec(memory_space=pltpu.VMEM)
NT = (((1,), (1,)), ((), ()))
TN = (((0,), (0,)), ((), ()))


def dot(left, right):
    return jnp.dot(left, right, preferred_element_type=F32)


def dot_nt(left, right):
    return lax.dot_general(left, right, NT, preferred_element_type=F32)


def dot_tn(left, right):
    return lax.dot_general(left, right, TN, preferred_element_type=F32)


def thirds(value):
    high = value.astype(BF).astype(F32)
    rest = value - high
    middle = rest.astype(BF).astype(F32)
    low = (rest - middle).astype(BF).astype(F32)
    return high, middle, low


MESH = pl.DeviceIdType.MESH
ANY = pl.BlockSpec(memory_space=pl.ANY)
WINDOW = 1280
UNITS = 1216
SHARD = 224
WIDTH = 896
MIB = 2**20


def place():
    ctx, f = lax.axis_index("ctx"), lax.axis_index("fsdp")
    return lax.div(ctx, 16), lax.rem(lax.div(ctx, 4), 4), lax.rem(ctx, 4), lax.div(f, 2), lax.rem(f, 2)


def at(yl, x, z, yh, c):
    return ((yl * 4 + x) * 4 + z, yh * 2 + c)


def turn(index, by):
    return lax.rem(index + by, 4)


def greet(devices):
    barrier = pltpu.get_barrier_semaphore()
    for device in devices:
        pl.semaphore_signal(barrier, inc=1, device_id=device, device_id_type=MESH)
    pl.semaphore_wait(barrier, len(devices))


class Links:
    def __init__(self, send, recv):
        self.send, self.recv, self.used = send, recv, 0

    def reserve(self, count):
        first = self.used
        self.used += count
        return first

    def copy(self, src, dst, device, slot):
        return pltpu.make_async_remote_copy(
            src_ref=src,
            dst_ref=dst,
            send_sem=self.send.at[slot],
            recv_sem=self.recv.at[slot],
            device_id=device,
            device_id_type=MESH,
        )

    def push(self, src, dst, device):
        copy = self.copy(src, dst, device, self.reserve(1))
        copy.start()
        return copy


class RingSum:
    def __init__(self, links, me, devices, chunk, relay, landing, staged):
        self.links, self.me, self.devices, self.chunk = links, me, devices, chunk
        self.relay, self.landing, self.staged = relay, landing, staged
        self.base = links.reserve(6)

    def copies(self, wanted):
        me, right, left = self.me, self.devices[0], self.devices[2]
        across, after, before = turn(me, 2), turn(me, 1), turn(me, 3)
        chunk, landing, staged = self.chunk, self.landing, self.staged
        moves = (
            (chunk(across, 0), self.relay.at[0], right),
            (chunk(across, 1), self.relay.at[1], left),
            (chunk(after, 1), landing.at[0, 1], right),
            (chunk(before, 0), landing.at[1, 0], left),
            (staged.at[0], landing.at[0, 0], right),
            (staged.at[1], landing.at[1, 1], left),
        )
        return [self.links.copy(*moves[n], self.base + n) for n in wanted]

    def start(self):
        for copy in self.copies((0, 1, 2, 3)):
            copy.start()

    def merge(self):
        for n in range(2):
            came, on = self.copies((n, 4 + n))
            came.wait_recv()
            self.staged[n] = (self.staged[n].astype(F32) + self.relay[n].astype(F32)).astype(BF)
            on.start()

    def finish(self):
        for copy in self.copies((0, 1)):
            copy.wait_send()
        for copy in self.copies((2, 3, 4, 5)):
            copy.wait()

    def arrived(self, half):
        return self.landing[0, half].astype(F32) + self.landing[1, half].astype(F32)


def lanes_below(shape, bound):
    return lax.broadcasted_iota(jnp.int32, shape, 1) < bound


def swap64(value):
    return pltpu.roll(value, 64, axis=1)


def turn_pairs(value, cosine, sine):
    lane = lax.broadcasted_iota(jnp.int32, value.shape, 1)
    other = jnp.where(
        lax.rem(lane, 64) < 32, pltpu.roll(value, 96, axis=1), pltpu.roll(value, 32, axis=1)
    )
    return value * cosine + other * sine


def key_extra(rows):
    count = rows.shape[0]
    return jnp.broadcast_to(rows[:, None, :], (count, BLK, 128)).reshape(count * BLK, 128).astype(BF)


def own_extra():
    lane = lax.broadcasted_iota(jnp.int32, (OWN, 128), 1)
    return jnp.where((lane >= 2) & (lane < 5), 1.0, 0.0).astype(BF)


def window_start(f):
    return pl.multiple_of(lax.div(19 * f, 2) * 128, 128)


def front_kernel(
    tokens_ref,
    wq_ref,
    wk_ref,
    wv_ref,
    small_ref,
    cos_ref,
    sin_ref,
    extra_ref,
    kpos_ref,
    qpos_ref,
    wo_ref,
    gate_ref,
    up_ref,
    cot_ref,
    attended_ref,
    ot_ref,
    lse_ref,
    q_ref,
    kv_ref,
    normed_ref,
    wq_all,
    wk_all,
    wv_all,
    small_all,
    wo_all,
    gate_all,
    up_all,
    cot_all,
    own,
    acc,
    top,
    natural,
    send,
    recv,
    local,
):
    yl, x, z, yh, c = place()
    f = yh * 2 + c
    f_cross = (1 - yh) * 2 + c
    f_sib = yh * 2 + 1 - c
    f_far = (1 - yh) * 2 + 1 - c
    sib = at(yl, x, z, yh, 1 - c)
    cross = at(1 - yl, x, z, 1 - yh, c)
    far = at(1 - yl, x, z, 1 - yh, 1 - c)
    mate = at(1 - yl, x, z, yh, c)
    on_x = [at(yl, turn(x, d), z, yh, c) for d in (1, 2, 3)]
    on_z = [at(yl, x, turn(z, d), yh, c) for d in (1, 2, 3)]
    links = Links(send, recv)
    greet([sib, cross, far, mate] + on_x + on_z)

    def gather_start(pairs):
        return [
            (links.push(mine, whole.at[f], sib), links.push(mine, whole.at[f], cross), whole)
            for mine, whole in pairs
        ]

    def gather_relay(started):
        relays = []
        for _, over, whole in started:
            over.wait_recv()
            relays.append(links.push(whole.at[f_cross], whole.at[f_cross], sib))
        return relays

    def gather_end(started, relays):
        for beside, over, _ in started:
            beside.wait()
            over.wait_send()
        for relay in relays:
            relay.wait()

    first = gather_start(
        [(wq_ref, wq_all), (wk_ref, wk_all), (wv_ref, wv_all), (small_ref, small_all)]
    )
    keep = []
    for n, (mine, whole) in enumerate(
        [(wo_ref, wo_all.at[f]), (cot_ref, cot_all.at[f])]
        + [
            (ref.at[:, pl.ds(window_start(f), WINDOW)], whole.at[f])
            for ref, whole in ((gate_ref, gate_all), (up_ref, up_all))
        ]
    ):
        copy = pltpu.make_async_copy(mine, whole, local.at[n])
        copy.start()
        keep.append(copy)
    wq_all[f] = wq_ref[...]
    wk_all[f] = wk_ref[...]
    wv_all[f] = wv_ref[...]
    small_all[f] = small_ref[...]
    inputs = tokens_ref[...].astype(F32)
    scale = lax.rsqrt(jnp.mean(inputs * inputs, axis=-1, keepdims=True) + EPSILON)
    relays = gather_relay(first)
    def quarter(n, start):
        rows = pl.ds(pl.multiple_of(lax.div(n, 2) * 112, 16), 112)
        return rows, pl.ds(pl.multiple_of(start + lax.rem(n, 2) * 640, 128), 640)

    spread = []
    for ref, whole, n in ((gate_ref, gate_all, x), (up_ref, up_all, z)):
        rows, lanes = quarter(n, 0)
        for device, index in ((cross, f_cross), (far, f_far)):
            part = ref.at[quarter(n, window_start(index))]
            spread.append(links.push(part, whole.at[f, rows, lanes], device))
    for ref, whole in ((gate_ref, gate_all), (up_ref, up_all)):
        part = ref.at[:, pl.ds(window_start(f_sib), WINDOW)]
        spread.append(links.push(part, whole.at[f], sib))
    gather_end(first, relays)

    def vector(row, count):
        return jnp.concatenate([small_all[n, row : row + 1, 0:count] for n in range(4)], axis=1)

    normed = (inputs * scale * vector(1, SHARD)).astype(BF)
    normed_ref[...] = normed
    cosine, sine = cos_ref[...], sin_ref[...]
    low = lanes_below((ROWS, 128), 64)

    queries = dot(normed, wq_all[...].reshape(WIDTH, WIDTH)) + vector(0, SHARD)
    keys = dot(normed, wk_all[...].reshape(WIDTH, 128)) + vector(3, 32)
    values = dot(normed, wv_all[...].reshape(WIDTH, 128)) + vector(4, 32)
    keys = turn_pairs(keys, cosine, sine).astype(BF).astype(F32)
    values = values.astype(BF).astype(F32)
    own[...] = jnp.zeros(own.shape, BF)
    own[0, 0:ROWS] = jnp.where(low, keys, swap64(values)).astype(BF)
    own[1, 0:ROWS] = jnp.where(low, swap64(keys), values).astype(BF)

    slab_of = (x, z)
    spot = [
        pl.ds(pl.multiple_of((z * 2 + yl) * ROWS, ROWS), ROWS),
        pl.ds(pl.multiple_of((x * 2 + yl) * ROWS, ROWS), ROWS),
    ]
    pair = [
        pl.ds(pl.multiple_of(z * 2 * ROWS, 2 * ROWS), 2 * ROWS),
        pl.ds(pl.multiple_of(x * 2 * ROWS, 2 * ROWS), 2 * ROWS),
    ]
    mates = [
        links.push(own.at[g, 0:ROWS], kv_ref.at[g, slab_of[g], spot[g]], mate) for g in range(KVH)
    ]
    for g in range(KVH):
        kv_ref[g, slab_of[g], spot[g], :] = own[g, 0:ROWS]

    for tile in range(H // 2):
        part = turn_pairs(queries[:, tile * 128 : tile * 128 + 128], cosine, sine)
        part = part.astype(BF).astype(F32) * (1.0 / math.sqrt(HD))
        for half in range(2):
            head = tile * 2 + half
            j = head % GROUP
            mine = part if half == 0 else swap64(part)
            q_ref[head // GROUP, j * ROWS : (j + 1) * ROWS, 0:128] = jnp.where(
                low, mine, 0.0
            ).astype(BF)
    row = lax.broadcasted_iota(jnp.int32, (LANES, 128), 0)
    lane = lax.broadcasted_iota(jnp.int32, (LANES, 128), 1)
    block = lax.rem(lax.div(row, BLK), 2)
    hot = jnp.where((block == lane) & (row < GROUP * ROWS), 1.0, 0.0).astype(BF)
    for g in range(KVH):
        q_ref[g, :, 128:256] = hot
        q_ref[g, GROUP * ROWS :, 0:128] = jnp.zeros((LANES - GROUP * ROWS, 128), BF)

    def mix(g, keys, scores):
        old = top[g, 0:1]
        new = jnp.maximum(old, jnp.max(scores, axis=0, keepdims=True))
        weights = jnp.exp(scores - new).astype(BF)
        acc[g] = acc[g] * jnp.exp(old - new) + dot(keys.T[64:136], weights)
        top[g, 0:1] = new

    top[...] = jnp.full(top.shape, MASKED, F32)
    acc[...] = jnp.zeros(acc.shape, F32)
    for copy in mates:
        copy.wait()
    pairs = [
        links.push(kv_ref.at[0, x, pair[0]], kv_ref.at[0, x, pair[0]], device) for device in on_z
    ] + [links.push(kv_ref.at[1, z, pair[1]], kv_ref.at[1, z, pair[1]], device) for device in on_x]
    mask = jnp.where(kpos_ref[:, 0:1] <= qpos_ref[0:1], 0.0, MASKED)
    for g in range(KVH):
        keys = jnp.concatenate([own[g], own_extra()], axis=1)
        mix(g, keys, dot_nt(keys, q_ref[g]) + mask)
    for copy in pairs:
        copy.wait()
    base = links.reserve(6)

    def slab_copy(g, d, slab):
        device = (
            ((yl * 4 + jnp.where(g == 0, turn(x, d), x)) * 4 + jnp.where(g == 0, z, turn(z, d))),
            f,
        )
        return links.copy(kv_ref.at[g, slab], kv_ref.at[g, slab], device, base + g * 3 + d - 1)

    slabs = [slab_copy(g, d, slab_of[g]) for d in (1, 3, 2) for g in range(KVH)]
    for copy in slabs:
        copy.start()
    again = links.reserve(12)

    def quarters():
        copies = []
        for whole, n, devices in ((gate_all, x, on_x), (up_all, z, on_z)):
            rows, lanes = quarter(n, 0)
            for index in (f_cross, f_far):
                part = whole.at[index, rows, lanes]
                copies += [
                    links.copy(part, part, device, again + len(copies) + m)
                    for m, device in enumerate(devices)
                ]
        return copies

    second = links.reserve(4)

    def outer():
        copies = []
        for mine, whole in ((wo_ref, wo_all), (cot_ref, cot_all)):
            for device in (sib, cross):
                copies.append(links.copy(mine, whole.at[f], device, second + len(copies)))
        return copies

    def spread_on():
        for copy in spread[0:4]:
            copy.wait_recv()
        for copy in quarters() + outer():
            copy.start()

    def step(i, _):
        g, n = lax.rem(i, 2), lax.div(i, 2)
        d = jnp.where(n == 2, 3, jnp.where(n == 3, 2, n))
        slab = turn(jnp.where(g == 0, x, z), d)

        @pl.when(n > 0)
        def _():
            slab_copy(g, 4 - d, slab).wait_recv()

        rows = extra_ref[g, pl.ds(pl.multiple_of(slab * 16, 16), 16), :]
        keys = jnp.concatenate([kv_ref[g, slab], key_extra(rows)], axis=1)
        mix(g, keys, dot_nt(keys, q_ref[g]))
        pl.when(i == 0)(spread_on)
        return 0

    lax.fori_loop(0, 8, step, 0)
    for copy in slabs:
        copy.wait_send()
    outers = outer()
    second = list(zip(outers[0::2], outers[1::2], (wo_all, cot_all)))
    relays = gather_relay(second)

    for g in range(KVH):
        total = acc[g, 66:67]
        out = acc[g, 0:64] / total
        ot_ref[g] = out
        lse_ref[g] = jnp.broadcast_to(top[g, 0:1] + jnp.log(total), (8, LANES))
        natural[g] = jnp.concatenate([out, jnp.zeros((64, LANES), F32)], axis=0).T
    for tile in range(H // 2):
        even, odd = tile * 2, tile * 2 + 1
        left = natural[even // GROUP, (even % GROUP) * ROWS : (even % GROUP + 1) * ROWS]
        right = natural[odd // GROUP, (odd % GROUP) * ROWS : (odd % GROUP + 1) * ROWS]
        attended_ref[:, tile * 128 : tile * 128 + 128] = jnp.where(
            low, left, swap64(right)
        ).astype(BF)
    for copy in spread[0:4]:
        copy.wait_send()
    for copy in spread[4:] + quarters():
        copy.wait()
    gather_end(second, relays)
    for copy in keep:
        copy.wait()


def front(tokens, wq, wk, wv, small, cosine, sine, extra, kpos, qpos, wo, gate, up, cot):
    shape = jax.ShapeDtypeStruct
    return pl.pallas_call(
        front_kernel,
        out_shape=[
            shape((ROWS, WIDTH), BF),
            shape((KVH, HD, LANES), F32),
            shape((KVH, 8, LANES), F32),
            shape((KVH, LANES, 256), BF),
            shape((KVH, SLABS, SLAB, 128), BF),
            shape((ROWS, WIDTH), BF),
            shape((4, SHARD, WIDTH), BF),
            shape((4, SHARD, 128), BF),
            shape((4, SHARD, 128), BF),
            shape((4, 8, 256), F32),
            shape((4, SHARD, WIDTH), BF),
            shape((4, SHARD, WINDOW), BF),
            shape((4, SHARD, WINDOW), BF),
            shape((4, ROWS, WIDTH), BF),
        ],
        in_specs=[VMEM] * 10 + [ANY] * 4,
        out_specs=[VMEM] * 10 + [ANY] * 4,
        scratch_shapes=[
            pltpu.VMEM((KVH, OWN, 128), BF),
            pltpu.VMEM((KVH, 72, LANES), F32),
            pltpu.VMEM((KVH, 8, LANES), F32),
            pltpu.VMEM((KVH, LANES, 128), F32),
            pltpu.SemaphoreType.DMA((64,)),
            pltpu.SemaphoreType.DMA((64,)),
            pltpu.SemaphoreType.DMA((4,)),
        ],
        compiler_params=pltpu.CompilerParams(
            vmem_limit_bytes=58 * MIB, collective_id=0, has_side_effects=True
        ),
        name="front",
    )(tokens, wq, wk, wv, small, cosine, sine, extra, kpos, qpos, wo, gate, up, cot)


def tile_stores(ref, value, first_row, first_lane, place_of):
    for r in range(value.shape[0] // 16):
        for n in range(value.shape[1] // 128):
            p, k = place_of(first_row + r, first_lane + n)
            ref[p // 4, p % 4, k] = value[r * 16 : r * 16 + 16, n * 128 : n * 128 + 128]


def gate_place(r, n):
    t = (r % 14) * 20 + n
    return t // 18, 18 * (r // 14) + t % 18


def down_place(r, n):
    t = r * 7 + n
    return t // 34, t % 34


def middle_kernel(
    attended_ref,
    tokens_ref,
    small_all,
    wo_all,
    cot_all,
    gate_hbm,
    up_hbm,
    down_hbm,
    output_ref,
    grad_middle_ref,
    grad_attn_ref,
    gain_ref,
    do_ref,
    grads_ref,
    sum_a_ref,
    sum_b_ref,
    gate_ref,
    up_ref,
    down_ref,
    blocks,
    back_gate,
    hidden_ref,
    down_grad,
    two,
    two_in,
    out,
    out_in,
    downs,
    relay,
    landing,
    staged,
    send,
    recv,
    local,
):
    yl, x, z, yh, c = place()
    f = yh * 2 + c
    f_cross = (1 - yh) * 2 + c
    f_sib = yh * 2 + 1 - c
    f_far = (1 - yh) * 2 + 1 - c
    sib = at(yl, x, z, yh, 1 - c)
    cross = at(1 - yl, x, z, 1 - yh, c)
    links = Links(send, recv)
    loads = [
        pltpu.make_async_copy(gate_hbm, gate_ref, local.at[0]),
        pltpu.make_async_copy(up_hbm, up_ref, local.at[1]),
        pltpu.make_async_copy(
            down_hbm, down_ref.at[pl.ds(pl.multiple_of(64 * c, 64), UNITS)], local.at[2]
        ),
    ]
    for copy in loads:
        copy.start()
    down_ref[pl.ds(pl.multiple_of((1 - c) * UNITS, 64), 64), :] = jnp.zeros((64, WIDTH), BF)
    on_x = [at(yl, turn(x, d), z, yh, c) for d in (1, 2, 3)]
    on_z = [at(yl, x, turn(z, d), yh, c) for d in (1, 2, 3)]
    greet([sib, cross, on_x[0], on_x[2], on_z[0], on_z[2]])
    rings = (
        RingSum(
            links,
            x,
            on_x,
            lambda n, half: downs.at[n, 2 * half : 2 * half + 2, 0:17],
            relay.at[0],
            landing.at[0],
            staged.at[0],
        ),
        RingSum(
            links,
            z,
            on_z,
            lambda n, half: downs.at[2 * half : 2 * half + 2, n, 17:34],
            relay.at[1],
            landing.at[1],
            staged.at[1],
        ),
    )

    gain = jnp.concatenate([small_all[n, 2:3, 0:SHARD] for n in range(4)], axis=1)
    wo = wo_all[...].reshape(WIDTH, WIDTH)
    middle = tokens_ref[...].astype(F32) + dot(attended_ref[...], wo)
    scale = lax.rsqrt(jnp.mean(middle * middle, axis=-1, keepdims=True) + EPSILON)
    grad_middle_ref[...] = middle
    blocks[0] = (middle * scale * gain).astype(BF)
    beside = links.push(blocks.at[0], blocks.at[1], sib)
    over = links.push(blocks.at[0], blocks.at[2], cross)
    order = ((f, f_sib), (f_cross, f_far))
    for copy in loads:
        copy.wait()

    def grads_of(p):
        return jnp.concatenate([cot_all[order[p][0]], cot_all[order[p][1]]], axis=0)

    def hidden_grad(p):
        return dot_nt(grads_of(p), down_ref[...])

    def units(p, grad_hidden):
        rows = slice(p * 2 * ROWS, (p + 1) * 2 * ROWS)
        block = blocks[2 * p : 2 * p + 2].reshape(2 * ROWS, WIDTH)
        gate_pre = dot(block, gate_ref[...].reshape(WIDTH, WINDOW))
        upward = dot(block, up_ref[...].reshape(WIDTH, WINDOW))
        sigmoid = 1.0 / (1.0 + jnp.exp(-gate_pre))
        swish = gate_pre * sigmoid
        hidden_ref[rows] = (swish * upward).astype(BF)
        back_gate[rows, 0:WINDOW] = (
            grad_hidden * upward * sigmoid * (1.0 + gate_pre * (1.0 - sigmoid))
        ).astype(BF)
        back_gate[rows, WINDOW:] = (grad_hidden * swish).astype(BF)

    def two_part(p):
        rows = slice(p * 2 * ROWS, (p + 1) * 2 * ROWS)
        return dot_nt(back_gate[rows, 0:WINDOW], gate_ref[...].reshape(WIDTH, WINDOW)) + dot_nt(
            back_gate[rows, WINDOW:], up_ref[...].reshape(WIDTH, WINDOW)
        )

    def out_part(p):
        rows = slice(p * 2 * ROWS, (p + 1) * 2 * ROWS)
        return dot(hidden_ref[rows], down_ref[...])

    beside.wait()
    units(0, hidden_grad(0))
    part = two_part(0)
    two_mine = part[0:ROWS]
    two[0] = part[ROWS:].astype(BF)
    two_copies = [links.push(two.at[0], two_in.at[0], sib)]
    far_grad = hidden_grad(1)
    over.wait()
    relay = links.push(blocks.at[2], blocks.at[3], sib)
    relay.wait()
    units(1, far_grad)
    part = two_part(1)
    two[1] = part[ROWS:].astype(BF)
    copy = links.push(two.at[1], two_in.at[1], sib)
    two_cross = part[0:ROWS]
    part = out_part(1)
    out[1] = part[ROWS:].astype(BF)
    copy.wait()
    two[2] = (two_cross + two_in[1].astype(F32)).astype(BF)
    two_copies.append(links.push(two.at[2], two_in.at[2], cross))
    copy = links.push(out.at[1], out_in.at[1], sib)
    out_cross = part[0:ROWS]
    part = out_part(0)
    out_mine = part[0:ROWS]
    out[0] = part[ROWS:].astype(BF)
    out_copies = [links.push(out.at[0], out_in.at[0], sib)]
    copy.wait()
    out[2] = (out_cross + out_in[1].astype(F32)).astype(BF)
    out_copies.append(links.push(out.at[2], out_in.at[2], cross))

    down_grad[...] = dot_tn(
        hidden_ref[...], jnp.concatenate([grads_of(0), grads_of(1)], axis=0)
    ).astype(BF)
    blank = jnp.zeros((16, 128), BF)
    product = down_grad[pl.ds(pl.multiple_of(64 * c, 64), UNITS), :]
    tile_stores(downs, product, 0, 0, down_place)
    for t in range(532, 544):
        downs[3, 3, t % 34] = blank
    for ring in rings:
        ring.start()
    staged[0, 0] = downs[turn(x, 1), 0:2, 0:17]
    staged[0, 1] = downs[turn(x, 3), 2:4, 0:17]
    staged[1, 0] = downs[0:2, turn(z, 1), 17:34]
    staged[1, 1] = downs[2:4, turn(z, 3), 17:34]
    block = blocks[...].reshape(4 * ROWS, WIDTH)
    for n in range(0, 2 * WINDOW, 512):
        product = dot_tn(block, back_gate[:, n : n + 512]).astype(BF)
        tile_stores(grads_ref, product, 0, n // 128, gate_place)
        if n == 1536:
            for ring in rings:
                ring.merge()
    for n in range(4):
        for t in range(280, 288):
            grads_ref[3, 3, 18 * n + t % 18] = blank

    for copy in two_copies:
        copy.wait()
    grad_two = two_mine + two_in[0].astype(F32) + two_in[2].astype(F32)
    middle = grad_middle_ref[...]
    scale = lax.rsqrt(jnp.mean(middle * middle, axis=-1, keepdims=True) + EPSILON)
    weighted = grad_two * gain
    grad_middle = (
        cot_all[f].astype(F32)
        + scale * weighted
        - middle * (scale * scale * scale) * jnp.mean(weighted * middle, axis=-1, keepdims=True)
    )
    gain_ref[...] = jnp.broadcast_to(
        jnp.sum(grad_two * middle * scale, axis=0, keepdims=True), (8, WIDTH)
    )
    grad_attn = grad_middle.astype(BF)
    grad_attn_ref[...] = grad_attn
    grad_middle_ref[...] = grad_middle
    grad_attended = dot_nt(grad_attn, wo_all[...].reshape(WIDTH, WIDTH)).astype(BF).astype(F32)
    low = lanes_below((ROWS, 128), 64)
    for tile in range(H // 2):
        part = grad_attended[:, tile * 128 : tile * 128 + 128]
        for half in range(2):
            head = tile * 2 + half
            j = head % GROUP
            mine = swap64(part) if half == 0 else part
            do_ref[head // GROUP, j * ROWS : (j + 1) * ROWS] = jnp.where(low, 0.0, mine).astype(BF)
    for g in range(KVH):
        do_ref[g, GROUP * ROWS :] = jnp.zeros((LANES - GROUP * ROWS, 128), BF)
    for copy in out_copies:
        copy.wait()
    total = out_mine + out_in[0].astype(F32) + out_in[2].astype(F32)
    output_ref[...] = (middle + total).astype(BF)
    for ring in rings:
        ring.finish()
    for half in range(2):
        two_of = slice(2 * half, 2 * half + 2)
        sum_a_ref[two_of] = (downs[x, two_of, 0:17].astype(F32) + rings[0].arrived(half)).astype(BF)
        sum_b_ref[two_of] = (downs[two_of, z, 17:34].astype(F32) + rings[1].arrived(half)).astype(BF)


def middle_call(*operands):
    shape = jax.ShapeDtypeStruct
    return pl.pallas_call(
        middle_kernel,
        out_shape=[
            shape((ROWS, WIDTH), BF),
            shape((ROWS, WIDTH), F32),
            shape((ROWS, WIDTH), BF),
            shape((8, WIDTH), F32),
            shape((KVH, LANES, 128), BF),
            shape((4, 4, 72, 16, 128), BF),
            shape((4, 17, 16, 128), BF),
            shape((4, 17, 16, 128), BF),
        ],
        in_specs=[VMEM] * 5 + [ANY] * 3,
        out_specs=[VMEM] * 8,
        scratch_shapes=[
            pltpu.VMEM((4, SHARD, WINDOW), BF),
            pltpu.VMEM((4, SHARD, WINDOW), BF),
            pltpu.VMEM((WINDOW, WIDTH), BF),
            pltpu.VMEM((4, ROWS, WIDTH), BF),
            pltpu.VMEM((4 * ROWS, 2 * WINDOW), BF),
            pltpu.VMEM((4 * ROWS, WINDOW), BF),
            pltpu.VMEM((WINDOW, WIDTH), BF),
            pltpu.VMEM((3, ROWS, WIDTH), BF),
            pltpu.VMEM((3, ROWS, WIDTH), BF),
            pltpu.VMEM((3, ROWS, WIDTH), BF),
            pltpu.VMEM((3, ROWS, WIDTH), BF),
            pltpu.VMEM((4, 4, 34, 16, 128), BF),
            pltpu.VMEM((2, 2, 2, 17, 16, 128), BF),
            pltpu.VMEM((2, 2, 2, 2, 17, 16, 128), BF),
            pltpu.VMEM((2, 2, 2, 17, 16, 128), BF),
            pltpu.SemaphoreType.DMA((24,)),
            pltpu.SemaphoreType.DMA((24,)),
            pltpu.SemaphoreType.DMA((3,)),
        ],
        compiler_params=pltpu.CompilerParams(
            vmem_limit_bytes=60 * MIB, collective_id=3, has_side_effects=True
        ),
        name="middle",
    )(*operands)


UNIT = 106
HALF = 53
UPPER = 36
CHUNK = 768


def widen(ref, index):
    return ref[index].astype(F32)


def back_kernel(
    q_ref,
    do_ref,
    ot_ref,
    lse_ref,
    kv_ref,
    extra_ref,
    kpos_ref,
    qpos_ref,
    down_a_ref,
    down_b_ref,
    grads_ref,
    dkv_ref,
    dq_ref,
    sum_ref,
    qx,
    dox,
    own,
    own_grad,
    parts,
    parts_in,
    pairs,
    pairs_in,
    single,
    single_in,
    side_a,
    side_b,
    relay,
    landing,
    staged,
    late_a,
    late_b,
    whole,
    whole_in,
    send,
    recv,
    local,
):
    yl, x, z, yh, c = place()
    f = yh * 2 + c
    mate = at(1 - yl, x, z, yh, c)
    on_x = [at(yl, turn(x, d), z, yh, c) for d in (1, 2, 3)]
    on_z = [at(yl, x, turn(z, d), yh, c) for d in (1, 2, 3)]
    links = Links(send, recv)
    greet([mate] + on_x + on_z)

    rings = (
        RingSum(
            links,
            x,
            on_x,
            lambda n, half: grads_ref.at[n, 2 * half : 2 * half + 2, 0:UPPER],
            relay.at[0],
            landing.at[0],
            staged.at[0],
        ),
        RingSum(
            links,
            z,
            on_z,
            lambda n, half: grads_ref.at[2 * half : 2 * half + 2, n, UPPER : 2 * UPPER],
            relay.at[1],
            landing.at[1],
            staged.at[1],
        ),
    )
    for ring in rings:
        ring.start()

    def keep():
        moves = (
            (grads_ref.at[turn(x, 1), 0:2, 0:UPPER], staged.at[0, 0]),
            (grads_ref.at[turn(x, 3), 2:4, 0:UPPER], staged.at[0, 1]),
            (grads_ref.at[0:2, turn(z, 1), UPPER : 2 * UPPER], staged.at[1, 0]),
            (grads_ref.at[2:4, turn(z, 3), UPPER : 2 * UPPER], staged.at[1, 1]),
            (grads_ref.at[x, :, 0:UPPER], side_a.at[:, 0:UPPER]),
            (grads_ref.at[:, z, UPPER : 2 * UPPER], side_b.at[:, 0:UPPER]),
        )
        return [pltpu.make_async_copy(*move, local.at[n]) for n, move in enumerate(moves)]

    for copy in keep():
        copy.start()
    side_a[:, UPPER:HALF] = down_a_ref[...]
    side_b[:, UPPER:HALF] = down_b_ref[...]

    row = lax.broadcasted_iota(jnp.int32, (128, LANES), 0)
    for g in range(KVH):
        lse = thirds(lse_ref[g, 0:1])
        inner = jnp.sum(do_ref[g].astype(F32).T[64:128] * ot_ref[g], axis=0, keepdims=True)
        inner = thirds(inner)
        extra_q = jnp.zeros((128, LANES), F32)
        extra_d = jnp.zeros((128, LANES), F32)
        for n in range(3):
            extra_q = jnp.where(row == 2 + n, -lse[n], extra_q)
            extra_d = jnp.where(row == 2 + n, -inner[n], extra_d)
        qx[g, :, 0:128] = q_ref[g, :, 0:128]
        qx[g, :, 128:256] = (q_ref[g, :, 128:256].astype(F32) + extra_q.T).astype(BF)
        dox[g, :, 0:128] = do_ref[g]
        dox[g, :, 128:256] = extra_d.T.astype(BF)

    def piece(g, keys, mask):
        scores = dot_nt(keys, qx[g])
        if mask is not None:
            scores = scores + mask
        probs = jnp.exp(scores)
        grad = (probs * dot_nt(keys, dox[g])).astype(BF)
        both = dot(grad, qx[g, :, 0:128]) + dot(probs.astype(BF), dox[g, :, 0:128])
        return both, dot(keys[:, 0:128].T[0:64], grad)

    mask = jnp.where(kpos_ref[:, 0:1] <= qpos_ref[0:1], 0.0, MASKED)
    spots = (
        pl.ds(pl.multiple_of((z * 2 + yl) * ROWS, ROWS), ROWS),
        pl.ds(pl.multiple_of((x * 2 + yl) * ROWS, ROWS), ROWS),
    )
    slab_of = (x, z)
    for g in range(KVH):
        own[...] = jnp.zeros(own.shape, BF)
        own[0:ROWS] = kv_ref[g, slab_of[g], spots[g], :]
        both, dq = piece(g, jnp.concatenate([own[...], own_extra()], axis=1), mask)
        own_grad[g] = both[0:ROWS]
        dq_ref[g] = dq
    count = SLAB // CHUNK
    base = links.reserve(6)

    def part_copy(g, d, slab):
        device = (
            ((yl * 4 + jnp.where(g == 0, slab, x)) * 4 + jnp.where(g == 0, z, slab)),
            f,
        )
        n = g * 3 + d - 1
        return links.copy(parts.at[g, slab], parts_in.at[g, d - 1], device, base + n)

    def step(i, _):
        n, part = lax.div(i, count), lax.rem(i, count)
        g = lax.rem(n, 2)
        d = lax.rem(lax.div(n, 2) + 1, 4)
        slab = turn(jnp.where(g == 0, x, z), d)
        start = pl.multiple_of(part * CHUNK, CHUNK)
        rows = extra_ref[g, pl.ds(pl.multiple_of(slab * 16 + part * 8, 8), 8), :]
        keys = jnp.concatenate([kv_ref[g, slab, pl.ds(start, CHUNK), :], key_extra(rows)], axis=1)
        both, dq = piece(g, keys, None)
        parts[g, slab, pl.ds(start, CHUNK), :] = both.astype(BF)
        dq_ref[g] += dq

        @pl.when((part == count - 1) & (d > 0))
        def _():
            part_copy(g, d, slab).start()

        for at_step, event in events:
            pl.when(i == at_step)(event)
        return 0

    pair_base, single_base, second_base, third_slot = (
        links.reserve(6),
        links.reserve(2),
        links.reserve(6),
        links.reserve(1),
    )

    def pair_copies(g):
        other, devices = (z, x)[g], (on_z, on_x)[g]
        return [
            links.copy(
                pairs.at[g, turn(other, n + 1)],
                pairs_in.at[g, n],
                devices[n],
                pair_base + 3 * g + n,
            )
            for n in range(3)
        ]

    def pair_start(g):
        slab = slab_of[g]
        for d in (1, 2, 3):
            part_copy(g, d, turn(slab, d)).wait()
        for n in range(4):
            rows = slice(n * 2 * ROWS, (n + 1) * 2 * ROWS)
            total = parts[g, slab, rows, :].astype(F32)
            for m in range(3):
                total = total + parts_in[g, m, rows, :].astype(F32)
            pairs[g, n] = total.astype(BF)
        for copy in pair_copies(g):
            copy.start()

    def single_copy(g):
        return links.copy(single_in.at[g, 0], single_in.at[g, 1], mate, single_base + g)

    def single_start(g):
        for copy in pair_copies(g):
            copy.wait()
        total = pairs[g, (z, x)[g]].astype(F32)
        for m in range(3):
            total = total + pairs_in[g, m].astype(F32)
        single[g, 0] = total[0:ROWS]
        single[g, 1] = total[ROWS:]
        single_in[g, 0] = jnp.where(yl == 0, total[ROWS:], total[0:ROWS]).astype(BF)
        single_copy(g).start()

    def single_end(g):
        single_copy(g).wait()
        dkv_ref[g] = single[g, yl] + single_in[g, 1].astype(F32) + own_grad[g]

    def merge():
        for copy in keep():
            copy.wait()
        for ring in rings:
            ring.merge()

    def second_copies():
        copies = []
        for n in range(3):
            for source, target, index, device in (
                (side_a, late_a, turn(z, n + 1), on_z[n]),
                (side_b, late_b, turn(x, n + 1), on_x[n]),
            ):
                copies.append(
                    links.copy(source.at[index], target.at[n], device, second_base + len(copies))
                )
        return copies

    def second_start():
        for side, ring in zip((side_a, side_b), rings):
            ring.finish()
            for half in range(2):
                rows = slice(2 * half, 2 * half + 2)
                total = side[rows, 0:UPPER].astype(F32) + ring.arrived(half)
                side[rows, 0:UPPER] = total.astype(BF)
        for copy in second_copies():
            copy.start()

    def third():
        return links.copy(whole, whole_in, mate, third_slot)

    def third_start():
        for copy in second_copies():
            copy.wait()
        a = side_a[z].astype(F32)
        b = side_b[x].astype(F32)
        for m in range(3):
            a = a + late_a[m].astype(F32)
            b = b + late_b[m].astype(F32)
        whole[0:HALF] = a.astype(BF)
        whole[HALF:UNIT] = b.astype(BF)
        third().start()

    events = (
        (3, merge),
        (9, second_start),
        (13, lambda: pair_start(0)),
        (14, third_start),
    )
    lax.fori_loop(0, KVH * SLABS * count, step, 0)
    pair_start(1)
    single_start(0)
    single_end(0)
    single_start(1)
    single_end(1)
    third().wait()
    sum_ref[...] = (whole[...].astype(F32) + whole_in[...].astype(F32)).astype(BF)


def back(q, do, ot, lse, kv, extra, kpos, qpos, down_a, down_b, grads):
    shape = jax.ShapeDtypeStruct
    return pl.pallas_call(
        back_kernel,
        out_shape=[
            shape((KVH, ROWS, 128), F32),
            shape((KVH, HD, LANES), F32),
            shape((UNIT, 16, 128), BF),
        ],
        in_specs=[VMEM] * 10 + [ANY],
        out_specs=[VMEM] * 3,
        scratch_shapes=[
            pltpu.VMEM((KVH, LANES, 256), BF),
            pltpu.VMEM((KVH, LANES, 256), BF),
            pltpu.VMEM((OWN, 128), BF),
            pltpu.VMEM((KVH, ROWS, 128), F32),
            pltpu.VMEM((KVH, SLABS, SLAB, 128), BF),
            pltpu.VMEM((KVH, 3, SLAB, 128), BF),
            pltpu.VMEM((KVH, 4, 2 * ROWS, 128), BF),
            pltpu.VMEM((KVH, 3, 2 * ROWS, 128), BF),
            pltpu.VMEM((KVH, 2, ROWS, 128), F32),
            pltpu.VMEM((KVH, 2, ROWS, 128), BF),
            pltpu.VMEM((4, HALF, 16, 128), BF),
            pltpu.VMEM((4, HALF, 16, 128), BF),
            pltpu.VMEM((2, 2, 2, UPPER, 16, 128), BF),
            pltpu.VMEM((2, 2, 2, 2, UPPER, 16, 128), BF),
            pltpu.VMEM((2, 2, 2, UPPER, 16, 128), BF),
            pltpu.VMEM((3, HALF, 16, 128), BF),
            pltpu.VMEM((3, HALF, 16, 128), BF),
            pltpu.VMEM((UNIT, 16, 128), BF),
            pltpu.VMEM((UNIT, 16, 128), BF),
            pltpu.SemaphoreType.DMA((48,)),
            pltpu.SemaphoreType.DMA((48,)),
            pltpu.SemaphoreType.DMA((6,)),
        ],
        compiler_params=pltpu.CompilerParams(
            vmem_limit_bytes=62 * MIB, collective_id=1, has_side_effects=True
        ),
        name="back",
    )(q, do, ot, lse, kv, extra, kpos, qpos, down_a, down_b, grads)


def last_kernel(
    sum_ref,
    dq_ref,
    dkv_ref,
    cos_ref,
    sin_ref,
    normed_ref,
    attended_ref,
    grad_attn_ref,
    grad_middle_ref,
    tokens_ref,
    wq_all,
    wk_all,
    wv_all,
    small_all,
    hidden_gain_ref,
    token_grad_ref,
    late_ref,
    thin_ref,
    whole_ref,
    natural,
    table,
    table_in,
    lines,
    lines_in,
    cols,
    cols_in,
    ends,
    ends_in,
    thin,
    send,
    recv,
    local,
):
    yl, x, z, yh, c = place()
    f = yh * 2 + c
    f_cross = (1 - yh) * 2 + c
    f_sib = yh * 2 + 1 - c
    f_far = (1 - yh) * 2 + 1 - c
    sib = at(yl, x, z, yh, 1 - c)
    cross = at(1 - yl, x, z, 1 - yh, c)
    far = at(1 - yl, x, z, 1 - yh, 1 - c)
    mate = at(1 - yl, x, z, yh, c)
    on_x = [at(yl, turn(x, d), z, yh, c) for d in (1, 2, 3)]
    on_z = [at(yl, x, turn(z, d), yh, c) for d in (1, 2, 3)]
    links = Links(send, recv)
    greet([sib, cross, far, mate] + on_x + on_z)

    shared = []

    def spot(index):
        return pl.ds(18 * index + 17 * lax.div(index, 2), 18)

    for device, index in ((sib, f_sib), (cross, f_cross), (far, f_far)):
        shared.append(
            links.push(sum_ref.at[spot(index)], whole_ref.at[x, z, spot(f)], device)
        )
    keep = [
        pltpu.make_async_copy(sum_ref.at[part], whole_ref.at[x, z, part], local.at[n])
        for n, part in enumerate((spot(f), slice(UPPER, HALF), slice(HALF + UPPER, UNIT)))
    ]
    for copy in keep:
        copy.start()

    def assemble(tile):
        even, odd = tile * 2, tile * 2 + 1
        left = natural[even // GROUP, (even % GROUP) * ROWS : (even % GROUP + 1) * ROWS]
        right = natural[odd // GROUP, (odd % GROUP) * ROWS : (odd % GROUP + 1) * ROWS]
        return jnp.where(low, left, swap64(right))

    low = lanes_below((ROWS, 128), 64)
    cosine, sine = cos_ref[...], -sin_ref[...]
    for g in range(KVH):
        natural[g] = jnp.concatenate([dq_ref[g], jnp.zeros((64, LANES), F32)], axis=0).T
    grad_queries = jnp.concatenate(
        [
            turn_pairs(assemble(tile) * (1.0 / math.sqrt(HD)), cosine, sine)
            for tile in range(H // 2)
        ],
        axis=1,
    ).astype(BF)
    grad_keys = turn_pairs(jnp.where(low, dkv_ref[0], swap64(dkv_ref[1])), cosine, sine).astype(BF)
    grad_values = jnp.where(low, swap64(dkv_ref[0]), dkv_ref[1]).astype(BF)

    for copy in keep + shared:
        copy.wait()
    spread = []
    for n in range(3):
        spread.append(
            links.push(whole_ref.at[x, z, 0:HALF], whole_ref.at[x, z, 0:HALF], on_z[n])
        )
        spread.append(
            links.push(whole_ref.at[x, z, HALF:UNIT], whole_ref.at[x, z, HALF:UNIT], on_x[n])
        )

    normed, attended = normed_ref[...], attended_ref[...]
    column = 0
    for left, right in (
        (normed, grad_queries),
        (normed, grad_keys),
        (normed, grad_values),
        (attended, grad_attn_ref[...]),
    ):
        product = dot_tn(left, right).astype(BF)
        for n in range(right.shape[1] // 128):
            table[column] = product[:, n * 128 : n * 128 + 128].reshape(4, SHARD, 128)
            column += 1
    beside = [
        links.push(table.at[:, 2 * n + 1 - c], table_in.at[n], sib) for n in range(2)
    ]

    inputs = tokens_ref[...].astype(F32)
    scale = lax.rsqrt(jnp.mean(inputs * inputs, axis=-1, keepdims=True) + EPSILON)

    def vector(row, count):
        return jnp.concatenate([small_all[n, row : row + 1, 0:count] for n in range(4)], axis=1)

    grad_normed = (
        dot_nt(grad_queries, wq_all[...].reshape(WIDTH, WIDTH))
        + dot_nt(grad_keys, wk_all[...].reshape(WIDTH, 128))
        + dot_nt(grad_values, wv_all[...].reshape(WIDTH, 128))
    )
    weighted = grad_normed * vector(1, SHARD)
    token_grad_ref[...] = (
        grad_middle_ref[...]
        + scale * weighted
        - inputs * (scale * scale * scale) * jnp.mean(weighted * inputs, axis=-1, keepdims=True)
    )
    thin[0, c] = jnp.concatenate(
        [
            jnp.sum(grad_queries.astype(F32), axis=0, keepdims=True),
            jnp.sum(grad_normed * inputs * scale, axis=0, keepdims=True),
            hidden_gain_ref[0:1],
            jnp.concatenate(
                [
                    jnp.sum(grad_keys.astype(F32), axis=0, keepdims=True),
                    jnp.sum(grad_values.astype(F32), axis=0, keepdims=True),
                    jnp.zeros((1, WIDTH - 256), F32),
                ],
                axis=1,
            ),
            jnp.zeros((4, WIDTH), F32),
        ],
        axis=0,
    )

    def thin_push(level, index, device):
        return links.push(thin.at[level, index], thin.at[level, index], device)

    thin_copies = [thin_push(0, c, sib)]

    for copy in spread:
        copy.wait()
    rounds = []
    for n in (0, 2):
        rounds.append(
            links.push(whole_ref.at[x, :, 0:HALF], whole_ref.at[x, :, 0:HALF], on_x[n])
        )
        rounds.append(
            links.push(whole_ref.at[:, z, HALF:UNIT], whole_ref.at[:, z, HALF:UNIT], on_z[n])
        )
    for copy in beside + thin_copies:
        copy.wait()

    def add_beside(n, _):
        for m in range(2):
            total = table[n, 2 * m + c].astype(F32) + table_in[m, n].astype(F32)
            lines[m, n] = total.astype(BF)
        return 0

    lax.fori_loop(0, 16, add_beside, 0)
    thin[1, x] = thin[0, 0] + thin[0, 1]
    along = []
    for n in range(3):
        xt, zt = turn(x, n + 1), turn(z, n + 1)
        along.append(links.push(lines.at[0, pl.ds(xt * 4, 4)], lines_in.at[0, n], on_x[n]))
        for m in range(4):
            along.append(
                links.push(lines.at[1, m * 4 + zt], lines_in.at[1, n, m], on_z[n])
            )
        along.append(thin_push(1, x, on_x[n]))
    for copy in along:
        copy.wait()
    for m in range(4):
        a = lines[0, x * 4 + m].astype(F32)
        b = lines[1, m * 4 + z].astype(F32)
        for n in range(3):
            a = a + lines_in[0, n, m].astype(F32)
            b = b + lines_in[1, n, m].astype(F32)
        cols[0, m] = a.astype(BF)
        cols[1, m] = b.astype(BF)
    thin[2, z] = (thin[1, 0] + thin[1, 1]) + (thin[1, 2] + thin[1, 3])
    along = []
    for n in range(3):
        along.append(links.push(cols.at[0, turn(z, n + 1)], cols_in.at[0, n], on_z[n]))
        along.append(links.push(cols.at[1, turn(x, n + 1)], cols_in.at[1, n], on_x[n]))
        along.append(thin_push(2, z, on_z[n]))
    for copy in along:
        copy.wait()
    a = cols[0, z].astype(F32)
    b = cols[1, x].astype(F32)
    for n in range(3):
        a = a + cols_in[0, n].astype(F32)
        b = b + cols_in[1, n].astype(F32)
    ends[0] = a.astype(BF)
    ends[1] = b.astype(BF)
    thin[3, yh] = (thin[2, 0] + thin[2, 1]) + (thin[2, 2] + thin[2, 3])
    along = [links.push(ends.at[1 - yh], ends_in.at[0], cross), thin_push(3, yh, cross)]
    for copy in along:
        copy.wait()
    ends[2] = (ends[yh].astype(F32) + ends_in[0].astype(F32)).astype(BF)
    thin[4, yl] = thin[3, 0] + thin[3, 1]
    along = [links.push(ends.at[2], ends_in.at[1], mate), thin_push(4, yl, mate)]
    for copy in along:
        copy.wait()
    late_ref[x, z] = (ends[2].astype(F32) + ends_in[1].astype(F32)).astype(BF)
    thin_ref[...] = thin[4, 0] + thin[4, 1]

    cut = SHARD // 2
    along = []
    for n in range(3):
        along.append(links.push(late_ref.at[x, z, 0:cut], late_ref.at[x, z, 0:cut], on_z[n]))
        along.append(links.push(late_ref.at[x, z, cut:], late_ref.at[x, z, cut:], on_x[n]))
    for copy in rounds:
        copy.wait()
    rounds = []
    for half, came, n in ((0, 3, 0), (1, 1, 2)):
        rows = slice(2 * half, 2 * half + 2)
        a = whole_ref.at[turn(x, came), rows, 0:HALF]
        b = whole_ref.at[rows, turn(z, came), HALF:UNIT]
        rounds += [links.push(a, a, on_x[n]), links.push(b, b, on_z[n])]
    for copy in along:
        copy.wait()
    along = []
    for n in range(3):
        along.append(links.push(late_ref.at[x, :, 0:cut], late_ref.at[x, :, 0:cut], on_x[n]))
        along.append(links.push(late_ref.at[:, z, cut:], late_ref.at[:, z, cut:], on_z[n]))
    for copy in along + rounds:
        copy.wait()


def last_call(*operands):
    shape = jax.ShapeDtypeStruct
    return pl.pallas_call(
        last_kernel,
        out_shape=[
            shape((ROWS, WIDTH), F32),
            shape((4, 4, SHARD, 128), BF),
            shape((8, WIDTH), F32),
            shape((4, 4, UNIT, 16, 128), BF),
        ],
        in_specs=[VMEM] * 15,
        out_specs=[VMEM] * 3 + [ANY],
        scratch_shapes=[
            pltpu.VMEM((KVH, LANES, 128), F32),
            pltpu.VMEM((16, 4, SHARD, 128), BF),
            pltpu.VMEM((2, 16, SHARD, 128), BF),
            pltpu.VMEM((2, 16, SHARD, 128), BF),
            pltpu.VMEM((2, 3, 4, SHARD, 128), BF),
            pltpu.VMEM((2, 4, SHARD, 128), BF),
            pltpu.VMEM((2, 3, SHARD, 128), BF),
            pltpu.VMEM((3, SHARD, 128), BF),
            pltpu.VMEM((2, SHARD, 128), BF),
            pltpu.VMEM((5, 4, 8, WIDTH), F32),
            pltpu.SemaphoreType.DMA((72,)),
            pltpu.SemaphoreType.DMA((72,)),
            pltpu.SemaphoreType.DMA((3,)),
        ],
        compiler_params=pltpu.CompilerParams(
            vmem_limit_bytes=58 * MIB, collective_id=2, has_side_effects=True
        ),
        name="last",
    )(*operands)


def finish_kernel(
    late_ref,
    thin_ref,
    whole_ref,
    q_out,
    k_out,
    v_out,
    o_out,
    gate_out,
    up_out,
    down_out,
    qb_out,
    kb_out,
    vb_out,
    ag_out,
    hg_out,
    q_val,
    k_val,
    v_val,
    o_val,
    gate_val,
    up_val,
    down_val,
    sems,
):
    copies = []

    def leave(value, out):
        copy = pltpu.make_async_copy(value, out, sems.at[len(copies)])
        copy.start()
        copies.append(copy)

    def gate_tile(n, r, lane):
        t = r * 20 + lane
        p, k = t // 18, 18 * n + 17 * (n // 2) + t % 18
        return whole_ref[p // 4, p % 4, k].astype(F32)

    for value, out, first in ((gate_val, gate_out, 0), (up_val, up_out, 10)):
        for r in range(14):
            for tile in range(38):
                parts = []
                for n in range(4):
                    lane = tile - (19 * n) // 2
                    if 0 <= lane < 10:
                        parts.append(gate_tile(n, r, first + lane))
                total = parts[0] if len(parts) == 1 else parts[0] + parts[1]
                value[r * 16 : r * 16 + 16, tile * 128 : tile * 128 + 128] = total
        leave(value, out)
    for r in range(76):
        for tile in range(7):
            t = r * 7 + tile
            p, k = t // 34, t % 34
            k = UPPER + k if k < 17 else HALF + UPPER + k - 17
            down_val[r * 16 : r * 16 + 16, tile * 128 : tile * 128 + 128] = whole_ref[
                p // 4, p % 4, k
            ].astype(F32)
    leave(down_val, down_out)
    column = 0
    for value, out, count in ((q_val, q_out, 7), (k_val, k_out, 1), (v_val, v_out, 1), (o_val, o_out, 7)):
        for tile in range(count):
            value[:, tile * 128 : tile * 128 + 128] = late_ref[column // 4, column % 4].astype(F32)
            column += 1
        leave(value, out)
    f = lax.axis_index("fsdp")

    def share(row, start, part):
        total = thin_ref[row : row + 1, start : start + part]
        for n in range(1, 4):
            first = start + n * part
            total = jnp.where(f == n, thin_ref[row : row + 1, first : first + part], total)
        return total

    qb_out[...] = share(0, 0, SHARD)
    kb_out[...] = share(3, 0, 32)
    vb_out[...] = share(3, 128, 32)
    ag_out[...] = share(1, 0, SHARD)
    hg_out[...] = share(2, 0, SHARD)
    for copy in copies:
        copy.wait()


def finish(late, thin, whole):
    shape = jax.ShapeDtypeStruct
    large = [
        (SHARD, WIDTH),
        (SHARD, 128),
        (SHARD, 128),
        (SHARD, WIDTH),
        (SHARD, 4 * UNITS),
        (SHARD, 4 * UNITS),
        (UNITS, WIDTH),
    ]
    tiny = [(1, SHARD), (1, 32), (1, 32), (1, SHARD), (1, SHARD)]
    return pl.pallas_call(
        finish_kernel,
        out_shape=[shape(size, F32) for size in large + tiny],
        in_specs=[VMEM] * 3,
        out_specs=[ANY] * 7 + [VMEM] * 5,
        scratch_shapes=[pltpu.VMEM(size, F32) for size in large]
        + [pltpu.SemaphoreType.DMA((7,))],
        compiler_params=pltpu.CompilerParams(vmem_limit_bytes=58 * MIB),
        name="finish",
    )(late, thin, whole)


def tables(block_order, ctx):
    own_blocks = lax.dynamic_slice_in_dim(block_order, ctx * 2, 2)
    own_pos = (own_blocks[:, None] * BLK + jnp.arange(BLK, dtype=jnp.int32)[None, :]).reshape(ROWS)
    own_pos = own_pos.astype(F32)
    frequency = jnp.exp(jnp.arange(HD // 2, dtype=F32) * (-2.0 * math.log(THETA) / HD))
    angles = own_pos[:, None] * frequency[None, :]
    cosine, sine = jnp.cos(angles), jnp.sin(angles)
    cosine = jnp.concatenate([cosine] * 4, axis=1)
    sine = jnp.concatenate([-sine, sine] * 2, axis=1)
    slots = jnp.arange(64, dtype=jnp.int32)
    shown = (block_order[:, None] < own_blocks[None, :]) & (slots // 2 != ctx)[:, None]
    lane = jnp.arange(128)[None, :]
    bias = jnp.where(shown, 0.0, MASKED)
    extra = jnp.where(lane == 0, bias[:, 0:1], jnp.where(lane == 1, bias[:, 1:2], 0.0))
    extra = jnp.where((lane >= 2) & (lane < 5), 1.0, extra).astype(F32).reshape(2, 4, 4, 2, 128)
    extra = jnp.stack(
        [
            extra.transpose(1, 2, 0, 3, 4).reshape(64, 128),
            extra.transpose(2, 1, 0, 3, 4).reshape(64, 128),
        ]
    )
    kpos = jnp.pad(own_pos, (0, OWN - ROWS), constant_values=1e9)
    kpos = jnp.broadcast_to(kpos[:, None], (OWN, 128))
    qpos = jnp.pad(jnp.tile(own_pos, GROUP), (0, LANES - GROUP * ROWS), constant_values=5e8)
    qpos = jnp.broadcast_to(qpos[None, :], (8, LANES))
    return cosine, sine, extra, kpos, qpos


def body(
    tokens,
    block_order,
    query_weight,
    key_weight,
    value_weight,
    output_weight,
    gate_weight,
    up_weight,
    down_weight,
    query_bias,
    key_bias,
    value_bias,
    attention_gain,
    hidden_gain,
    cotangent,
):
    ctx = lax.axis_index("ctx")
    cosine, sine, extra, kpos, qpos = tables(block_order, ctx)

    def line(vector):
        return jnp.pad(vector.astype(F32), (0, 256 - vector.shape[0]))

    small = jnp.stack(
        [line(v) for v in (query_bias, attention_gain, hidden_gain, key_bias, value_bias)]
        + [jnp.zeros((256,), F32)] * 3
    )
    (
        attended,
        ot,
        lse,
        q,
        kv,
        normed,
        wq_all,
        wk_all,
        wv_all,
        small_all,
        wo_all,
        gate_all,
        up_all,
        cot_all,
    ) = front(
        tokens[0],
        query_weight,
        key_weight,
        value_weight,
        small,
        cosine,
        sine,
        extra,
        kpos,
        qpos,
        output_weight,
        gate_weight,
        up_weight,
        cotangent[0],
    )
    (
        output,
        grad_middle,
        grad_attn,
        hidden_gain_part,
        grad_attended,
        grads,
        down_a,
        down_b,
    ) = middle_call(
        attended, tokens[0], small_all, wo_all, cot_all, gate_all, up_all, down_weight
    )
    dkv, dq, total = back(
        q, grad_attended, ot, lse, kv, extra, kpos, qpos, down_a, down_b, grads
    )
    token_grad, late, thin, whole = last_call(
        total,
        dq,
        dkv,
        cosine,
        sine,
        normed,
        attended,
        grad_attn,
        grad_middle,
        tokens[0],
        wq_all,
        wk_all,
        wv_all,
        small_all,
        hidden_gain_part,
    )
    ends = finish(late, thin, whole)
    return (output[None], token_grad[None], *ends[:7], *(end.reshape(-1) for end in ends[7:]))


def solution(mesh):
    rows = P("fsdp", "ctx", None)
    matrix = P("fsdp", None)
    vector = P("fsdp")
    placed = (rows, P()) + (matrix,) * 7 + (vector,) * 5 + (rows,)
    return jax.shard_map(
        body,
        mesh=mesh,
        in_specs=placed,
        out_specs=(rows, rows) + (matrix,) * 7 + (vector,) * 5,
        check_vma=False,
    )
```

```python
import math

import jax
import jax.numpy as jnp
import numpy as np
from jax import lax
from jax.experimental import pallas as pl
from jax.experimental.pallas import tpu as pltpu
from jax.sharding import PartitionSpec as P

H = 14
KVH = 2
GROUP = H // KVH
HD = 64
ROWS = 192
BLK = 96
LANES = 1408
SLAB = 1536
SLABS = 4
OWN = 256

EPSILON = 1e-06
THETA = 1000000.0
MASKED = -1e30

BF = jnp.bfloat16
F32 = jnp.float32
VMEM = pl.BlockSpec(memory_space=pltpu.VMEM)
NT = (((1,), (1,)), ((), ()))
TN = (((0,), (0,)), ((), ()))


def dot(left, right):
    return jnp.dot(left, right, preferred_element_type=F32)


def dot_nt(left, right):
    return lax.dot_general(left, right, NT, preferred_element_type=F32)


def dot_tn(left, right):
    return lax.dot_general(left, right, TN, preferred_element_type=F32)


def thirds(value):
    high = value.astype(BF).astype(F32)
    rest = value - high
    middle = rest.astype(BF).astype(F32)
    low = (rest - middle).astype(BF).astype(F32)
    return high, middle, low


MESH = pl.DeviceIdType.MESH
ANY = pl.BlockSpec(memory_space=pl.ANY)
WINDOW = 1280
UNITS = 1216
SHARD = 224
WIDTH = 896
MIB = 2**20


def place():
    ctx, f = lax.axis_index("ctx"), lax.axis_index("fsdp")
    return lax.div(ctx, 16), lax.rem(lax.div(ctx, 4), 4), lax.rem(ctx, 4), lax.div(f, 2), lax.rem(f, 2)


def at(yl, x, z, yh, c):
    return ((yl * 4 + x) * 4 + z, yh * 2 + c)


def turn(index, by):
    return lax.rem(index + by, 4)


def greet(devices):
    barrier = pltpu.get_barrier_semaphore()
    for device in devices:
        pl.semaphore_signal(barrier, inc=1, device_id=device, device_id_type=MESH)
    pl.semaphore_wait(barrier, len(devices))


class Links:
    def __init__(self, send, recv):
        self.send, self.recv, self.used = send, recv, 0

    def reserve(self, count):
        first = self.used
        self.used += count
        return first

    def copy(self, src, dst, device, slot):
        return pltpu.make_async_remote_copy(
            src_ref=src,
            dst_ref=dst,
            send_sem=self.send.at[slot],
            recv_sem=self.recv.at[slot],
            device_id=device,
            device_id_type=MESH,
        )

    def push(self, src, dst, device):
        copy = self.copy(src, dst, device, self.reserve(1))
        copy.start()
        return copy


class RingSum:
    def __init__(self, links, me, devices, chunk, relay, landing, staged):
        self.links, self.me, self.devices, self.chunk = links, me, devices, chunk
        self.relay, self.landing, self.staged = relay, landing, staged
        self.base = links.reserve(6)

    def copies(self, wanted):
        me, right, left = self.me, self.devices[0], self.devices[2]
        across, after, before = turn(me, 2), turn(me, 1), turn(me, 3)
        chunk, landing, staged = self.chunk, self.landing, self.staged
        moves = (
            (chunk(across, 0), self.relay.at[0], right),
            (chunk(across, 1), self.relay.at[1], left),
            (chunk(after, 1), landing.at[0, 1], right),
            (chunk(before, 0), landing.at[1, 0], left),
            (staged.at[0], landing.at[0, 0], right),
            (staged.at[1], landing.at[1, 1], left),
        )
        return [self.links.copy(*moves[n], self.base + n) for n in wanted]

    def start(self):
        for copy in self.copies((0, 1, 2, 3)):
            copy.start()

    def merge(self):
        for n in range(2):
            came, on = self.copies((n, 4 + n))
            came.wait_recv()
            self.staged[n] = (self.staged[n].astype(F32) + self.relay[n].astype(F32)).astype(BF)
            on.start()

    def finish(self):
        for copy in self.copies((0, 1)):
            copy.wait_send()
        for copy in self.copies((2, 3, 4, 5)):
            copy.wait()

    def arrived(self, half):
        return self.landing[0, half].astype(F32) + self.landing[1, half].astype(F32)


def lanes_below(shape, bound):
    return lax.broadcasted_iota(jnp.int32, shape, 1) < bound


def swap64(value):
    return pltpu.roll(value, 64, axis=1)


def turn_pairs(value, cosine, sine):
    lane = lax.broadcasted_iota(jnp.int32, value.shape, 1)
    other = jnp.where(
        lax.rem(lane, 64) < 32, pltpu.roll(value, 96, axis=1), pltpu.roll(value, 32, axis=1)
    )
    return value * cosine + other * sine


def key_extra(rows):
    count = rows.shape[0]
    return jnp.broadcast_to(rows[:, None, :], (count, BLK, 128)).reshape(count * BLK, 128).astype(BF)


def own_extra():
    lane = lax.broadcasted_iota(jnp.int32, (OWN, 128), 1)
    return jnp.where((lane >= 2) & (lane < 5), 1.0, 0.0).astype(BF)


def window_start(f):
    return pl.multiple_of(lax.div(19 * f, 2) * 128, 128)


def tables(order_ref, token_angle, block_angle, cos_ref, sin_ref, extra_ref, kpos_ref, qpos_ref):
    ctx = lax.axis_index("ctx")
    mine = [order_ref[2 * ctx], order_ref[2 * ctx + 1]]
    lane = lax.broadcasted_iota(jnp.int32, (BLK, 128), 1)
    sign = jnp.where(lax.rem(lane, 64) < 32, -1.0, 1.0)
    for n in range(2):
        rows = slice(n * BLK, (n + 1) * BLK)
        cosine, sine = block_angle[0, pl.ds(mine[n], 1), :], block_angle[1, pl.ds(mine[n], 1), :]
        cos_ref[rows] = token_angle[0] * cosine - token_angle[1] * sine
        sin_ref[rows] = (token_angle[1] * cosine + token_angle[0] * sine) * sign
    lane = lax.broadcasted_iota(jnp.int32, (1, 128), 1)
    ones = jnp.where((lane >= 2) & (lane < 5), 1.0, 0.0)
    for slot in range(64):
        block = order_ref[slot]
        other = slot // 2 != ctx
        row = ones
        for n in range(2):
            shown = jnp.where((block < mine[n]) & other, 0.0, MASKED)
            row = jnp.where(lane == n, shown, row)
        yl, x, z, n = slot // 32, slot // 8 % 4, slot // 2 % 4, slot % 2
        for g, spot in enumerate((((x * 4 + z) * 2 + yl) * 2 + n, ((z * 4 + x) * 2 + yl) * 2 + n)):
            extra_ref[g, spot : spot + 1, :] = row

    def position(index):
        block = jnp.where(index < BLK, mine[0], mine[1])
        return (block * BLK + lax.rem(index, BLK)).astype(F32)

    row = lax.broadcasted_iota(jnp.int32, (OWN, 128), 0)
    kpos_ref[...] = jnp.where(row < ROWS, position(row), 1e9)
    lane = lax.broadcasted_iota(jnp.int32, (8, LANES), 1)
    qpos_ref[...] = jnp.where(lane < GROUP * ROWS, position(lax.rem(lane, ROWS)), 5e8)


def angle_tables():
    lane = np.arange(128) % 32
    frequency = np.exp(lane * (-2.0 * math.log(THETA) / HD))
    token = np.arange(BLK)[:, None] * frequency
    block = np.arange(64)[:, None] * BLK * frequency
    return [np.stack([np.cos(a), np.sin(a)]).astype(np.float32) for a in (token, block)]


def front_kernel(
    tokens_ref,
    wq_ref,
    wk_ref,
    wv_ref,
    qb_ref,
    ag_ref,
    hg_ref,
    kb_ref,
    vb_ref,
    order_ref,
    token_angle_ref,
    block_angle_ref,
    wo_ref,
    gate_ref,
    up_ref,
    cot_ref,
    attended_ref,
    ot_ref,
    lse_ref,
    q_ref,
    kv_ref,
    normed_ref,
    wq_all,
    wk_all,
    wv_all,
    small_all,
    cos_ref,
    sin_ref,
    extra_ref,
    kpos_ref,
    qpos_ref,
    wo_all,
    gate_all,
    up_all,
    cot_all,
    own,
    acc,
    top,
    natural,
    send,
    recv,
    local,
):
    yl, x, z, yh, c = place()
    f = yh * 2 + c
    f_cross = (1 - yh) * 2 + c
    f_sib = yh * 2 + 1 - c
    f_far = (1 - yh) * 2 + 1 - c
    sib = at(yl, x, z, yh, 1 - c)
    cross = at(1 - yl, x, z, 1 - yh, c)
    far = at(1 - yl, x, z, 1 - yh, 1 - c)
    mate = at(1 - yl, x, z, yh, c)
    on_x = [at(yl, turn(x, d), z, yh, c) for d in (1, 2, 3)]
    on_z = [at(yl, x, turn(z, d), yh, c) for d in (1, 2, 3)]
    links = Links(send, recv)
    greet([sib, cross, far, mate] + on_x + on_z)

    def gather_start(pairs):
        return [
            (links.push(mine, whole.at[f], sib), links.push(mine, whole.at[f], cross), whole)
            for mine, whole in pairs
        ]

    def gather_relay(started):
        relays = []
        for _, over, whole in started:
            over.wait_recv()
            relays.append(links.push(whole.at[f_cross], whole.at[f_cross], sib))
        return relays

    def gather_end(started, relays):
        for beside, over, _ in started:
            beside.wait()
            over.wait_send()
        for relay in relays:
            relay.wait()

    first = gather_start([(wq_ref, wq_all), (wk_ref, wk_all), (wv_ref, wv_all)])
    small_all[f] = jnp.zeros((8, 256), F32)
    for row, (ref, count) in enumerate(
        ((qb_ref, SHARD), (ag_ref, SHARD), (hg_ref, SHARD), (kb_ref, 32), (vb_ref, 32))
    ):
        small_all[f, row : row + 1, 0:count] = ref[...].astype(F32)
    first += gather_start([(small_all.at[f], small_all)])
    keep = [
        pltpu.make_async_copy(mine, whole.at[f], local.at[n])
        for n, (mine, whole) in enumerate(((wo_ref, wo_all), (cot_ref, cot_all)))
    ]
    for copy in keep:
        copy.start()
    tables(
        order_ref, token_angle_ref, block_angle_ref, cos_ref, sin_ref, extra_ref, kpos_ref, qpos_ref
    )
    wq_all[f] = wq_ref[...]
    wk_all[f] = wk_ref[...]
    wv_all[f] = wv_ref[...]
    inputs = tokens_ref[...].astype(F32)
    scale = lax.rsqrt(jnp.mean(inputs * inputs, axis=-1, keepdims=True) + EPSILON)
    relays = gather_relay(first)
    def quarter(n, start):
        rows = pl.ds(pl.multiple_of(lax.div(n, 2) * 112, 16), 112)
        return rows, pl.ds(pl.multiple_of(start + lax.rem(n, 2) * 640, 128), 640)

    spread = []
    for ref, whole, n in ((gate_ref, gate_all, x), (up_ref, up_all, z)):
        rows, lanes = quarter(n, 0)
        for device, index in ((cross, f_cross), (far, f_far)):
            part = ref.at[quarter(n, window_start(index))]
            spread.append(links.push(part, whole.at[f, rows, lanes], device))
    for ref, whole in ((gate_ref, gate_all), (up_ref, up_all)):
        part = ref.at[:, pl.ds(window_start(f_sib), WINDOW)]
        spread.append(links.push(part, whole.at[f], sib))
    gather_end(first, relays)

    def vector(row, count):
        return jnp.concatenate([small_all[n, row : row + 1, 0:count] for n in range(4)], axis=1)

    normed = (inputs * scale * vector(1, SHARD)).astype(BF)
    normed_ref[...] = normed
    cosine, sine = cos_ref[...], sin_ref[...]
    low = lanes_below((ROWS, 128), 64)

    queries = dot(normed, wq_all[...].reshape(WIDTH, WIDTH)) + vector(0, SHARD)
    keys = dot(normed, wk_all[...].reshape(WIDTH, 128)) + vector(3, 32)
    values = dot(normed, wv_all[...].reshape(WIDTH, 128)) + vector(4, 32)
    keys = turn_pairs(keys, cosine, sine).astype(BF).astype(F32)
    values = values.astype(BF).astype(F32)
    own[...] = jnp.zeros(own.shape, BF)
    own[0, 0:ROWS] = jnp.where(low, keys, swap64(values)).astype(BF)
    own[1, 0:ROWS] = jnp.where(low, swap64(keys), values).astype(BF)

    slab_of = (x, z)
    spot = [
        pl.ds(pl.multiple_of((z * 2 + yl) * ROWS, ROWS), ROWS),
        pl.ds(pl.multiple_of((x * 2 + yl) * ROWS, ROWS), ROWS),
    ]
    pair = [
        pl.ds(pl.multiple_of(z * 2 * ROWS, 2 * ROWS), 2 * ROWS),
        pl.ds(pl.multiple_of(x * 2 * ROWS, 2 * ROWS), 2 * ROWS),
    ]
    mates = [
        links.push(own.at[g, 0:ROWS], kv_ref.at[g, slab_of[g], spot[g]], mate) for g in range(KVH)
    ]
    for g in range(KVH):
        kv_ref[g, slab_of[g], spot[g], :] = own[g, 0:ROWS]

    for tile in range(H // 2):
        part = turn_pairs(queries[:, tile * 128 : tile * 128 + 128], cosine, sine)
        part = part.astype(BF).astype(F32) * (1.0 / math.sqrt(HD))
        for half in range(2):
            head = tile * 2 + half
            j = head % GROUP
            mine = part if half == 0 else swap64(part)
            q_ref[head // GROUP, j * ROWS : (j + 1) * ROWS, 0:128] = jnp.where(
                low, mine, 0.0
            ).astype(BF)
    row = lax.broadcasted_iota(jnp.int32, (LANES, 128), 0)
    lane = lax.broadcasted_iota(jnp.int32, (LANES, 128), 1)
    block = lax.rem(lax.div(row, BLK), 2)
    hot = jnp.where((block == lane) & (row < GROUP * ROWS), 1.0, 0.0).astype(BF)
    for g in range(KVH):
        q_ref[g, :, 128:256] = hot
        q_ref[g, GROUP * ROWS :, 0:128] = jnp.zeros((LANES - GROUP * ROWS, 128), BF)

    def mix(g, keys, scores):
        old = top[g, 0:1]
        new = jnp.maximum(old, jnp.max(scores, axis=0, keepdims=True))
        weights = jnp.exp(scores - new).astype(BF)
        acc[g] = acc[g] * jnp.exp(old - new) + dot(keys.T[64:136], weights)
        top[g, 0:1] = new

    top[...] = jnp.full(top.shape, MASKED, F32)
    acc[...] = jnp.zeros(acc.shape, F32)
    for copy in mates:
        copy.wait()
    pairs = [
        links.push(kv_ref.at[0, x, pair[0]], kv_ref.at[0, x, pair[0]], device) for device in on_z
    ] + [links.push(kv_ref.at[1, z, pair[1]], kv_ref.at[1, z, pair[1]], device) for device in on_x]
    mask = jnp.where(kpos_ref[:, 0:1] <= qpos_ref[0:1], 0.0, MASKED)
    for g in range(KVH):
        keys = jnp.concatenate([own[g], own_extra()], axis=1)
        mix(g, keys, dot_nt(keys, q_ref[g]) + mask)
    for copy in pairs:
        copy.wait()
    base = links.reserve(6)

    def slab_copy(g, d, slab):
        device = (
            ((yl * 4 + jnp.where(g == 0, turn(x, d), x)) * 4 + jnp.where(g == 0, z, turn(z, d))),
            f,
        )
        return links.copy(kv_ref.at[g, slab], kv_ref.at[g, slab], device, base + g * 3 + d - 1)

    for d in (1, 3):
        for g in range(KVH):
            slab_copy(g, d, slab_of[g]).start()
    again = links.reserve(12)

    def quarters():
        copies = []
        for whole, n, devices in ((gate_all, x, on_x), (up_all, z, on_z)):
            rows, lanes = quarter(n, 0)
            for index in (f_cross, f_far):
                part = whole.at[index, rows, lanes]
                copies += [
                    links.copy(part, part, device, again + len(copies) + m)
                    for m, device in enumerate(devices)
                ]
        return copies

    second = links.reserve(4)

    def outer():
        copies = []
        for mine, whole in ((wo_ref, wo_all), (cot_ref, cot_all)):
            for device in (sib, cross):
                copies.append(links.copy(mine, whole.at[f], device, second + len(copies)))
        return copies

    def slabs_on():
        for g in range(KVH):
            slab_copy(g, 2, slab_of[g]).start()

    def spread_on():
        for copy in spread[0:4]:
            copy.wait_recv()
        for copy in quarters() + outer():
            copy.start()

    def step(i, _):
        g, n = lax.rem(i, 2), lax.div(i, 2)
        d = jnp.where(n == 2, 3, jnp.where(n == 3, 2, n))
        slab = turn(jnp.where(g == 0, x, z), d)

        @pl.when(n > 0)
        def _():
            slab_copy(g, 4 - d, slab).wait_recv()

        rows = extra_ref[g, pl.ds(pl.multiple_of(slab * 16, 16), 16), :]
        keys = jnp.concatenate([kv_ref[g, slab], key_extra(rows)], axis=1)
        mix(g, keys, dot_nt(keys, q_ref[g]))
        pl.when(i == 1)(slabs_on)
        pl.when(i == 3)(spread_on)
        return 0

    lax.fori_loop(0, 8, step, 0)
    for d in (1, 2, 3):
        for g in range(KVH):
            slab_copy(g, d, slab_of[g]).wait_send()
    outers = outer()
    second = list(zip(outers[0::2], outers[1::2], (wo_all, cot_all)))
    relays = gather_relay(second)

    for g in range(KVH):
        total = acc[g, 66:67]
        out = acc[g, 0:64] / total
        ot_ref[g] = out
        lse_ref[g] = jnp.broadcast_to(top[g, 0:1] + jnp.log(total), (8, LANES))
        natural[g] = jnp.concatenate([out, jnp.zeros((64, LANES), F32)], axis=0).T
    for tile in range(H // 2):
        even, odd = tile * 2, tile * 2 + 1
        left = natural[even // GROUP, (even % GROUP) * ROWS : (even % GROUP + 1) * ROWS]
        right = natural[odd // GROUP, (odd % GROUP) * ROWS : (odd % GROUP + 1) * ROWS]
        attended_ref[:, tile * 128 : tile * 128 + 128] = jnp.where(
            low, left, swap64(right)
        ).astype(BF)
    for copy in spread[0:4]:
        copy.wait_send()
    for copy in spread[4:] + quarters():
        copy.wait()
    gather_end(second, relays)
    for copy in keep:
        copy.wait()


def front(*operands):
    shape = jax.ShapeDtypeStruct
    scalars = pl.BlockSpec(memory_space=pltpu.SMEM)
    return pl.pallas_call(
        front_kernel,
        out_shape=[
            shape((ROWS, WIDTH), BF),
            shape((KVH, HD, LANES), F32),
            shape((KVH, 8, LANES), F32),
            shape((KVH, LANES, 256), BF),
            shape((KVH, SLABS, SLAB, 128), BF),
            shape((ROWS, WIDTH), BF),
            shape((4, SHARD, WIDTH), BF),
            shape((4, SHARD, 128), BF),
            shape((4, SHARD, 128), BF),
            shape((4, 8, 256), F32),
            shape((ROWS, 128), F32),
            shape((ROWS, 128), F32),
            shape((KVH, 64, 128), F32),
            shape((OWN, 128), F32),
            shape((8, LANES), F32),
            shape((4, SHARD, WIDTH), BF),
            shape((4, SHARD, WINDOW), BF),
            shape((4, SHARD, WINDOW), BF),
            shape((4, ROWS, WIDTH), BF),
        ],
        in_specs=[VMEM] * 9 + [scalars] + [VMEM] * 2 + [ANY] * 4,
        out_specs=[VMEM] * 15 + [ANY] * 4,
        scratch_shapes=[
            pltpu.VMEM((KVH, OWN, 128), BF),
            pltpu.VMEM((KVH, 72, LANES), F32),
            pltpu.VMEM((KVH, 8, LANES), F32),
            pltpu.VMEM((KVH, LANES, 128), F32),
            pltpu.SemaphoreType.DMA((64,)),
            pltpu.SemaphoreType.DMA((64,)),
            pltpu.SemaphoreType.DMA((4,)),
        ],
        compiler_params=pltpu.CompilerParams(
            vmem_limit_bytes=58 * MIB, collective_id=0, has_side_effects=True
        ),
        name="front",
    )(*operands)


def tile_stores(ref, value, first_row, first_lane, place_of):
    for r in range(value.shape[0] // 16):
        for n in range(value.shape[1] // 128):
            p, k = place_of(first_row + r, first_lane + n)
            ref[p // 4, p % 4, k] = value[r * 16 : r * 16 + 16, n * 128 : n * 128 + 128]


def gate_place(r, n):
    t = (r % 14) * 20 + n
    return t // 18, 18 * (r // 14) + t % 18


def down_place(r, n):
    t = r * 7 + n
    return t // 34, t % 34


def middle_kernel(
    attended_ref,
    tokens_ref,
    small_all,
    wo_all,
    cot_all,
    gate_hbm,
    up_hbm,
    gate_own,
    up_own,
    down_hbm,
    output_ref,
    grad_middle_ref,
    grad_attn_ref,
    gain_ref,
    do_ref,
    grads_ref,
    sum_a_ref,
    sum_b_ref,
    gate_ref,
    up_ref,
    down_ref,
    blocks,
    back_gate,
    hidden_ref,
    down_grad,
    two,
    two_in,
    out,
    out_in,
    downs,
    relay,
    landing,
    staged,
    send,
    recv,
    local,
):
    yl, x, z, yh, c = place()
    f = yh * 2 + c
    f_cross = (1 - yh) * 2 + c
    f_sib = yh * 2 + 1 - c
    f_far = (1 - yh) * 2 + 1 - c
    sib = at(yl, x, z, yh, 1 - c)
    cross = at(1 - yl, x, z, 1 - yh, c)
    links = Links(send, recv)
    window = pl.ds(window_start(f), WINDOW)
    loads = [
        pltpu.make_async_copy(
            down_hbm, down_ref.at[pl.ds(pl.multiple_of(64 * c, 64), UNITS)], local.at[0]
        ),
        pltpu.make_async_copy(gate_own.at[:, window], gate_ref.at[f], local.at[1]),
        pltpu.make_async_copy(up_own.at[:, window], up_ref.at[f], local.at[2]),
    ]
    for n, index in enumerate((f_sib, f_cross, f_far)):
        loads += [
            pltpu.make_async_copy(gate_hbm.at[index], gate_ref.at[index], local.at[3 + 2 * n]),
            pltpu.make_async_copy(up_hbm.at[index], up_ref.at[index], local.at[4 + 2 * n]),
        ]
    for copy in loads:
        copy.start()
    down_ref[pl.ds(pl.multiple_of((1 - c) * UNITS, 64), 64), :] = jnp.zeros((64, WIDTH), BF)
    on_x = [at(yl, turn(x, d), z, yh, c) for d in (1, 2, 3)]
    on_z = [at(yl, x, turn(z, d), yh, c) for d in (1, 2, 3)]
    greet([sib, cross, on_x[0], on_x[2], on_z[0], on_z[2]])
    rings = (
        RingSum(
            links,
            x,
            on_x,
            lambda n, half: downs.at[n, 2 * half : 2 * half + 2, 0:17],
            relay.at[0],
            landing.at[0],
            staged.at[0],
        ),
        RingSum(
            links,
            z,
            on_z,
            lambda n, half: downs.at[2 * half : 2 * half + 2, n, 17:34],
            relay.at[1],
            landing.at[1],
            staged.at[1],
        ),
    )

    gain = jnp.concatenate([small_all[n, 2:3, 0:SHARD] for n in range(4)], axis=1)
    wo = wo_all[...].reshape(WIDTH, WIDTH)
    middle = tokens_ref[...].astype(F32) + dot(attended_ref[...], wo)
    scale = lax.rsqrt(jnp.mean(middle * middle, axis=-1, keepdims=True) + EPSILON)
    grad_middle_ref[...] = middle
    blocks[0] = (middle * scale * gain).astype(BF)
    beside = links.push(blocks.at[0], blocks.at[1], sib)
    over = links.push(blocks.at[0], blocks.at[2], cross)
    order = ((f, f_sib), (f_cross, f_far))
    for copy in loads:
        copy.wait()

    def grads_of(p):
        return jnp.concatenate([cot_all[order[p][0]], cot_all[order[p][1]]], axis=0)

    def hidden_grad(p):
        return dot_nt(grads_of(p), down_ref[...])

    def units(p, grad_hidden):
        rows = slice(p * 2 * ROWS, (p + 1) * 2 * ROWS)
        block = blocks[2 * p : 2 * p + 2].reshape(2 * ROWS, WIDTH)
        gate_pre = dot(block, gate_ref[...].reshape(WIDTH, WINDOW))
        upward = dot(block, up_ref[...].reshape(WIDTH, WINDOW))
        sigmoid = 1.0 / (1.0 + jnp.exp(-gate_pre))
        swish = gate_pre * sigmoid
        hidden_ref[rows] = (swish * upward).astype(BF)
        back_gate[rows, 0:WINDOW] = (
            grad_hidden * upward * sigmoid * (1.0 + gate_pre * (1.0 - sigmoid))
        ).astype(BF)
        back_gate[rows, WINDOW:] = (grad_hidden * swish).astype(BF)

    def two_part(p):
        rows = slice(p * 2 * ROWS, (p + 1) * 2 * ROWS)
        return dot_nt(back_gate[rows, 0:WINDOW], gate_ref[...].reshape(WIDTH, WINDOW)) + dot_nt(
            back_gate[rows, WINDOW:], up_ref[...].reshape(WIDTH, WINDOW)
        )

    def out_part(p):
        rows = slice(p * 2 * ROWS, (p + 1) * 2 * ROWS)
        return dot(hidden_ref[rows], down_ref[...])

    beside.wait()
    units(0, hidden_grad(0))
    part = two_part(0)
    two_mine = part[0:ROWS]
    two[0] = part[ROWS:].astype(BF)
    two_copies = [links.push(two.at[0], two_in.at[0], sib)]
    far_grad = hidden_grad(1)
    over.wait()
    relay = links.push(blocks.at[2], blocks.at[3], sib)
    relay.wait()
    units(1, far_grad)
    part = two_part(1)
    two[1] = part[ROWS:].astype(BF)
    copy = links.push(two.at[1], two_in.at[1], sib)
    two_cross = part[0:ROWS]
    part = out_part(1)
    out[1] = part[ROWS:].astype(BF)
    copy.wait()
    two[2] = (two_cross + two_in[1].astype(F32)).astype(BF)
    two_copies.append(links.push(two.at[2], two_in.at[2], cross))
    copy = links.push(out.at[1], out_in.at[1], sib)
    out_cross = part[0:ROWS]
    part = out_part(0)
    out_mine = part[0:ROWS]
    out[0] = part[ROWS:].astype(BF)
    out_copies = [links.push(out.at[0], out_in.at[0], sib)]
    copy.wait()
    out[2] = (out_cross + out_in[1].astype(F32)).astype(BF)
    out_copies.append(links.push(out.at[2], out_in.at[2], cross))

    down_grad[...] = dot_tn(
        hidden_ref[...], jnp.concatenate([grads_of(0), grads_of(1)], axis=0)
    ).astype(BF)
    blank = jnp.zeros((16, 128), BF)
    product = down_grad[pl.ds(pl.multiple_of(64 * c, 64), UNITS), :]
    tile_stores(downs, product, 0, 0, down_place)
    for t in range(532, 544):
        downs[3, 3, t % 34] = blank
    for ring in rings:
        ring.start()
    staged[0, 0] = downs[turn(x, 1), 0:2, 0:17]
    staged[0, 1] = downs[turn(x, 3), 2:4, 0:17]
    staged[1, 0] = downs[0:2, turn(z, 1), 17:34]
    staged[1, 1] = downs[2:4, turn(z, 3), 17:34]
    block = blocks[...].reshape(4 * ROWS, WIDTH)
    for n in range(0, 2 * WINDOW, 512):
        product = dot_tn(block, back_gate[:, n : n + 512]).astype(BF)
        tile_stores(grads_ref, product, 0, n // 128, gate_place)
        if n == 1536:
            for ring in rings:
                ring.merge()
    for n in range(4):
        for t in range(280, 288):
            grads_ref[3, 3, 18 * n + t % 18] = blank

    for copy in two_copies:
        copy.wait()
    grad_two = two_mine + two_in[0].astype(F32) + two_in[2].astype(F32)
    middle = grad_middle_ref[...]
    scale = lax.rsqrt(jnp.mean(middle * middle, axis=-1, keepdims=True) + EPSILON)
    weighted = grad_two * gain
    grad_middle = (
        cot_all[f].astype(F32)
        + scale * weighted
        - middle * (scale * scale * scale) * jnp.mean(weighted * middle, axis=-1, keepdims=True)
    )
    gain_ref[...] = jnp.broadcast_to(
        jnp.sum(grad_two * middle * scale, axis=0, keepdims=True), (8, WIDTH)
    )
    grad_attn = grad_middle.astype(BF)
    grad_attn_ref[...] = grad_attn
    grad_middle_ref[...] = grad_middle
    grad_attended = dot_nt(grad_attn, wo_all[...].reshape(WIDTH, WIDTH)).astype(BF).astype(F32)
    low = lanes_below((ROWS, 128), 64)
    for tile in range(H // 2):
        part = grad_attended[:, tile * 128 : tile * 128 + 128]
        for half in range(2):
            head = tile * 2 + half
            j = head % GROUP
            mine = swap64(part) if half == 0 else part
            do_ref[head // GROUP, j * ROWS : (j + 1) * ROWS] = jnp.where(low, 0.0, mine).astype(BF)
    for g in range(KVH):
        do_ref[g, GROUP * ROWS :] = jnp.zeros((LANES - GROUP * ROWS, 128), BF)
    for copy in out_copies:
        copy.wait()
    total = out_mine + out_in[0].astype(F32) + out_in[2].astype(F32)
    output_ref[...] = (middle + total).astype(BF)
    for ring in rings:
        ring.finish()
    for half in range(2):
        two_of = slice(2 * half, 2 * half + 2)
        sum_a_ref[two_of] = (downs[x, two_of, 0:17].astype(F32) + rings[0].arrived(half)).astype(BF)
        sum_b_ref[two_of] = (downs[two_of, z, 17:34].astype(F32) + rings[1].arrived(half)).astype(BF)


def middle_call(*operands):
    shape = jax.ShapeDtypeStruct
    return pl.pallas_call(
        middle_kernel,
        out_shape=[
            shape((ROWS, WIDTH), BF),
            shape((ROWS, WIDTH), F32),
            shape((ROWS, WIDTH), BF),
            shape((8, WIDTH), F32),
            shape((KVH, LANES, 128), BF),
            shape((4, 4, 72, 16, 128), BF),
            shape((4, 17, 16, 128), BF),
            shape((4, 17, 16, 128), BF),
        ],
        in_specs=[VMEM] * 5 + [ANY] * 5,
        out_specs=[VMEM] * 8,
        scratch_shapes=[
            pltpu.VMEM((4, SHARD, WINDOW), BF),
            pltpu.VMEM((4, SHARD, WINDOW), BF),
            pltpu.VMEM((WINDOW, WIDTH), BF),
            pltpu.VMEM((4, ROWS, WIDTH), BF),
            pltpu.VMEM((4 * ROWS, 2 * WINDOW), BF),
            pltpu.VMEM((4 * ROWS, WINDOW), BF),
            pltpu.VMEM((WINDOW, WIDTH), BF),
            pltpu.VMEM((3, ROWS, WIDTH), BF),
            pltpu.VMEM((3, ROWS, WIDTH), BF),
            pltpu.VMEM((3, ROWS, WIDTH), BF),
            pltpu.VMEM((3, ROWS, WIDTH), BF),
            pltpu.VMEM((4, 4, 34, 16, 128), BF),
            pltpu.VMEM((2, 2, 2, 17, 16, 128), BF),
            pltpu.VMEM((2, 2, 2, 2, 17, 16, 128), BF),
            pltpu.VMEM((2, 2, 2, 17, 16, 128), BF),
            pltpu.SemaphoreType.DMA((24,)),
            pltpu.SemaphoreType.DMA((24,)),
            pltpu.SemaphoreType.DMA((9,)),
        ],
        compiler_params=pltpu.CompilerParams(
            vmem_limit_bytes=60 * MIB, collective_id=3, has_side_effects=True
        ),
        name="middle",
    )(*operands)


UNIT = 72
HALF = 36
DOWN = 17
CHUNK = 768


def widen(ref, index):
    return ref[index].astype(F32)


def back_kernel(
    q_ref,
    do_ref,
    ot_ref,
    lse_ref,
    kv_ref,
    extra_ref,
    kpos_ref,
    qpos_ref,
    down_a_ref,
    down_b_ref,
    cos_ref,
    sin_ref,
    normed_ref,
    attended_ref,
    grad_attn_ref,
    grad_middle_ref,
    tokens_ref,
    wq_all,
    wk_all,
    wv_all,
    small_all,
    hidden_gain_ref,
    grads_ref,
    token_grad_ref,
    late_ref,
    thin_ref,
    whole_ref,
    downs_ref,
    dq_ref,
    dkv_ref,
    sum_ref,
    qx,
    dox,
    own,
    own_grad,
    parts,
    parts_in,
    pairs,
    pairs_in,
    across,
    side_a,
    side_b,
    relay,
    landing,
    staged,
    late_a,
    late_b,
    whole,
    whole_in,
    down_late,
    down_whole,
    down_in,
    natural,
    table,
    table_in,
    lines,
    lines_in,
    cols,
    cols_in,
    ends,
    ends_in,
    thin,
    send,
    recv,
    local,
):
    yl, x, z, yh, c = place()
    f = yh * 2 + c
    f_cross = (1 - yh) * 2 + c
    f_sib = yh * 2 + 1 - c
    f_far = (1 - yh) * 2 + 1 - c
    sib = at(yl, x, z, yh, 1 - c)
    cross = at(1 - yl, x, z, 1 - yh, c)
    far = at(1 - yl, x, z, 1 - yh, 1 - c)
    mate = at(1 - yl, x, z, yh, c)
    on_x = [at(yl, turn(x, d), z, yh, c) for d in (1, 2, 3)]
    on_z = [at(yl, x, turn(z, d), yh, c) for d in (1, 2, 3)]
    links = Links(send, recv)
    greet([sib, cross, far, mate] + on_x + on_z)

    rings = (
        RingSum(
            links,
            x,
            on_x,
            lambda n, half: grads_ref.at[n, 2 * half : 2 * half + 2, 0:HALF],
            relay.at[0],
            landing.at[0],
            staged.at[0],
        ),
        RingSum(
            links,
            z,
            on_z,
            lambda n, half: grads_ref.at[2 * half : 2 * half + 2, n, HALF:UNIT],
            relay.at[1],
            landing.at[1],
            staged.at[1],
        ),
    )
    def keep():
        moves = (
            (grads_ref.at[turn(x, 1), 0:2, 0:HALF], staged.at[0, 0]),
            (grads_ref.at[turn(x, 3), 2:4, 0:HALF], staged.at[0, 1]),
            (grads_ref.at[0:2, turn(z, 1), HALF:UNIT], staged.at[1, 0]),
            (grads_ref.at[2:4, turn(z, 3), HALF:UNIT], staged.at[1, 1]),
            (grads_ref.at[x, :, 0:HALF], side_a),
            (grads_ref.at[:, z, HALF:UNIT], side_b),
        )
        return [pltpu.make_async_copy(*move, local.at[n]) for n, move in enumerate(moves)]

    for copy in keep():
        copy.start()

    down_second, down_third, down_fourth, down_fifth, down_sixth = (
        links.reserve(6),
        links.reserve(1),
        links.reserve(6),
        links.reserve(4),
        links.reserve(4),
    )

    def down_copies():
        copies = []
        for n in range(3):
            for source, half, index, device in (
                (down_a_ref, 0, turn(z, n + 1), on_z[n]),
                (down_b_ref, 1, turn(x, n + 1), on_x[n]),
            ):
                copies.append(
                    links.copy(
                        source.at[index],
                        down_late.at[half, n],
                        device,
                        down_second + len(copies),
                    )
                )
        return copies

    def down_mate():
        return links.copy(down_whole, down_in, mate, down_third)

    def down_third_start():
        for copy in down_copies():
            copy.wait()
        for half, own_part in ((0, down_a_ref[z]), (1, down_b_ref[x])):
            total = own_part.astype(F32)
            for m in range(3):
                total = total + down_late[half, m].astype(F32)
            down_whole[half] = total.astype(BF)
        down_mate().start()

    def down_spread():
        copies = []
        for n in range(3):
            for half, device in ((0, on_z[n]), (1, on_x[n])):
                part = downs_ref.at[half, x, z]
                copies.append(links.copy(part, part, device, down_fourth + len(copies)))
        return copies

    def down_spread_start():
        down_mate().wait()
        downs_ref[:, x, z] = (
            down_whole[...].astype(F32) + down_in[...].astype(F32)
        ).astype(BF)
        for copy in down_spread():
            copy.start()

    def down_rounds():
        copies = []
        for n in (0, 2):
            for part, device in (
                (downs_ref.at[0, x], on_x[n]),
                (downs_ref.at[1, :, z], on_z[n]),
            ):
                copies.append(links.copy(part, part, device, down_fifth + len(copies)))
        return copies

    def down_rounds_start():
        for copy in down_spread():
            copy.wait()
        for copy in down_rounds():
            copy.start()

    def down_last():
        copies = []
        for half, came, n in ((0, 3, 0), (1, 1, 2)):
            rows = slice(2 * half, 2 * half + 2)
            for part, device in (
                (downs_ref.at[0, turn(x, came), rows], on_x[n]),
                (downs_ref.at[1, rows, turn(z, came)], on_z[n]),
            ):
                copies.append(links.copy(part, part, device, down_sixth + len(copies)))
        return copies

    def down_last_start():
        for copy in down_rounds():
            copy.wait()
        for copy in down_last():
            copy.start()


    for copy in down_copies():
        copy.start()
    for ring in rings:
        ring.start()

    row = lax.broadcasted_iota(jnp.int32, (128, LANES), 0)
    for g in range(KVH):
        lse = thirds(lse_ref[g, 0:1])
        inner = jnp.sum(do_ref[g].astype(F32).T[64:128] * ot_ref[g], axis=0, keepdims=True)
        inner = thirds(inner)
        extra_q = jnp.zeros((128, LANES), F32)
        extra_d = jnp.zeros((128, LANES), F32)
        for n in range(3):
            extra_q = jnp.where(row == 2 + n, -lse[n], extra_q)
            extra_d = jnp.where(row == 2 + n, -inner[n], extra_d)
        qx[g, :, 0:128] = q_ref[g, :, 0:128]
        qx[g, :, 128:256] = (q_ref[g, :, 128:256].astype(F32) + extra_q.T).astype(BF)
        dox[g, :, 0:128] = do_ref[g]
        dox[g, :, 128:256] = extra_d.T.astype(BF)

    def piece(g, keys, mask):
        scores = dot_nt(keys, qx[g])
        if mask is not None:
            scores = scores + mask
        probs = jnp.exp(scores)
        grad = (probs * dot_nt(keys, dox[g])).astype(BF)
        both = dot(grad, qx[g, :, 0:128]) + dot(probs.astype(BF), dox[g, :, 0:128])
        return both, dot(keys[:, 0:128].T[0:64], grad)

    mask = jnp.where(kpos_ref[:, 0:1] <= qpos_ref[0:1], 0.0, MASKED)
    spots = (
        pl.ds(pl.multiple_of((z * 2 + yl) * ROWS, ROWS), ROWS),
        pl.ds(pl.multiple_of((x * 2 + yl) * ROWS, ROWS), ROWS),
    )
    slab_of = (x, z)
    for g in range(KVH):
        own[...] = jnp.zeros(own.shape, BF)
        own[0:ROWS] = kv_ref[g, slab_of[g], spots[g], :]
        both, dq = piece(g, jnp.concatenate([own[...], own_extra()], axis=1), mask)
        own_grad[g] = both[0:ROWS]
        dq_ref[g] = dq
    count = SLAB // CHUNK
    base = links.reserve(6)

    across_base = links.reserve(16)

    def across_copy(g, d, slab, part):
        rows = pl.ds(2 * part, 2)
        return links.copy(
            parts.at[g, slab, rows, 1 - yl],
            across.at[g, d, rows],
            mate,
            across_base + (g * 4 + d) * 2 + part,
        )

    def part_copy(g, d, slab):
        device = (
            ((yl * 4 + jnp.where(g == 0, slab, x)) * 4 + jnp.where(g == 0, z, slab)),
            f,
        )
        return links.copy(
            across.at[g, d], parts_in.at[g, d - 1], device, base + g * 3 + d - 1
        )

    def combine(g, d, slab):
        for part in range(count):
            across_copy(g, d, slab, part).wait()
        total = parts[g, slab, :, yl].astype(F32) + across[g, d].astype(F32)
        across[g, d] = total.astype(BF)

    def slab_at(n):
        g, d = lax.rem(n, 2), lax.rem(lax.div(n, 2) + 1, 4)
        return g, d, turn(jnp.where(g == 0, x, z), d)

    def step(i, _):
        n, part = lax.div(i, count), lax.rem(i, count)
        g, d, slab = slab_at(n)
        start = pl.multiple_of(part * CHUNK, CHUNK)
        rows = extra_ref[g, pl.ds(pl.multiple_of(slab * 16 + part * 8, 8), 8), :]
        keys = jnp.concatenate([kv_ref[g, slab, pl.ds(start, CHUNK), :], key_extra(rows)], axis=1)
        both, dq = piece(g, keys, None)
        parts[g, slab, pl.ds(2 * part, 2)] = both.astype(BF).reshape(2, 2, ROWS, 128)
        dq_ref[g] += dq

        across_copy(g, d, slab, part).start()

        @pl.when((part == count - 1) & (n > 0))
        def _():
            before = slab_at(n - 1)
            combine(*before)

            @pl.when(n < 7)
            def _():
                part_copy(*before).start()

        for at_step, event in events:
            pl.when(i == at_step)(event)
        return 0

    pair_base, second_base, third_slot = (
        links.reserve(6),
        links.reserve(6),
        links.reserve(1),
    )

    def pair_copies(g):
        other, devices = (z, x)[g], (on_z, on_x)[g]
        return [
            links.copy(
                pairs.at[g, turn(other, n + 1)],
                pairs_in.at[g, n],
                devices[n],
                pair_base + 3 * g + n,
            )
            for n in range(3)
        ]

    def pair_start(g):
        slab = slab_of[g]
        for d in (1, 2, 3):
            part_copy(g, d, turn(slab, d)).wait()
        for n in range(4):
            total = across[g, 0, n].astype(F32)
            for m in range(3):
                total = total + parts_in[g, m, n].astype(F32)
            pairs[g, n] = total.astype(BF)
        for copy in pair_copies(g):
            copy.start()

    def pair_end(g):
        for copy in pair_copies(g):
            copy.wait()
        total = pairs[g, (z, x)[g]].astype(F32) + own_grad[g]
        for m in range(3):
            total = total + pairs_in[g, m].astype(F32)
        dkv_ref[g] = total

    def merge():
        for copy in keep():
            copy.wait()
        for ring in rings:
            ring.merge()

    def second_copies():
        copies = []
        for n in range(3):
            for source, target, index, device in (
                (side_a, late_a, turn(z, n + 1), on_z[n]),
                (side_b, late_b, turn(x, n + 1), on_x[n]),
            ):
                copies.append(
                    links.copy(source.at[index], target.at[n], device, second_base + len(copies))
                )
        return copies

    def second_start():
        for side, ring in zip((side_a, side_b), rings):
            ring.finish()
            for half in range(2):
                rows = slice(2 * half, 2 * half + 2)
                side[rows] = (side[rows].astype(F32) + ring.arrived(half)).astype(BF)
        for copy in second_copies():
            copy.start()

    def third():
        return links.copy(whole, whole_in, mate, third_slot)

    def third_start():
        for copy in second_copies():
            copy.wait()
        a = side_a[z].astype(F32)
        b = side_b[x].astype(F32)
        for m in range(3):
            a = a + late_a[m].astype(F32)
            b = b + late_b[m].astype(F32)
        whole[0:HALF] = a.astype(BF)
        whole[HALF:UNIT] = b.astype(BF)
        third().start()

    events = (
        (1, down_third_start),
        (6, down_spread_start),
        (5, merge),
        (10, second_start),
        (11, down_rounds_start),
        (13, third_start),
        (15, down_last_start),
    )
    lax.fori_loop(0, KVH * SLABS * count, step, 0)
    pair_start(0)

    low = lanes_below((ROWS, 128), 64)
    cosine, sine = cos_ref[...], -sin_ref[...]

    def assemble(tile):
        even, odd = tile * 2, tile * 2 + 1
        left = natural[even // GROUP, (even % GROUP) * ROWS : (even % GROUP + 1) * ROWS]
        right = natural[odd // GROUP, (odd % GROUP) * ROWS : (odd % GROUP + 1) * ROWS]
        return jnp.where(low, left, swap64(right))

    for g in range(KVH):
        natural[g] = jnp.concatenate([dq_ref[g], jnp.zeros((64, LANES), F32)], axis=0).T
    grad_queries = jnp.concatenate(
        [
            turn_pairs(assemble(tile) * (1.0 / math.sqrt(HD)), cosine, sine)
            for tile in range(H // 2)
        ],
        axis=1,
    ).astype(BF)

    combine(1, 0, slab_of[1])
    pair_start(1)

    normed = normed_ref[...]

    def table_columns(first, left, right):
        product = dot_tn(left, right).astype(BF)
        for n in range(right.shape[1] // 128):
            table[first + n] = product[:, n * 128 : n * 128 + 128].reshape(4, SHARD, 128)

    def beside(slot, start, stop):
        return [
            links.copy(
                table.at[start:stop, 2 * n + 1 - c], table_in.at[n, start:stop], sib, slot + n
            )
            for n in range(2)
        ]

    def add_beside(n, _):
        for m in range(2):
            total = table[n, 2 * m + c].astype(F32) + table_in[m, n].astype(F32)
            lines[m, n] = total.astype(BF)
        return 0

    beside_slots = links.reserve(6)
    table_columns(0, normed, grad_queries)
    for copy in beside(beside_slots, 0, 7):
        copy.start()
    table_columns(9, attended_ref[...], grad_attn_ref[...])
    for copy in beside(beside_slots + 2, 9, 16):
        copy.start()
    pair_end(0)

    third().wait()
    sum_ref[...] = (whole[...].astype(F32) + whole_in[...].astype(F32)).astype(BF)

    def spot(index):
        return pl.ds(18 * index, 18)

    shared = [
        links.push(sum_ref.at[spot(index)], whole_ref.at[x, z, spot(f)], device)
        for device, index in ((cross, f_cross), (far, f_far), (sib, f_sib))
    ]
    keep_own = [
        pltpu.make_async_copy(sum_ref.at[spot(f)], whole_ref.at[x, z, spot(f)], local.at[0])
    ]
    for copy in keep_own:
        copy.start()
    for copy in beside(beside_slots, 0, 7) + beside(beside_slots + 2, 9, 16):
        copy.wait()
    lax.fori_loop(0, 7, add_beside, 0)
    lax.fori_loop(9, 16, add_beside, 0)

    pair_end(1)
    grad_keys = turn_pairs(jnp.where(low, dkv_ref[0], swap64(dkv_ref[1])), cosine, sine).astype(BF)
    grad_values = jnp.where(low, swap64(dkv_ref[0]), dkv_ref[1]).astype(BF)
    table_columns(7, normed, grad_keys)
    table_columns(8, normed, grad_values)
    for copy in beside(beside_slots + 4, 7, 9):
        copy.start()

    for copy in keep_own + shared:
        copy.wait()
    spread = []
    for n in range(3):
        spread.append(
            links.push(whole_ref.at[x, z, 0:HALF], whole_ref.at[x, z, 0:HALF], on_z[n])
        )
        spread.append(
            links.push(whole_ref.at[x, z, HALF:UNIT], whole_ref.at[x, z, HALF:UNIT], on_x[n])
        )
    for copy in beside(beside_slots + 4, 7, 9):
        copy.wait()
    lax.fori_loop(7, 9, add_beside, 0)

    along = []
    for n in range(3):
        xt, zt = turn(x, n + 1), turn(z, n + 1)
        along.append(links.push(lines.at[0, pl.ds(xt * 4, 4)], lines_in.at[0, n], on_x[n]))
        for m in range(4):
            along.append(
                links.push(lines.at[1, m * 4 + zt], lines_in.at[1, n, m], on_z[n])
            )

    inputs = tokens_ref[...].astype(F32)
    scale = lax.rsqrt(jnp.mean(inputs * inputs, axis=-1, keepdims=True) + EPSILON)

    def vector(row, count):
        return jnp.concatenate([small_all[n, row : row + 1, 0:count] for n in range(4)], axis=1)

    grad_normed = (
        dot_nt(grad_queries, wq_all[...].reshape(WIDTH, WIDTH))
        + dot_nt(grad_keys, wk_all[...].reshape(WIDTH, 128))
        + dot_nt(grad_values, wv_all[...].reshape(WIDTH, 128))
    )
    weighted = grad_normed * vector(1, SHARD)
    token_grad_ref[...] = (
        grad_middle_ref[...]
        + scale * weighted
        - inputs * (scale * scale * scale) * jnp.mean(weighted * inputs, axis=-1, keepdims=True)
    )
    thin[0, c] = jnp.concatenate(
        [
            jnp.sum(grad_queries.astype(F32), axis=0, keepdims=True),
            jnp.sum(grad_normed * inputs * scale, axis=0, keepdims=True),
            hidden_gain_ref[0:1],
            jnp.concatenate(
                [
                    jnp.sum(grad_keys.astype(F32), axis=0, keepdims=True),
                    jnp.sum(grad_values.astype(F32), axis=0, keepdims=True),
                    jnp.zeros((1, WIDTH - 256), F32),
                ],
                axis=1,
            ),
            jnp.zeros((4, WIDTH), F32),
        ],
        axis=0,
    )

    def thin_push(level, index, device):
        return links.push(thin.at[level, index], thin.at[level, index], device)

    thin_copy = thin_push(0, c, sib)
    thin_copy.wait()
    thin[1, x] = thin[0, 0] + thin[0, 1]
    for n in range(3):
        along.append(thin_push(1, x, on_x[n]))

    for copy in spread:
        copy.wait()
    rounds = []
    for n in (0, 2):
        rounds.append(
            links.push(whole_ref.at[x, :, 0:HALF], whole_ref.at[x, :, 0:HALF], on_x[n])
        )
        rounds.append(
            links.push(whole_ref.at[:, z, HALF:UNIT], whole_ref.at[:, z, HALF:UNIT], on_z[n])
        )
    for copy in along:
        copy.wait()
    for m in range(4):
        a = lines[0, x * 4 + m].astype(F32)
        b = lines[1, m * 4 + z].astype(F32)
        for n in range(3):
            a = a + lines_in[0, n, m].astype(F32)
            b = b + lines_in[1, n, m].astype(F32)
        cols[0, m] = a.astype(BF)
        cols[1, m] = b.astype(BF)
    thin[2, z] = (thin[1, 0] + thin[1, 1]) + (thin[1, 2] + thin[1, 3])
    along = []
    for n in range(3):
        along.append(links.push(cols.at[0, turn(z, n + 1)], cols_in.at[0, n], on_z[n]))
        along.append(links.push(cols.at[1, turn(x, n + 1)], cols_in.at[1, n], on_x[n]))
        along.append(thin_push(2, z, on_z[n]))
    for copy in along:
        copy.wait()
    a = cols[0, z].astype(F32)
    b = cols[1, x].astype(F32)
    for n in range(3):
        a = a + cols_in[0, n].astype(F32)
        b = b + cols_in[1, n].astype(F32)
    ends[0] = a.astype(BF)
    ends[1] = b.astype(BF)
    thin[3, yh] = (thin[2, 0] + thin[2, 1]) + (thin[2, 2] + thin[2, 3])
    along = [links.push(ends.at[1 - yh], ends_in.at[0], cross), thin_push(3, yh, cross)]
    for copy in along:
        copy.wait()
    ends[2] = (ends[yh].astype(F32) + ends_in[0].astype(F32)).astype(BF)
    thin[4, yl] = thin[3, 0] + thin[3, 1]
    along = [links.push(ends.at[2], ends_in.at[1], mate), thin_push(4, yl, mate)]
    for copy in along:
        copy.wait()
    late_ref[x, z] = (ends[2].astype(F32) + ends_in[1].astype(F32)).astype(BF)
    thin_ref[...] = thin[4, 0] + thin[4, 1]

    cut = SHARD // 2
    along = []
    for n in range(3):
        along.append(links.push(late_ref.at[x, z, 0:cut], late_ref.at[x, z, 0:cut], on_z[n]))
        along.append(links.push(late_ref.at[x, z, cut:], late_ref.at[x, z, cut:], on_x[n]))
    for copy in rounds:
        copy.wait()
    rounds = []
    for half, came, n in ((0, 3, 0), (1, 1, 2)):
        rows = slice(2 * half, 2 * half + 2)
        a = whole_ref.at[turn(x, came), rows, 0:HALF]
        b = whole_ref.at[rows, turn(z, came), HALF:UNIT]
        rounds += [links.push(a, a, on_x[n]), links.push(b, b, on_z[n])]
    for copy in along:
        copy.wait()
    along = []
    for n in range(3):
        along.append(links.push(late_ref.at[x, :, 0:cut], late_ref.at[x, :, 0:cut], on_x[n]))
        along.append(links.push(late_ref.at[:, z, cut:], late_ref.at[:, z, cut:], on_z[n]))
    for copy in along + rounds + down_last():
        copy.wait()


def back(*operands):
    shape = jax.ShapeDtypeStruct
    return pl.pallas_call(
        back_kernel,
        out_shape=[
            shape((ROWS, WIDTH), F32),
            shape((4, 4, SHARD, 128), BF),
            shape((8, WIDTH), F32),
            shape((4, 4, UNIT, 16, 128), BF),
            shape((2, 4, 4, DOWN, 16, 128), BF),
        ],
        in_specs=[VMEM] * 22 + [ANY],
        out_specs=[VMEM] * 3 + [ANY, VMEM],
        scratch_shapes=[
            pltpu.VMEM((KVH, HD, LANES), F32),
            pltpu.VMEM((KVH, ROWS, 128), F32),
            pltpu.VMEM((UNIT, 16, 128), BF),
            pltpu.VMEM((KVH, LANES, 256), BF),
            pltpu.VMEM((KVH, LANES, 256), BF),
            pltpu.VMEM((OWN, 128), BF),
            pltpu.VMEM((KVH, ROWS, 128), F32),
            pltpu.VMEM((KVH, SLABS, 4, 2, ROWS, 128), BF),
            pltpu.VMEM((KVH, 3, 4, ROWS, 128), BF),
            pltpu.VMEM((KVH, 4, ROWS, 128), BF),
            pltpu.VMEM((KVH, 3, ROWS, 128), BF),
            pltpu.VMEM((KVH, 4, 4, ROWS, 128), BF),
            pltpu.VMEM((4, HALF, 16, 128), BF),
            pltpu.VMEM((4, HALF, 16, 128), BF),
            pltpu.VMEM((2, 2, 2, HALF, 16, 128), BF),
            pltpu.VMEM((2, 2, 2, 2, HALF, 16, 128), BF),
            pltpu.VMEM((2, 2, 2, HALF, 16, 128), BF),
            pltpu.VMEM((3, HALF, 16, 128), BF),
            pltpu.VMEM((3, HALF, 16, 128), BF),
            pltpu.VMEM((UNIT, 16, 128), BF),
            pltpu.VMEM((UNIT, 16, 128), BF),
            pltpu.VMEM((2, 3, DOWN, 16, 128), BF),
            pltpu.VMEM((2, DOWN, 16, 128), BF),
            pltpu.VMEM((2, DOWN, 16, 128), BF),
            pltpu.VMEM((KVH, LANES, 128), F32),
            pltpu.VMEM((16, 4, SHARD, 128), BF),
            pltpu.VMEM((2, 16, SHARD, 128), BF),
            pltpu.VMEM((2, 16, SHARD, 128), BF),
            pltpu.VMEM((2, 3, 4, SHARD, 128), BF),
            pltpu.VMEM((2, 4, SHARD, 128), BF),
            pltpu.VMEM((2, 3, SHARD, 128), BF),
            pltpu.VMEM((3, SHARD, 128), BF),
            pltpu.VMEM((2, SHARD, 128), BF),
            pltpu.VMEM((5, 4, 8, WIDTH), F32),
            pltpu.SemaphoreType.DMA((144,)),
            pltpu.SemaphoreType.DMA((144,)),
            pltpu.SemaphoreType.DMA((6,)),
        ],
        compiler_params=pltpu.CompilerParams(
            vmem_limit_bytes=63 * MIB, collective_id=1, has_side_effects=True
        ),
        name="back",
    )(*operands)


def finish_kernel(
    late_ref,
    thin_ref,
    whole_ref,
    downs_ref,
    q_out,
    k_out,
    v_out,
    o_out,
    gate_out,
    up_out,
    down_out,
    qb_out,
    kb_out,
    vb_out,
    ag_out,
    hg_out,
    q_val,
    k_val,
    v_val,
    o_val,
    gate_val,
    up_val,
    down_val,
    sems,
):
    copies = []

    def leave(value, out):
        copy = pltpu.make_async_copy(value, out, sems.at[len(copies)])
        copy.start()
        copies.append(copy)

    def gate_tile(n, r, lane):
        t = r * 20 + lane
        p, k = t // 18, 18 * n + t % 18
        return whole_ref[p // 4, p % 4, k].astype(F32)

    for value, out, first in ((gate_val, gate_out, 0), (up_val, up_out, 10)):
        for r in range(14):
            for tile in range(38):
                parts = []
                for n in range(4):
                    lane = tile - (19 * n) // 2
                    if 0 <= lane < 10:
                        parts.append(gate_tile(n, r, first + lane))
                total = parts[0] if len(parts) == 1 else parts[0] + parts[1]
                value[r * 16 : r * 16 + 16, tile * 128 : tile * 128 + 128] = total
        leave(value, out)
    for r in range(76):
        for tile in range(7):
            t = r * 7 + tile
            p, k = t // 34, t % 34
            down_val[r * 16 : r * 16 + 16, tile * 128 : tile * 128 + 128] = downs_ref[
                k // DOWN, p // 4, p % 4, k % DOWN
            ].astype(F32)
    leave(down_val, down_out)
    column = 0
    for value, out, count in ((q_val, q_out, 7), (k_val, k_out, 1), (v_val, v_out, 1), (o_val, o_out, 7)):
        for tile in range(count):
            value[:, tile * 128 : tile * 128 + 128] = late_ref[column // 4, column % 4].astype(F32)
            column += 1
        leave(value, out)
    f = lax.axis_index("fsdp")

    def share(row, start, part):
        total = thin_ref[row : row + 1, start : start + part]
        for n in range(1, 4):
            first = start + n * part
            total = jnp.where(f == n, thin_ref[row : row + 1, first : first + part], total)
        return total

    qb_out[...] = share(0, 0, SHARD)
    kb_out[...] = share(3, 0, 32)
    vb_out[...] = share(3, 128, 32)
    ag_out[...] = share(1, 0, SHARD)
    hg_out[...] = share(2, 0, SHARD)
    for copy in copies:
        copy.wait()


def finish(late, thin, whole, downs):
    shape = jax.ShapeDtypeStruct
    large = [
        (SHARD, WIDTH),
        (SHARD, 128),
        (SHARD, 128),
        (SHARD, WIDTH),
        (SHARD, 4 * UNITS),
        (SHARD, 4 * UNITS),
        (UNITS, WIDTH),
    ]
    tiny = [(1, SHARD), (1, 32), (1, 32), (1, SHARD), (1, SHARD)]
    return pl.pallas_call(
        finish_kernel,
        out_shape=[shape(size, F32) for size in large + tiny],
        in_specs=[VMEM] * 4,
        out_specs=[ANY] * 7 + [VMEM] * 5,
        scratch_shapes=[pltpu.VMEM(size, F32) for size in large]
        + [pltpu.SemaphoreType.DMA((7,))],
        compiler_params=pltpu.CompilerParams(vmem_limit_bytes=58 * MIB),
        name="finish",
    )(late, thin, whole, downs)

def body(
    tokens,
    block_order,
    query_weight,
    key_weight,
    value_weight,
    output_weight,
    gate_weight,
    up_weight,
    down_weight,
    query_bias,
    key_bias,
    value_bias,
    attention_gain,
    hidden_gain,
    cotangent,
):
    def row(vector):
        return vector.reshape(1, -1)

    (
        attended,
        ot,
        lse,
        q,
        kv,
        normed,
        wq_all,
        wk_all,
        wv_all,
        small_all,
        cosine,
        sine,
        extra,
        kpos,
        qpos,
        wo_all,
        gate_all,
        up_all,
        cot_all,
    ) = front(
        tokens[0],
        query_weight,
        key_weight,
        value_weight,
        row(query_bias),
        row(attention_gain),
        row(hidden_gain),
        row(key_bias),
        row(value_bias),
        block_order,
        *angle_tables(),
        output_weight,
        gate_weight,
        up_weight,
        cotangent[0],
    )
    (
        output,
        grad_middle,
        grad_attn,
        hidden_gain_part,
        grad_attended,
        grads,
        down_a,
        down_b,
    ) = middle_call(
        attended,
        tokens[0],
        small_all,
        wo_all,
        cot_all,
        gate_all,
        up_all,
        gate_weight,
        up_weight,
        down_weight,
    )
    token_grad, late, thin, whole, downs = back(
        q,
        grad_attended,
        ot,
        lse,
        kv,
        extra,
        kpos,
        qpos,
        down_a,
        down_b,
        cosine,
        sine,
        normed,
        attended,
        grad_attn,
        grad_middle,
        tokens[0],
        wq_all,
        wk_all,
        wv_all,
        small_all,
        hidden_gain_part,
        grads,
    )
    ends = finish(late, thin, whole, downs)
    return (output[None], token_grad[None], *ends[:7], *(end.reshape(-1) for end in ends[7:]))


def solution(mesh):
    rows = P("fsdp", "ctx", None)
    matrix = P("fsdp", None)
    vector = P("fsdp")
    placed = (rows, P()) + (matrix,) * 7 + (vector,) * 5 + (rows,)
    return jax.shard_map(
        body,
        mesh=mesh,
        in_specs=placed,
        out_specs=(rows, rows) + (matrix,) * 7 + (vector,) * 5,
        check_vma=False,
    )
```

```python
import math

import jax
import jax.numpy as jnp
import numpy as np
from jax import lax
from jax.experimental import pallas as pl
from jax.experimental.pallas import tpu as pltpu
from jax.sharding import PartitionSpec as P

H = 14
KVH = 2
GROUP = H // KVH
HD = 64
ROWS = 192
BLK = 96
LANES = 1408
SLAB = 1536
SLABS = 4
OWN = 256

EPSILON = 1e-06
THETA = 1000000.0
MASKED = -1e30

BF = jnp.bfloat16
F32 = jnp.float32
VMEM = pl.BlockSpec(memory_space=pltpu.VMEM)
NT = (((1,), (1,)), ((), ()))
TN = (((0,), (0,)), ((), ()))


def dot(left, right):
    return jnp.dot(left, right, preferred_element_type=F32)


def dot_nt(left, right):
    return lax.dot_general(left, right, NT, preferred_element_type=F32)


def dot_tn(left, right):
    return lax.dot_general(left, right, TN, preferred_element_type=F32)


def thirds(value):
    high = value.astype(BF).astype(F32)
    rest = value - high
    middle = rest.astype(BF).astype(F32)
    low = (rest - middle).astype(BF).astype(F32)
    return high, middle, low


MESH = pl.DeviceIdType.MESH
ANY = pl.BlockSpec(memory_space=pl.ANY)
WINDOW = 1280
UNITS = 1216
SHARD = 224
WIDTH = 896
MIB = 2**20


def place():
    ctx, f = lax.axis_index("ctx"), lax.axis_index("fsdp")
    return lax.div(ctx, 16), lax.rem(lax.div(ctx, 4), 4), lax.rem(ctx, 4), lax.div(f, 2), lax.rem(f, 2)


def at(yl, x, z, yh, c):
    return ((yl * 4 + x) * 4 + z, yh * 2 + c)


def turn(index, by):
    return lax.rem(index + by, 4)


def greet(devices):
    barrier = pltpu.get_barrier_semaphore()
    for device in devices:
        pl.semaphore_signal(barrier, inc=1, device_id=device, device_id_type=MESH)
    pl.semaphore_wait(barrier, len(devices))


class Links:
    def __init__(self, send, recv):
        self.send, self.recv, self.used = send, recv, 0

    def reserve(self, count):
        first = self.used
        self.used += count
        return first

    def copy(self, src, dst, device, slot):
        return pltpu.make_async_remote_copy(
            src_ref=src,
            dst_ref=dst,
            send_sem=self.send.at[slot],
            recv_sem=self.recv.at[slot],
            device_id=device,
            device_id_type=MESH,
        )

    def push(self, src, dst, device):
        copy = self.copy(src, dst, device, self.reserve(1))
        copy.start()
        return copy


class RingSum:
    def __init__(self, links, me, devices, chunk, relay, landing, staged):
        self.links, self.me, self.devices, self.chunk = links, me, devices, chunk
        self.relay, self.landing, self.staged = relay, landing, staged
        self.base = links.reserve(6)

    def copies(self, wanted):
        me, right, left = self.me, self.devices[0], self.devices[2]
        across, after, before = turn(me, 2), turn(me, 1), turn(me, 3)
        chunk, landing, staged = self.chunk, self.landing, self.staged
        moves = (
            (chunk(across, 0), self.relay.at[0], right),
            (chunk(across, 1), self.relay.at[1], left),
            (chunk(after, 1), landing.at[0, 1], right),
            (chunk(before, 0), landing.at[1, 0], left),
            (staged.at[0], landing.at[0, 0], right),
            (staged.at[1], landing.at[1, 1], left),
        )
        return [self.links.copy(*moves[n], self.base + n) for n in wanted]

    def start(self):
        for copy in self.copies((0, 1, 2, 3)):
            copy.start()

    def merge(self):
        for n in range(2):
            came, on = self.copies((n, 4 + n))
            came.wait_recv()
            self.staged[n] = (self.staged[n].astype(F32) + self.relay[n].astype(F32)).astype(BF)
            on.start()

    def finish(self):
        for copy in self.copies((0, 1)):
            copy.wait_send()
        for copy in self.copies((2, 3, 4, 5)):
            copy.wait()

    def arrived(self, half):
        return self.landing[0, half].astype(F32) + self.landing[1, half].astype(F32)


def lanes_below(shape, bound):
    return lax.broadcasted_iota(jnp.int32, shape, 1) < bound


def swap64(value):
    return pltpu.roll(value, 64, axis=1)


def turn_pairs(value, cosine, sine):
    lane = lax.broadcasted_iota(jnp.int32, value.shape, 1)
    other = jnp.where(
        lax.rem(lane, 64) < 32, pltpu.roll(value, 96, axis=1), pltpu.roll(value, 32, axis=1)
    )
    return value * cosine + other * sine


def key_extra(rows):
    count = rows.shape[0]
    return jnp.broadcast_to(rows[:, None, :], (count, BLK, 128)).reshape(count * BLK, 128).astype(BF)


def own_extra():
    lane = lax.broadcasted_iota(jnp.int32, (OWN, 128), 1)
    return jnp.where((lane >= 2) & (lane < 5), 1.0, 0.0).astype(BF)


def window_start(f):
    return pl.multiple_of(lax.div(19 * f, 2) * 128, 128)


def tables(order_ref, token_angle, block_angle, cos_ref, sin_ref, extra_ref, kpos_ref, qpos_ref):
    ctx = lax.axis_index("ctx")
    mine = [order_ref[2 * ctx], order_ref[2 * ctx + 1]]
    lane = lax.broadcasted_iota(jnp.int32, (BLK, 128), 1)
    sign = jnp.where(lax.rem(lane, 64) < 32, -1.0, 1.0)
    for n in range(2):
        rows = slice(n * BLK, (n + 1) * BLK)
        cosine, sine = block_angle[0, pl.ds(mine[n], 1), :], block_angle[1, pl.ds(mine[n], 1), :]
        cos_ref[rows] = token_angle[0] * cosine - token_angle[1] * sine
        sin_ref[rows] = (token_angle[1] * cosine + token_angle[0] * sine) * sign
    lane = lax.broadcasted_iota(jnp.int32, (1, 128), 1)
    ones = jnp.where((lane >= 2) & (lane < 5), 1.0, 0.0)
    for slot in range(64):
        block = order_ref[slot]
        other = slot // 2 != ctx
        row = ones
        for n in range(2):
            shown = jnp.where((block < mine[n]) & other, 0.0, MASKED)
            row = jnp.where(lane == n, shown, row)
        yl, x, z, n = slot // 32, slot // 8 % 4, slot // 2 % 4, slot % 2
        for g, spot in enumerate((((x * 4 + z) * 2 + yl) * 2 + n, ((z * 4 + x) * 2 + yl) * 2 + n)):
            extra_ref[g, spot : spot + 1, :] = row

    def position(index):
        block = jnp.where(index < BLK, mine[0], mine[1])
        return (block * BLK + lax.rem(index, BLK)).astype(F32)

    row = lax.broadcasted_iota(jnp.int32, (OWN, 128), 0)
    kpos_ref[...] = jnp.where(row < ROWS, position(row), 1e9)
    lane = lax.broadcasted_iota(jnp.int32, (8, LANES), 1)
    qpos_ref[...] = jnp.where(lane < GROUP * ROWS, position(lax.rem(lane, ROWS)), 5e8)


def angle_tables():
    lane = np.arange(128) % 32
    frequency = np.exp(lane * (-2.0 * math.log(THETA) / HD))
    token = np.arange(BLK)[:, None] * frequency
    block = np.arange(64)[:, None] * BLK * frequency
    return [np.stack([np.cos(a), np.sin(a)]).astype(np.float32) for a in (token, block)]


def front_kernel(
    tokens_ref,
    wq_ref,
    wk_ref,
    wv_ref,
    qb_ref,
    ag_ref,
    hg_ref,
    kb_ref,
    vb_ref,
    order_ref,
    token_angle_ref,
    block_angle_ref,
    wo_ref,
    gate_ref,
    up_ref,
    cot_ref,
    attended_ref,
    ot_ref,
    lse_ref,
    q_ref,
    kv_ref,
    normed_ref,
    wq_all,
    wk_all,
    wv_all,
    small_all,
    cos_ref,
    sin_ref,
    extra_ref,
    kpos_ref,
    qpos_ref,
    wo_all,
    gate_all,
    up_all,
    cot_all,
    own,
    acc,
    top,
    natural,
    send,
    recv,
    local,
):
    yl, x, z, yh, c = place()
    f = yh * 2 + c
    f_cross = (1 - yh) * 2 + c
    f_sib = yh * 2 + 1 - c
    f_far = (1 - yh) * 2 + 1 - c
    sib = at(yl, x, z, yh, 1 - c)
    cross = at(1 - yl, x, z, 1 - yh, c)
    far = at(1 - yl, x, z, 1 - yh, 1 - c)
    mate = at(1 - yl, x, z, yh, c)
    on_x = [at(yl, turn(x, d), z, yh, c) for d in (1, 2, 3)]
    on_z = [at(yl, x, turn(z, d), yh, c) for d in (1, 2, 3)]
    links = Links(send, recv)
    greet([sib, cross, far, mate] + on_x + on_z)

    def gather_start(pairs):
        return [
            (links.push(mine, whole.at[f], sib), links.push(mine, whole.at[f], cross), whole)
            for mine, whole in pairs
        ]

    def gather_relay(started):
        relays = []
        for _, over, whole in started:
            over.wait_recv()
            relays.append(links.push(whole.at[f_cross], whole.at[f_cross], sib))
        return relays

    def gather_end(started, relays):
        for beside, over, _ in started:
            beside.wait()
            over.wait_send()
        for relay in relays:
            relay.wait()

    first = gather_start([(wq_ref, wq_all), (wk_ref, wk_all), (wv_ref, wv_all)])
    small_all[f] = jnp.zeros((8, 256), F32)
    for row, (ref, count) in enumerate(
        ((qb_ref, SHARD), (ag_ref, SHARD), (hg_ref, SHARD), (kb_ref, 32), (vb_ref, 32))
    ):
        small_all[f, row : row + 1, 0:count] = ref[...].astype(F32).reshape(1, count)
    first += gather_start([(small_all.at[f], small_all)])
    keep = [
        pltpu.make_async_copy(mine, whole.at[f], local.at[n])
        for n, (mine, whole) in enumerate(((wo_ref, wo_all), (cot_ref, cot_all)))
    ]
    for copy in keep:
        copy.start()
    tables(
        order_ref, token_angle_ref, block_angle_ref, cos_ref, sin_ref, extra_ref, kpos_ref, qpos_ref
    )
    wq_all[f] = wq_ref[...]
    wk_all[f] = wk_ref[...]
    wv_all[f] = wv_ref[...]
    inputs = tokens_ref[...].astype(F32)
    scale = lax.rsqrt(jnp.mean(inputs * inputs, axis=-1, keepdims=True) + EPSILON)
    relays = gather_relay(first)
    def quarter(n, start):
        rows = pl.ds(pl.multiple_of(lax.div(n, 2) * 112, 16), 112)
        return rows, pl.ds(pl.multiple_of(start + lax.rem(n, 2) * 640, 128), 640)

    spread = []
    for ref, whole, n in ((gate_ref, gate_all, x), (up_ref, up_all, z)):
        rows, lanes = quarter(n, 0)
        for device, index in ((cross, f_cross), (far, f_far)):
            part = ref.at[quarter(n, window_start(index))]
            spread.append(links.push(part, whole.at[f, rows, lanes], device))
    for ref, whole in ((gate_ref, gate_all), (up_ref, up_all)):
        part = ref.at[:, pl.ds(window_start(f_sib), WINDOW)]
        spread.append(links.push(part, whole.at[f], sib))
    gather_end(first, relays)

    def vector(row, count):
        return jnp.concatenate([small_all[n, row : row + 1, 0:count] for n in range(4)], axis=1)

    normed = (inputs * scale * vector(1, SHARD)).astype(BF)
    normed_ref[...] = normed
    cosine, sine = cos_ref[...], sin_ref[...]
    low = lanes_below((ROWS, 128), 64)

    queries = dot(normed, wq_all[...].reshape(WIDTH, WIDTH)) + vector(0, SHARD)
    keys = dot(normed, wk_all[...].reshape(WIDTH, 128)) + vector(3, 32)
    values = dot(normed, wv_all[...].reshape(WIDTH, 128)) + vector(4, 32)
    keys = turn_pairs(keys, cosine, sine).astype(BF).astype(F32)
    values = values.astype(BF).astype(F32)
    own[...] = jnp.zeros(own.shape, BF)
    own[0, 0:ROWS] = jnp.where(low, keys, swap64(values)).astype(BF)
    own[1, 0:ROWS] = jnp.where(low, swap64(keys), values).astype(BF)

    slab_of = (x, z)
    spot = [
        pl.ds(pl.multiple_of((z * 2 + yl) * ROWS, ROWS), ROWS),
        pl.ds(pl.multiple_of((x * 2 + yl) * ROWS, ROWS), ROWS),
    ]
    pair = [
        pl.ds(pl.multiple_of(z * 2 * ROWS, 2 * ROWS), 2 * ROWS),
        pl.ds(pl.multiple_of(x * 2 * ROWS, 2 * ROWS), 2 * ROWS),
    ]
    mates = [
        links.push(own.at[g, 0:ROWS], kv_ref.at[g, slab_of[g], spot[g]], mate) for g in range(KVH)
    ]
    for g in range(KVH):
        kv_ref[g, slab_of[g], spot[g], :] = own[g, 0:ROWS]

    for tile in range(H // 2):
        part = turn_pairs(queries[:, tile * 128 : tile * 128 + 128], cosine, sine)
        part = part.astype(BF).astype(F32) * (1.0 / math.sqrt(HD))
        for half in range(2):
            head = tile * 2 + half
            j = head % GROUP
            mine = part if half == 0 else swap64(part)
            q_ref[head // GROUP, j * ROWS : (j + 1) * ROWS, 0:128] = jnp.where(
                low, mine, 0.0
            ).astype(BF)
    row = lax.broadcasted_iota(jnp.int32, (LANES, 128), 0)
    lane = lax.broadcasted_iota(jnp.int32, (LANES, 128), 1)
    block = lax.rem(lax.div(row, BLK), 2)
    hot = jnp.where((block == lane) & (row < GROUP * ROWS), 1.0, 0.0).astype(BF)
    for g in range(KVH):
        q_ref[g, :, 128:256] = hot
        q_ref[g, GROUP * ROWS :, 0:128] = jnp.zeros((LANES - GROUP * ROWS, 128), BF)

    def mix(g, keys, scores):
        old = top[g, 0:1]
        new = jnp.maximum(old, jnp.max(scores, axis=0, keepdims=True))
        weights = jnp.exp(scores - new).astype(BF)
        acc[g] = acc[g] * jnp.exp(old - new) + dot(keys.T[64:136], weights)
        top[g, 0:1] = new

    top[...] = jnp.full(top.shape, MASKED, F32)
    acc[...] = jnp.zeros(acc.shape, F32)
    for copy in mates:
        copy.wait()
    pairs = [
        links.push(kv_ref.at[0, x, pair[0]], kv_ref.at[0, x, pair[0]], device) for device in on_z
    ] + [links.push(kv_ref.at[1, z, pair[1]], kv_ref.at[1, z, pair[1]], device) for device in on_x]
    mask = jnp.where(kpos_ref[:, 0:1] <= qpos_ref[0:1], 0.0, MASKED)
    for g in range(KVH):
        keys = jnp.concatenate([own[g], own_extra()], axis=1)
        mix(g, keys, dot_nt(keys, q_ref[g]) + mask)
    for copy in pairs:
        copy.wait()
    base = links.reserve(6)

    def slab_copy(g, d, slab):
        device = (
            ((yl * 4 + jnp.where(g == 0, turn(x, d), x)) * 4 + jnp.where(g == 0, z, turn(z, d))),
            f,
        )
        return links.copy(kv_ref.at[g, slab], kv_ref.at[g, slab], device, base + g * 3 + d - 1)

    for d in (1, 3):
        for g in range(KVH):
            slab_copy(g, d, slab_of[g]).start()
    again = links.reserve(12)

    def quarters():
        copies = []
        for whole, n, devices in ((gate_all, x, on_x), (up_all, z, on_z)):
            rows, lanes = quarter(n, 0)
            for index in (f_cross, f_far):
                part = whole.at[index, rows, lanes]
                copies += [
                    links.copy(part, part, device, again + len(copies) + m)
                    for m, device in enumerate(devices)
                ]
        return copies

    second = links.reserve(4)

    def outer():
        copies = []
        for mine, whole in ((wo_ref, wo_all), (cot_ref, cot_all)):
            for device in (sib, cross):
                copies.append(links.copy(mine, whole.at[f], device, second + len(copies)))
        return copies

    def slabs_on():
        for g in range(KVH):
            slab_copy(g, 2, slab_of[g]).start()

    def spread_on():
        for copy in spread[0:4]:
            copy.wait_recv()
        for copy in quarters() + outer():
            copy.start()

    def step(i, _):
        g, n = lax.rem(i, 2), lax.div(i, 2)
        d = jnp.where(n == 2, 3, jnp.where(n == 3, 2, n))
        slab = turn(jnp.where(g == 0, x, z), d)

        @pl.when(n > 0)
        def _():
            slab_copy(g, 4 - d, slab).wait_recv()

        rows = extra_ref[g, pl.ds(pl.multiple_of(slab * 16, 16), 16), :]
        keys = jnp.concatenate([kv_ref[g, slab], key_extra(rows)], axis=1)
        mix(g, keys, dot_nt(keys, q_ref[g]))
        pl.when(i == 1)(slabs_on)
        pl.when(i == 3)(spread_on)
        return 0

    lax.fori_loop(0, 8, step, 0)
    for d in (1, 2, 3):
        for g in range(KVH):
            slab_copy(g, d, slab_of[g]).wait_send()
    outers = outer()
    second = list(zip(outers[0::2], outers[1::2], (wo_all, cot_all)))
    relays = gather_relay(second)

    for g in range(KVH):
        total = acc[g, 66:67]
        out = acc[g, 0:64] / total
        ot_ref[g] = out
        lse_ref[g] = jnp.broadcast_to(top[g, 0:1] + jnp.log(total), (8, LANES))
        natural[g] = jnp.concatenate([out, jnp.zeros((64, LANES), F32)], axis=0).T
    for tile in range(H // 2):
        even, odd = tile * 2, tile * 2 + 1
        left = natural[even // GROUP, (even % GROUP) * ROWS : (even % GROUP + 1) * ROWS]
        right = natural[odd // GROUP, (odd % GROUP) * ROWS : (odd % GROUP + 1) * ROWS]
        attended_ref[:, tile * 128 : tile * 128 + 128] = jnp.where(
            low, left, swap64(right)
        ).astype(BF)
    for copy in spread[0:4]:
        copy.wait_send()
    for copy in spread[4:] + quarters():
        copy.wait()
    gather_end(second, relays)
    for copy in keep:
        copy.wait()


def front(*operands):
    shape = jax.ShapeDtypeStruct
    scalars = pl.BlockSpec(memory_space=pltpu.SMEM)
    return pl.pallas_call(
        front_kernel,
        out_shape=[
            shape((ROWS, WIDTH), BF),
            shape((KVH, HD, LANES), F32),
            shape((KVH, 8, LANES), F32),
            shape((KVH, LANES, 256), BF),
            shape((KVH, SLABS, SLAB, 128), BF),
            shape((ROWS, WIDTH), BF),
            shape((4, SHARD, WIDTH), BF),
            shape((4, SHARD, 128), BF),
            shape((4, SHARD, 128), BF),
            shape((4, 8, 256), F32),
            shape((ROWS, 128), F32),
            shape((ROWS, 128), F32),
            shape((KVH, 64, 128), F32),
            shape((OWN, 128), F32),
            shape((8, LANES), F32),
            shape((4, SHARD, WIDTH), BF),
            shape((4, SHARD, WINDOW), BF),
            shape((4, SHARD, WINDOW), BF),
            shape((4, ROWS, WIDTH), BF),
        ],
        in_specs=[VMEM] * 9 + [scalars] + [VMEM] * 2 + [ANY] * 4,
        out_specs=[VMEM] * 15 + [ANY] * 4,
        scratch_shapes=[
            pltpu.VMEM((KVH, OWN, 128), BF),
            pltpu.VMEM((KVH, 72, LANES), F32),
            pltpu.VMEM((KVH, 8, LANES), F32),
            pltpu.VMEM((KVH, LANES, 128), F32),
            pltpu.SemaphoreType.DMA((64,)),
            pltpu.SemaphoreType.DMA((64,)),
            pltpu.SemaphoreType.DMA((4,)),
        ],
        compiler_params=pltpu.CompilerParams(
            vmem_limit_bytes=58 * MIB, collective_id=0, has_side_effects=True
        ),
        name="front",
    )(*operands)


def tile_stores(ref, value, first_row, first_lane, place_of):
    for r in range(value.shape[0] // 16):
        for n in range(value.shape[1] // 128):
            p, k = place_of(first_row + r, first_lane + n)
            ref[p // 4, p % 4, k] = value[r * 16 : r * 16 + 16, n * 128 : n * 128 + 128]


def gate_place(r, n):
    t = (r % 14) * 20 + n
    return t // 18, 18 * (r // 14) + t % 18


def down_place(r, n):
    t = r * 7 + n
    return t // 34, t % 34


def middle_kernel(
    attended_ref,
    tokens_ref,
    small_all,
    wo_all,
    cot_all,
    gate_hbm,
    up_hbm,
    gate_own,
    up_own,
    down_hbm,
    output_ref,
    grad_middle_ref,
    grad_attn_ref,
    gain_ref,
    do_ref,
    grads_ref,
    sum_a_ref,
    sum_b_ref,
    gate_ref,
    up_ref,
    down_ref,
    blocks,
    back_gate,
    hidden_ref,
    down_grad,
    two,
    two_in,
    out,
    out_in,
    downs,
    relay,
    landing,
    staged,
    send,
    recv,
    local,
):
    yl, x, z, yh, c = place()
    f = yh * 2 + c
    f_cross = (1 - yh) * 2 + c
    f_sib = yh * 2 + 1 - c
    f_far = (1 - yh) * 2 + 1 - c
    sib = at(yl, x, z, yh, 1 - c)
    cross = at(1 - yl, x, z, 1 - yh, c)
    links = Links(send, recv)
    window = pl.ds(window_start(f), WINDOW)
    loads = [
        pltpu.make_async_copy(
            down_hbm, down_ref.at[pl.ds(pl.multiple_of(64 * c, 64), UNITS)], local.at[0]
        ),
        pltpu.make_async_copy(gate_own.at[:, window], gate_ref.at[f], local.at[1]),
        pltpu.make_async_copy(up_own.at[:, window], up_ref.at[f], local.at[2]),
    ]
    for n, index in enumerate((f_sib, f_cross, f_far)):
        loads += [
            pltpu.make_async_copy(gate_hbm.at[index], gate_ref.at[index], local.at[3 + 2 * n]),
            pltpu.make_async_copy(up_hbm.at[index], up_ref.at[index], local.at[4 + 2 * n]),
        ]
    for copy in loads:
        copy.start()
    down_ref[pl.ds(pl.multiple_of((1 - c) * UNITS, 64), 64), :] = jnp.zeros((64, WIDTH), BF)
    on_x = [at(yl, turn(x, d), z, yh, c) for d in (1, 2, 3)]
    on_z = [at(yl, x, turn(z, d), yh, c) for d in (1, 2, 3)]
    greet([sib, cross, on_x[0], on_x[2], on_z[0], on_z[2]])
    rings = (
        RingSum(
            links,
            x,
            on_x,
            lambda n, half: downs.at[n, 2 * half : 2 * half + 2, 0:17],
            relay.at[0],
            landing.at[0],
            staged.at[0],
        ),
        RingSum(
            links,
            z,
            on_z,
            lambda n, half: downs.at[2 * half : 2 * half + 2, n, 17:34],
            relay.at[1],
            landing.at[1],
            staged.at[1],
        ),
    )

    gain = jnp.concatenate([small_all[n, 2:3, 0:SHARD] for n in range(4)], axis=1)
    wo = wo_all[...].reshape(WIDTH, WIDTH)
    middle = tokens_ref[...].astype(F32) + dot(attended_ref[...], wo)
    scale = lax.rsqrt(jnp.mean(middle * middle, axis=-1, keepdims=True) + EPSILON)
    grad_middle_ref[...] = middle
    blocks[0] = (middle * scale * gain).astype(BF)
    beside = links.push(blocks.at[0], blocks.at[1], sib)
    over = links.push(blocks.at[0], blocks.at[2], cross)
    order = ((f, f_sib), (f_cross, f_far))
    for copy in loads:
        copy.wait()

    def grads_of(p):
        return jnp.concatenate([cot_all[order[p][0]], cot_all[order[p][1]]], axis=0)

    def hidden_grad(p):
        return dot_nt(grads_of(p), down_ref[...])

    def units(p, grad_hidden):
        rows = slice(p * 2 * ROWS, (p + 1) * 2 * ROWS)
        block = blocks[2 * p : 2 * p + 2].reshape(2 * ROWS, WIDTH)
        gate_pre = dot(block, gate_ref[...].reshape(WIDTH, WINDOW))
        upward = dot(block, up_ref[...].reshape(WIDTH, WINDOW))
        sigmoid = 1.0 / (1.0 + jnp.exp(-gate_pre))
        swish = gate_pre * sigmoid
        hidden_ref[rows] = (swish * upward).astype(BF)
        back_gate[rows, 0:WINDOW] = (
            grad_hidden * upward * sigmoid * (1.0 + gate_pre * (1.0 - sigmoid))
        ).astype(BF)
        back_gate[rows, WINDOW:] = (grad_hidden * swish).astype(BF)

    def two_part(p):
        rows = slice(p * 2 * ROWS, (p + 1) * 2 * ROWS)
        return dot_nt(back_gate[rows, 0:WINDOW], gate_ref[...].reshape(WIDTH, WINDOW)) + dot_nt(
            back_gate[rows, WINDOW:], up_ref[...].reshape(WIDTH, WINDOW)
        )

    def out_part(p):
        rows = slice(p * 2 * ROWS, (p + 1) * 2 * ROWS)
        return dot(hidden_ref[rows], down_ref[...])

    beside.wait()
    units(0, hidden_grad(0))
    part = two_part(0)
    two_mine = part[0:ROWS]
    two[0] = part[ROWS:].astype(BF)
    two_copies = [links.push(two.at[0], two_in.at[0], sib)]
    far_grad = hidden_grad(1)
    over.wait()
    relay = links.push(blocks.at[2], blocks.at[3], sib)
    relay.wait()
    units(1, far_grad)
    part = two_part(1)
    two[1] = part[ROWS:].astype(BF)
    copy = links.push(two.at[1], two_in.at[1], sib)
    two_cross = part[0:ROWS]
    part = out_part(1)
    out[1] = part[ROWS:].astype(BF)
    copy.wait()
    two[2] = (two_cross + two_in[1].astype(F32)).astype(BF)
    two_copies.append(links.push(two.at[2], two_in.at[2], cross))
    copy = links.push(out.at[1], out_in.at[1], sib)
    out_cross = part[0:ROWS]
    part = out_part(0)
    out_mine = part[0:ROWS]
    out[0] = part[ROWS:].astype(BF)
    out_copies = [links.push(out.at[0], out_in.at[0], sib)]
    copy.wait()
    out[2] = (out_cross + out_in[1].astype(F32)).astype(BF)
    out_copies.append(links.push(out.at[2], out_in.at[2], cross))

    down_grad[...] = dot_tn(
        hidden_ref[...], jnp.concatenate([grads_of(0), grads_of(1)], axis=0)
    ).astype(BF)
    blank = jnp.zeros((16, 128), BF)
    product = down_grad[pl.ds(pl.multiple_of(64 * c, 64), UNITS), :]
    tile_stores(downs, product, 0, 0, down_place)
    for t in range(532, 544):
        downs[3, 3, t % 34] = blank
    for ring in rings:
        ring.start()
    staged[0, 0] = downs[turn(x, 1), 0:2, 0:17]
    staged[0, 1] = downs[turn(x, 3), 2:4, 0:17]
    staged[1, 0] = downs[0:2, turn(z, 1), 17:34]
    staged[1, 1] = downs[2:4, turn(z, 3), 17:34]
    block = blocks[...].reshape(4 * ROWS, WIDTH)
    for n in range(0, 2 * WINDOW, 512):
        product = dot_tn(block, back_gate[:, n : n + 512]).astype(BF)
        tile_stores(grads_ref, product, 0, n // 128, gate_place)
        if n == 1536:
            for ring in rings:
                ring.merge()
    for n in range(4):
        for t in range(280, 288):
            grads_ref[3, 3, 18 * n + t % 18] = blank

    for copy in two_copies:
        copy.wait()
    grad_two = two_mine + two_in[0].astype(F32) + two_in[2].astype(F32)
    middle = grad_middle_ref[...]
    scale = lax.rsqrt(jnp.mean(middle * middle, axis=-1, keepdims=True) + EPSILON)
    weighted = grad_two * gain
    grad_middle = (
        cot_all[f].astype(F32)
        + scale * weighted
        - middle * (scale * scale * scale) * jnp.mean(weighted * middle, axis=-1, keepdims=True)
    )
    gain_ref[...] = jnp.broadcast_to(
        jnp.sum(grad_two * middle * scale, axis=0, keepdims=True), (8, WIDTH)
    )
    grad_attn = grad_middle.astype(BF)
    grad_attn_ref[...] = grad_attn
    grad_middle_ref[...] = grad_middle
    grad_attended = dot_nt(grad_attn, wo_all[...].reshape(WIDTH, WIDTH)).astype(BF).astype(F32)
    low = lanes_below((ROWS, 128), 64)
    for tile in range(H // 2):
        part = grad_attended[:, tile * 128 : tile * 128 + 128]
        for half in range(2):
            head = tile * 2 + half
            j = head % GROUP
            mine = swap64(part) if half == 0 else part
            do_ref[head // GROUP, j * ROWS : (j + 1) * ROWS] = jnp.where(low, 0.0, mine).astype(BF)
    for g in range(KVH):
        do_ref[g, GROUP * ROWS :] = jnp.zeros((LANES - GROUP * ROWS, 128), BF)
    for copy in out_copies:
        copy.wait()
    total = out_mine + out_in[0].astype(F32) + out_in[2].astype(F32)
    output_ref[...] = (middle + total).astype(BF)
    for ring in rings:
        ring.finish()
    for half in range(2):
        two_of = slice(2 * half, 2 * half + 2)
        sum_a_ref[two_of] = (downs[x, two_of, 0:17].astype(F32) + rings[0].arrived(half)).astype(BF)
        sum_b_ref[two_of] = (downs[two_of, z, 17:34].astype(F32) + rings[1].arrived(half)).astype(BF)


def middle_call(*operands):
    shape = jax.ShapeDtypeStruct
    return pl.pallas_call(
        middle_kernel,
        out_shape=[
            shape((ROWS, WIDTH), BF),
            shape((ROWS, WIDTH), F32),
            shape((ROWS, WIDTH), BF),
            shape((8, WIDTH), F32),
            shape((KVH, LANES, 128), BF),
            shape((4, 4, 72, 16, 128), BF),
            shape((4, 17, 16, 128), BF),
            shape((4, 17, 16, 128), BF),
        ],
        in_specs=[VMEM] * 5 + [ANY] * 5,
        out_specs=[VMEM] * 8,
        scratch_shapes=[
            pltpu.VMEM((4, SHARD, WINDOW), BF),
            pltpu.VMEM((4, SHARD, WINDOW), BF),
            pltpu.VMEM((WINDOW, WIDTH), BF),
            pltpu.VMEM((4, ROWS, WIDTH), BF),
            pltpu.VMEM((4 * ROWS, 2 * WINDOW), BF),
            pltpu.VMEM((4 * ROWS, WINDOW), BF),
            pltpu.VMEM((WINDOW, WIDTH), BF),
            pltpu.VMEM((3, ROWS, WIDTH), BF),
            pltpu.VMEM((3, ROWS, WIDTH), BF),
            pltpu.VMEM((3, ROWS, WIDTH), BF),
            pltpu.VMEM((3, ROWS, WIDTH), BF),
            pltpu.VMEM((4, 4, 34, 16, 128), BF),
            pltpu.VMEM((2, 2, 2, 17, 16, 128), BF),
            pltpu.VMEM((2, 2, 2, 2, 17, 16, 128), BF),
            pltpu.VMEM((2, 2, 2, 17, 16, 128), BF),
            pltpu.SemaphoreType.DMA((24,)),
            pltpu.SemaphoreType.DMA((24,)),
            pltpu.SemaphoreType.DMA((9,)),
        ],
        compiler_params=pltpu.CompilerParams(
            vmem_limit_bytes=60 * MIB, collective_id=3, has_side_effects=True
        ),
        name="middle",
    )(*operands)


UNIT = 72
HALF = 36
DOWN = 17
CHUNK = 768


def widen(ref, index):
    return ref[index].astype(F32)


def back_kernel(
    q_ref,
    do_ref,
    ot_ref,
    lse_ref,
    kv_ref,
    extra_ref,
    kpos_ref,
    qpos_ref,
    down_a_ref,
    down_b_ref,
    cos_ref,
    sin_ref,
    normed_ref,
    attended_ref,
    grad_attn_ref,
    grad_middle_ref,
    tokens_ref,
    wq_all,
    wk_all,
    wv_all,
    small_all,
    hidden_gain_ref,
    grads_ref,
    token_grad_ref,
    late_ref,
    thin_ref,
    whole_ref,
    downs_ref,
    dq_ref,
    dkv_ref,
    sum_ref,
    qx,
    dox,
    own,
    own_grad,
    parts,
    parts_in,
    pairs,
    pairs_in,
    across,
    side_a,
    side_b,
    relay,
    landing,
    staged,
    late_a,
    late_b,
    whole,
    whole_in,
    down_late,
    down_whole,
    down_in,
    natural,
    table,
    table_in,
    lines,
    lines_in,
    cols,
    cols_in,
    ends,
    ends_in,
    thin,
    send,
    recv,
    local,
):
    yl, x, z, yh, c = place()
    f = yh * 2 + c
    f_cross = (1 - yh) * 2 + c
    f_sib = yh * 2 + 1 - c
    f_far = (1 - yh) * 2 + 1 - c
    sib = at(yl, x, z, yh, 1 - c)
    cross = at(1 - yl, x, z, 1 - yh, c)
    far = at(1 - yl, x, z, 1 - yh, 1 - c)
    mate = at(1 - yl, x, z, yh, c)
    on_x = [at(yl, turn(x, d), z, yh, c) for d in (1, 2, 3)]
    on_z = [at(yl, x, turn(z, d), yh, c) for d in (1, 2, 3)]
    links = Links(send, recv)
    greet([sib, cross, far, mate] + on_x + on_z)

    rings = (
        RingSum(
            links,
            x,
            on_x,
            lambda n, half: grads_ref.at[n, 2 * half : 2 * half + 2, 0:HALF],
            relay.at[0],
            landing.at[0],
            staged.at[0],
        ),
        RingSum(
            links,
            z,
            on_z,
            lambda n, half: grads_ref.at[2 * half : 2 * half + 2, n, HALF:UNIT],
            relay.at[1],
            landing.at[1],
            staged.at[1],
        ),
    )
    def keep():
        moves = (
            (grads_ref.at[turn(x, 1), 0:2, 0:HALF], staged.at[0, 0]),
            (grads_ref.at[turn(x, 3), 2:4, 0:HALF], staged.at[0, 1]),
            (grads_ref.at[0:2, turn(z, 1), HALF:UNIT], staged.at[1, 0]),
            (grads_ref.at[2:4, turn(z, 3), HALF:UNIT], staged.at[1, 1]),
            (grads_ref.at[x, :, 0:HALF], side_a),
            (grads_ref.at[:, z, HALF:UNIT], side_b),
        )
        return [pltpu.make_async_copy(*move, local.at[n]) for n, move in enumerate(moves)]

    for copy in keep():
        copy.start()

    down_second, down_third, down_fourth, down_fifth, down_sixth = (
        links.reserve(6),
        links.reserve(1),
        links.reserve(6),
        links.reserve(4),
        links.reserve(4),
    )

    def down_copies():
        copies = []
        for n in range(3):
            for source, half, index, device in (
                (down_a_ref, 0, turn(z, n + 1), on_z[n]),
                (down_b_ref, 1, turn(x, n + 1), on_x[n]),
            ):
                copies.append(
                    links.copy(
                        source.at[index],
                        down_late.at[half, n],
                        device,
                        down_second + len(copies),
                    )
                )
        return copies

    def down_mate():
        return links.copy(down_whole, down_in, mate, down_third)

    def down_third_start():
        for copy in down_copies():
            copy.wait()
        for half, own_part in ((0, down_a_ref[z]), (1, down_b_ref[x])):
            total = own_part.astype(F32)
            for m in range(3):
                total = total + down_late[half, m].astype(F32)
            down_whole[half] = total.astype(BF)
        down_mate().start()

    def down_spread():
        copies = []
        for n in range(3):
            for half, device in ((0, on_z[n]), (1, on_x[n])):
                part = downs_ref.at[half, x, z]
                copies.append(links.copy(part, part, device, down_fourth + len(copies)))
        return copies

    def down_spread_start():
        down_mate().wait()
        downs_ref[:, x, z] = (
            down_whole[...].astype(F32) + down_in[...].astype(F32)
        ).astype(BF)
        for copy in down_spread():
            copy.start()

    def down_rounds():
        copies = []
        for n in (0, 2):
            for part, device in (
                (downs_ref.at[0, x], on_x[n]),
                (downs_ref.at[1, :, z], on_z[n]),
            ):
                copies.append(links.copy(part, part, device, down_fifth + len(copies)))
        return copies

    def down_rounds_start():
        for copy in down_spread():
            copy.wait()
        for copy in down_rounds():
            copy.start()

    def down_last():
        copies = []
        for half, came, n in ((0, 3, 0), (1, 1, 2)):
            rows = slice(2 * half, 2 * half + 2)
            for part, device in (
                (downs_ref.at[0, turn(x, came), rows], on_x[n]),
                (downs_ref.at[1, rows, turn(z, came)], on_z[n]),
            ):
                copies.append(links.copy(part, part, device, down_sixth + len(copies)))
        return copies

    def down_last_start():
        for copy in down_rounds():
            copy.wait()
        for copy in down_last():
            copy.start()


    for copy in down_copies():
        copy.start()
    for ring in rings:
        ring.start()

    row = lax.broadcasted_iota(jnp.int32, (128, LANES), 0)
    for g in range(KVH):
        lse = thirds(lse_ref[g, 0:1])
        inner = jnp.sum(do_ref[g].astype(F32).T[64:128] * ot_ref[g], axis=0, keepdims=True)
        inner = thirds(inner)
        extra_q = jnp.zeros((128, LANES), F32)
        extra_d = jnp.zeros((128, LANES), F32)
        for n in range(3):
            extra_q = jnp.where(row == 2 + n, -lse[n], extra_q)
            extra_d = jnp.where(row == 2 + n, -inner[n], extra_d)
        qx[g, :, 0:128] = q_ref[g, :, 0:128]
        qx[g, :, 128:256] = (q_ref[g, :, 128:256].astype(F32) + extra_q.T).astype(BF)
        dox[g, :, 0:128] = do_ref[g]
        dox[g, :, 128:256] = extra_d.T.astype(BF)

    def piece(g, keys, mask):
        scores = dot_nt(keys, qx[g])
        if mask is not None:
            scores = scores + mask
        probs = jnp.exp(scores)
        grad = (probs * dot_nt(keys, dox[g])).astype(BF)
        both = dot(grad, qx[g, :, 0:128]) + dot(probs.astype(BF), dox[g, :, 0:128])
        return both, dot(keys[:, 0:128].T[0:64], grad)

    mask = jnp.where(kpos_ref[:, 0:1] <= qpos_ref[0:1], 0.0, MASKED)
    spots = (
        pl.ds(pl.multiple_of((z * 2 + yl) * ROWS, ROWS), ROWS),
        pl.ds(pl.multiple_of((x * 2 + yl) * ROWS, ROWS), ROWS),
    )
    slab_of = (x, z)
    for g in range(KVH):
        own[...] = jnp.zeros(own.shape, BF)
        own[0:ROWS] = kv_ref[g, slab_of[g], spots[g], :]
        both, dq = piece(g, jnp.concatenate([own[...], own_extra()], axis=1), mask)
        own_grad[g] = both[0:ROWS]
        dq_ref[g] = dq
    count = SLAB // CHUNK
    base = links.reserve(6)

    across_base = links.reserve(16)

    def across_copy(g, d, slab, part):
        rows = pl.ds(2 * part, 2)
        return links.copy(
            parts.at[g, slab, rows, 1 - yl],
            across.at[g, d, rows],
            mate,
            across_base + (g * 4 + d) * 2 + part,
        )

    def part_copy(g, d, slab):
        device = (
            ((yl * 4 + jnp.where(g == 0, slab, x)) * 4 + jnp.where(g == 0, z, slab)),
            f,
        )
        return links.copy(
            across.at[g, d], parts_in.at[g, d - 1], device, base + g * 3 + d - 1
        )

    def combine(g, d, slab):
        for part in range(count):
            across_copy(g, d, slab, part).wait()
        total = parts[g, slab, :, yl].astype(F32) + across[g, d].astype(F32)
        across[g, d] = total.astype(BF)

    def slab_at(n):
        g, d = lax.rem(n, 2), lax.rem(lax.div(n, 2) + 1, 4)
        return g, d, turn(jnp.where(g == 0, x, z), d)

    def step(i, _):
        n, part = lax.div(i, count), lax.rem(i, count)
        g, d, slab = slab_at(n)
        start = pl.multiple_of(part * CHUNK, CHUNK)
        rows = extra_ref[g, pl.ds(pl.multiple_of(slab * 16 + part * 8, 8), 8), :]
        keys = jnp.concatenate([kv_ref[g, slab, pl.ds(start, CHUNK), :], key_extra(rows)], axis=1)
        both, dq = piece(g, keys, None)
        parts[g, slab, pl.ds(2 * part, 2)] = both.astype(BF).reshape(2, 2, ROWS, 128)
        dq_ref[g] += dq

        across_copy(g, d, slab, part).start()

        @pl.when((part == count - 1) & (n > 0))
        def _():
            before = slab_at(n - 1)
            combine(*before)

            @pl.when(n < 7)
            def _():
                part_copy(*before).start()

        for at_step, event in events:
            pl.when(i == at_step)(event)
        return 0

    pair_base, second_base, third_slot = (
        links.reserve(6),
        links.reserve(6),
        links.reserve(1),
    )

    def pair_copies(g):
        other, devices = (z, x)[g], (on_z, on_x)[g]
        return [
            links.copy(
                pairs.at[g, turn(other, n + 1)],
                pairs_in.at[g, n],
                devices[n],
                pair_base + 3 * g + n,
            )
            for n in range(3)
        ]

    def pair_start(g):
        slab = slab_of[g]
        for d in (1, 2, 3):
            part_copy(g, d, turn(slab, d)).wait()
        for n in range(4):
            total = across[g, 0, n].astype(F32)
            for m in range(3):
                total = total + parts_in[g, m, n].astype(F32)
            pairs[g, n] = total.astype(BF)
        for copy in pair_copies(g):
            copy.start()

    def pair_end(g):
        for copy in pair_copies(g):
            copy.wait()
        total = pairs[g, (z, x)[g]].astype(F32) + own_grad[g]
        for m in range(3):
            total = total + pairs_in[g, m].astype(F32)
        dkv_ref[g] = total

    def merge():
        for copy in keep():
            copy.wait()
        for ring in rings:
            ring.merge()

    def second_copies():
        copies = []
        for n in range(3):
            for source, target, index, device in (
                (side_a, late_a, turn(z, n + 1), on_z[n]),
                (side_b, late_b, turn(x, n + 1), on_x[n]),
            ):
                copies.append(
                    links.copy(source.at[index], target.at[n], device, second_base + len(copies))
                )
        return copies

    def second_start():
        for side, ring in zip((side_a, side_b), rings):
            ring.finish()
            for half in range(2):
                rows = slice(2 * half, 2 * half + 2)
                side[rows] = (side[rows].astype(F32) + ring.arrived(half)).astype(BF)
        for copy in second_copies():
            copy.start()

    def third():
        return links.copy(whole, whole_in, mate, third_slot)

    def third_start():
        for copy in second_copies():
            copy.wait()
        a = side_a[z].astype(F32)
        b = side_b[x].astype(F32)
        for m in range(3):
            a = a + late_a[m].astype(F32)
            b = b + late_b[m].astype(F32)
        whole[0:HALF] = a.astype(BF)
        whole[HALF:UNIT] = b.astype(BF)
        third().start()

    events = (
        (1, down_third_start),
        (6, down_spread_start),
        (5, merge),
        (10, second_start),
        (11, down_rounds_start),
        (13, third_start),
        (15, down_last_start),
    )
    lax.fori_loop(0, KVH * SLABS * count, step, 0)
    pair_start(0)

    low = lanes_below((ROWS, 128), 64)
    cosine, sine = cos_ref[...], -sin_ref[...]

    def assemble(tile):
        even, odd = tile * 2, tile * 2 + 1
        left = natural[even // GROUP, (even % GROUP) * ROWS : (even % GROUP + 1) * ROWS]
        right = natural[odd // GROUP, (odd % GROUP) * ROWS : (odd % GROUP + 1) * ROWS]
        return jnp.where(low, left, swap64(right))

    for g in range(KVH):
        natural[g] = jnp.concatenate([dq_ref[g], jnp.zeros((64, LANES), F32)], axis=0).T
    grad_queries = jnp.concatenate(
        [
            turn_pairs(assemble(tile) * (1.0 / math.sqrt(HD)), cosine, sine)
            for tile in range(H // 2)
        ],
        axis=1,
    ).astype(BF)

    combine(1, 0, slab_of[1])
    pair_start(1)

    normed = normed_ref[...]

    def table_columns(first, left, right):
        product = dot_tn(left, right).astype(BF)
        for n in range(right.shape[1] // 128):
            table[first + n] = product[:, n * 128 : n * 128 + 128].reshape(4, SHARD, 128)

    def beside(slot, start, stop):
        return [
            links.copy(
                table.at[start:stop, 2 * n + 1 - c], table_in.at[n, start:stop], sib, slot + n
            )
            for n in range(2)
        ]

    def add_beside(n, _):
        for m in range(2):
            total = table[n, 2 * m + c].astype(F32) + table_in[m, n].astype(F32)
            lines[m, n] = total.astype(BF)
        return 0

    beside_slots = links.reserve(6)
    table_columns(0, normed, grad_queries)
    for copy in beside(beside_slots, 0, 7):
        copy.start()
    table_columns(9, attended_ref[...], grad_attn_ref[...])
    for copy in beside(beside_slots + 2, 9, 16):
        copy.start()
    pair_end(0)

    third().wait()
    sum_ref[...] = (whole[...].astype(F32) + whole_in[...].astype(F32)).astype(BF)

    def spot(index):
        return pl.ds(18 * index, 18)

    shared = [
        links.push(sum_ref.at[spot(index)], whole_ref.at[x, z, spot(f)], device)
        for device, index in ((cross, f_cross), (far, f_far), (sib, f_sib))
    ]
    keep_own = [
        pltpu.make_async_copy(sum_ref.at[spot(f)], whole_ref.at[x, z, spot(f)], local.at[0])
    ]
    for copy in keep_own:
        copy.start()
    for copy in beside(beside_slots, 0, 7) + beside(beside_slots + 2, 9, 16):
        copy.wait()
    lax.fori_loop(0, 7, add_beside, 0)
    lax.fori_loop(9, 16, add_beside, 0)

    pair_end(1)
    grad_keys = turn_pairs(jnp.where(low, dkv_ref[0], swap64(dkv_ref[1])), cosine, sine).astype(BF)
    grad_values = jnp.where(low, swap64(dkv_ref[0]), dkv_ref[1]).astype(BF)
    table_columns(7, normed, grad_keys)
    table_columns(8, normed, grad_values)
    for copy in beside(beside_slots + 4, 7, 9):
        copy.start()

    for copy in keep_own + shared:
        copy.wait()
    spread = []
    for n in range(3):
        spread.append(
            links.push(whole_ref.at[x, z, 0:HALF], whole_ref.at[x, z, 0:HALF], on_z[n])
        )
        spread.append(
            links.push(whole_ref.at[x, z, HALF:UNIT], whole_ref.at[x, z, HALF:UNIT], on_x[n])
        )
    for copy in beside(beside_slots + 4, 7, 9):
        copy.wait()
    lax.fori_loop(7, 9, add_beside, 0)

    along = []
    for n in range(3):
        xt, zt = turn(x, n + 1), turn(z, n + 1)
        along.append(links.push(lines.at[0, pl.ds(xt * 4, 4)], lines_in.at[0, n], on_x[n]))
        for m in range(4):
            along.append(
                links.push(lines.at[1, m * 4 + zt], lines_in.at[1, n, m], on_z[n])
            )

    inputs = tokens_ref[...].astype(F32)
    scale = lax.rsqrt(jnp.mean(inputs * inputs, axis=-1, keepdims=True) + EPSILON)

    def vector(row, count):
        return jnp.concatenate([small_all[n, row : row + 1, 0:count] for n in range(4)], axis=1)

    grad_normed = (
        dot_nt(grad_queries, wq_all[...].reshape(WIDTH, WIDTH))
        + dot_nt(grad_keys, wk_all[...].reshape(WIDTH, 128))
        + dot_nt(grad_values, wv_all[...].reshape(WIDTH, 128))
    )
    weighted = grad_normed * vector(1, SHARD)
    token_grad_ref[...] = (
        grad_middle_ref[...]
        + scale * weighted
        - inputs * (scale * scale * scale) * jnp.mean(weighted * inputs, axis=-1, keepdims=True)
    )
    thin[0, c] = jnp.concatenate(
        [
            jnp.sum(grad_queries.astype(F32), axis=0, keepdims=True),
            jnp.sum(grad_normed * inputs * scale, axis=0, keepdims=True),
            hidden_gain_ref[0:1],
            jnp.concatenate(
                [
                    jnp.sum(grad_keys.astype(F32), axis=0, keepdims=True),
                    jnp.sum(grad_values.astype(F32), axis=0, keepdims=True),
                    jnp.zeros((1, WIDTH - 256), F32),
                ],
                axis=1,
            ),
            jnp.zeros((4, WIDTH), F32),
        ],
        axis=0,
    )

    def thin_push(level, index, device):
        return links.push(thin.at[level, index], thin.at[level, index], device)

    thin_copy = thin_push(0, c, sib)
    thin_copy.wait()
    thin[1, x] = thin[0, 0] + thin[0, 1]
    for n in range(3):
        along.append(thin_push(1, x, on_x[n]))

    for copy in spread:
        copy.wait()
    rounds = []
    for n in (0, 2):
        rounds.append(
            links.push(whole_ref.at[x, :, 0:HALF], whole_ref.at[x, :, 0:HALF], on_x[n])
        )
        rounds.append(
            links.push(whole_ref.at[:, z, HALF:UNIT], whole_ref.at[:, z, HALF:UNIT], on_z[n])
        )
    for copy in along:
        copy.wait()
    for m in range(4):
        a = lines[0, x * 4 + m].astype(F32)
        b = lines[1, m * 4 + z].astype(F32)
        for n in range(3):
            a = a + lines_in[0, n, m].astype(F32)
            b = b + lines_in[1, n, m].astype(F32)
        cols[0, m] = a.astype(BF)
        cols[1, m] = b.astype(BF)
    thin[2, z] = (thin[1, 0] + thin[1, 1]) + (thin[1, 2] + thin[1, 3])
    along = []
    for n in range(3):
        along.append(links.push(cols.at[0, turn(z, n + 1)], cols_in.at[0, n], on_z[n]))
        along.append(links.push(cols.at[1, turn(x, n + 1)], cols_in.at[1, n], on_x[n]))
        along.append(thin_push(2, z, on_z[n]))
    for copy in along:
        copy.wait()
    a = cols[0, z].astype(F32)
    b = cols[1, x].astype(F32)
    for n in range(3):
        a = a + cols_in[0, n].astype(F32)
        b = b + cols_in[1, n].astype(F32)
    ends[0] = a.astype(BF)
    ends[1] = b.astype(BF)
    thin[3, yh] = (thin[2, 0] + thin[2, 1]) + (thin[2, 2] + thin[2, 3])
    along = [links.push(ends.at[1 - yh], ends_in.at[0], cross), thin_push(3, yh, cross)]
    for copy in along:
        copy.wait()
    ends[2] = (ends[yh].astype(F32) + ends_in[0].astype(F32)).astype(BF)
    thin[4, yl] = thin[3, 0] + thin[3, 1]
    along = [links.push(ends.at[2], ends_in.at[1], mate), thin_push(4, yl, mate)]
    for copy in along:
        copy.wait()
    late_ref[x, z] = (ends[2].astype(F32) + ends_in[1].astype(F32)).astype(BF)
    thin_ref[...] = thin[4, 0] + thin[4, 1]

    cut = SHARD // 2
    along = []
    for n in range(3):
        along.append(links.push(late_ref.at[x, z, 0:cut], late_ref.at[x, z, 0:cut], on_z[n]))
        along.append(links.push(late_ref.at[x, z, cut:], late_ref.at[x, z, cut:], on_x[n]))
    for copy in rounds:
        copy.wait()
    rounds = []
    for half, came, n in ((0, 3, 0), (1, 1, 2)):
        rows = slice(2 * half, 2 * half + 2)
        a = whole_ref.at[turn(x, came), rows, 0:HALF]
        b = whole_ref.at[rows, turn(z, came), HALF:UNIT]
        rounds += [links.push(a, a, on_x[n]), links.push(b, b, on_z[n])]
    for copy in along:
        copy.wait()
    along = []
    for n in range(3):
        along.append(links.push(late_ref.at[x, :, 0:cut], late_ref.at[x, :, 0:cut], on_x[n]))
        along.append(links.push(late_ref.at[:, z, cut:], late_ref.at[:, z, cut:], on_z[n]))
    for copy in along + rounds + down_last():
        copy.wait()


def back(*operands):
    shape = jax.ShapeDtypeStruct
    return pl.pallas_call(
        back_kernel,
        out_shape=[
            shape((ROWS, WIDTH), F32),
            shape((4, 4, SHARD, 128), BF),
            shape((8, WIDTH), F32),
            shape((4, 4, UNIT, 16, 128), BF),
            shape((2, 4, 4, DOWN, 16, 128), BF),
        ],
        in_specs=[VMEM] * 22 + [ANY],
        out_specs=[VMEM] * 3 + [ANY, VMEM],
        scratch_shapes=[
            pltpu.VMEM((KVH, HD, LANES), F32),
            pltpu.VMEM((KVH, ROWS, 128), F32),
            pltpu.VMEM((UNIT, 16, 128), BF),
            pltpu.VMEM((KVH, LANES, 256), BF),
            pltpu.VMEM((KVH, LANES, 256), BF),
            pltpu.VMEM((OWN, 128), BF),
            pltpu.VMEM((KVH, ROWS, 128), F32),
            pltpu.VMEM((KVH, SLABS, 4, 2, ROWS, 128), BF),
            pltpu.VMEM((KVH, 3, 4, ROWS, 128), BF),
            pltpu.VMEM((KVH, 4, ROWS, 128), BF),
            pltpu.VMEM((KVH, 3, ROWS, 128), BF),
            pltpu.VMEM((KVH, 4, 4, ROWS, 128), BF),
            pltpu.VMEM((4, HALF, 16, 128), BF),
            pltpu.VMEM((4, HALF, 16, 128), BF),
            pltpu.VMEM((2, 2, 2, HALF, 16, 128), BF),
            pltpu.VMEM((2, 2, 2, 2, HALF, 16, 128), BF),
            pltpu.VMEM((2, 2, 2, HALF, 16, 128), BF),
            pltpu.VMEM((3, HALF, 16, 128), BF),
            pltpu.VMEM((3, HALF, 16, 128), BF),
            pltpu.VMEM((UNIT, 16, 128), BF),
            pltpu.VMEM((UNIT, 16, 128), BF),
            pltpu.VMEM((2, 3, DOWN, 16, 128), BF),
            pltpu.VMEM((2, DOWN, 16, 128), BF),
            pltpu.VMEM((2, DOWN, 16, 128), BF),
            pltpu.VMEM((KVH, LANES, 128), F32),
            pltpu.VMEM((16, 4, SHARD, 128), BF),
            pltpu.VMEM((2, 16, SHARD, 128), BF),
            pltpu.VMEM((2, 16, SHARD, 128), BF),
            pltpu.VMEM((2, 3, 4, SHARD, 128), BF),
            pltpu.VMEM((2, 4, SHARD, 128), BF),
            pltpu.VMEM((2, 3, SHARD, 128), BF),
            pltpu.VMEM((3, SHARD, 128), BF),
            pltpu.VMEM((2, SHARD, 128), BF),
            pltpu.VMEM((5, 4, 8, WIDTH), F32),
            pltpu.SemaphoreType.DMA((144,)),
            pltpu.SemaphoreType.DMA((144,)),
            pltpu.SemaphoreType.DMA((6,)),
        ],
        compiler_params=pltpu.CompilerParams(
            vmem_limit_bytes=63 * MIB, collective_id=1, has_side_effects=True
        ),
        name="back",
    )(*operands)


def finish_kernel(
    late_ref,
    thin_ref,
    whole_hbm,
    downs_hbm,
    q_out,
    k_out,
    v_out,
    o_out,
    gate_out,
    up_out,
    down_out,
    qb_out,
    kb_out,
    vb_out,
    ag_out,
    hg_out,
    q_val,
    k_val,
    v_val,
    o_val,
    gate_val,
    up_val,
    down_val,
    whole_ref,
    downs_ref,
    loads,
    sems,
):
    parts = [
        pltpu.make_async_copy(whole_hbm.at[n], whole_ref.at[n], loads.at[n]) for n in range(4)
    ] + [pltpu.make_async_copy(downs_hbm, downs_ref, loads.at[4])]
    for part in parts:
        part.start()
    copies = []

    def leave(value, out):
        copy = pltpu.make_async_copy(value, out, sems.at[len(copies)])
        copy.start()
        copies.append(copy)

    def gate_tile(n, r, lane):
        t = r * 20 + lane
        p, k = t // 18, 18 * n + t % 18
        return whole_ref[p // 4, p % 4, k].astype(F32)

    arrived = 0
    for r in range(14):
        while arrived <= (r * 20 + 19) // 18 // 4:
            parts[arrived].wait()
            arrived += 1
        for value, first in ((gate_val, 0), (up_val, 10)):
            for tile in range(38):
                pieces = []
                for n in range(4):
                    lane = tile - (19 * n) // 2
                    if 0 <= lane < 10:
                        pieces.append(gate_tile(n, r, first + lane))
                total = pieces[0] if len(pieces) == 1 else pieces[0] + pieces[1]
                value[r * 16 : r * 16 + 16, tile * 128 : tile * 128 + 128] = total
        if r % 7 == 6:
            rows = pl.ds((r // 7) * 112, 112)
            leave(gate_val.at[rows], gate_out.at[rows])
            leave(up_val.at[rows], up_out.at[rows])
    parts[4].wait()
    for r in range(76):
        for tile in range(7):
            t = r * 7 + tile
            p, k = t // 34, t % 34
            down_val[r * 16 : r * 16 + 16, tile * 128 : tile * 128 + 128] = downs_ref[
                k // DOWN, p // 4, p % 4, k % DOWN
            ].astype(F32)
    leave(down_val, down_out)
    column = 0
    for value, out, count in ((q_val, q_out, 7), (k_val, k_out, 1), (v_val, v_out, 1), (o_val, o_out, 7)):
        for tile in range(count):
            value[:, tile * 128 : tile * 128 + 128] = late_ref[column // 4, column % 4].astype(F32)
            column += 1
        leave(value, out)
    f = lax.axis_index("fsdp")

    def share(row, start, part):
        total = thin_ref[row : row + 1, start : start + part]
        for n in range(1, 4):
            first = start + n * part
            total = jnp.where(f == n, thin_ref[row : row + 1, first : first + part], total)
        return total

    qb_out[...] = share(0, 0, SHARD)
    kb_out[...] = share(3, 0, 32)
    vb_out[...] = share(3, 128, 32)
    ag_out[...] = share(1, 0, SHARD)
    hg_out[...] = share(2, 0, SHARD)
    for copy in copies:
        copy.wait()


def finish(late, thin, whole, downs):
    shape = jax.ShapeDtypeStruct
    large = [
        (SHARD, WIDTH),
        (SHARD, 128),
        (SHARD, 128),
        (SHARD, WIDTH),
        (SHARD, 4 * UNITS),
        (SHARD, 4 * UNITS),
        (UNITS, WIDTH),
    ]
    tiny = [(1, SHARD), (1, 32), (1, 32), (1, SHARD), (1, SHARD)]
    return pl.pallas_call(
        finish_kernel,
        out_shape=[shape(size, F32) for size in large + tiny],
        in_specs=[VMEM] * 2 + [ANY] * 2,
        out_specs=[ANY] * 7 + [VMEM] * 5,
        scratch_shapes=[pltpu.VMEM(size, F32) for size in large]
        + [
            pltpu.VMEM((4, 4, UNIT, 16, 128), BF),
            pltpu.VMEM((2, 4, 4, DOWN, 16, 128), BF),
            pltpu.SemaphoreType.DMA((5,)),
            pltpu.SemaphoreType.DMA((9,)),
        ],
        compiler_params=pltpu.CompilerParams(vmem_limit_bytes=58 * MIB),
        name="finish",
    )(late, thin, whole, downs)

def body(
    tokens,
    block_order,
    query_weight,
    key_weight,
    value_weight,
    output_weight,
    gate_weight,
    up_weight,
    down_weight,
    query_bias,
    key_bias,
    value_bias,
    attention_gain,
    hidden_gain,
    cotangent,
):

    (
        attended,
        ot,
        lse,
        q,
        kv,
        normed,
        wq_all,
        wk_all,
        wv_all,
        small_all,
        cosine,
        sine,
        extra,
        kpos,
        qpos,
        wo_all,
        gate_all,
        up_all,
        cot_all,
    ) = front(
        tokens[0],
        query_weight,
        key_weight,
        value_weight,
        query_bias,
        attention_gain,
        hidden_gain,
        key_bias,
        value_bias,
        block_order,
        *angle_tables(),
        output_weight,
        gate_weight,
        up_weight,
        cotangent[0],
    )
    (
        output,
        grad_middle,
        grad_attn,
        hidden_gain_part,
        grad_attended,
        grads,
        down_a,
        down_b,
    ) = middle_call(
        attended,
        tokens[0],
        small_all,
        wo_all,
        cot_all,
        gate_all,
        up_all,
        gate_weight,
        up_weight,
        down_weight,
    )
    token_grad, late, thin, whole, downs = back(
        q,
        grad_attended,
        ot,
        lse,
        kv,
        extra,
        kpos,
        qpos,
        down_a,
        down_b,
        cosine,
        sine,
        normed,
        attended,
        grad_attn,
        grad_middle,
        tokens[0],
        wq_all,
        wk_all,
        wv_all,
        small_all,
        hidden_gain_part,
        grads,
    )
    ends = finish(late, thin, whole, downs)
    return (output[None], token_grad[None], *ends[:7], *(end.reshape(-1) for end in ends[7:]))


def solution(mesh):
    rows = P("fsdp", "ctx", None)
    matrix = P("fsdp", None)
    vector = P("fsdp")
    placed = (rows, P()) + (matrix,) * 7 + (vector,) * 5 + (rows,)
    return jax.shard_map(
        body,
        mesh=mesh,
        in_specs=placed,
        out_specs=(rows, rows) + (matrix,) * 7 + (vector,) * 5,
        check_vma=False,
    )
```
